32 devices in a mesh: row: 2 (over core), col: 4 (over y, x), seed: 4 (over z).
Axes of the slice: x: 2, y: 2, z: 4, core: 2. Of those that a mesh axis runs over, the one named last changes fastest.
Arguments:
- tiles: bfloat16 [2, 4, 384, 128, 128], P('row', 'col'), may hold values from -0.0390625 to 0.0390625
- tile_out: int32 [2, 4, 384], P('row', 'col'), may hold values from 0 to 1, as said below
- tile_in: int32 [2, 4, 384], P('row', 'col'), may hold values from 0 to 3
- tile_count: int32 [2, 4], P('row', 'col'), may hold values from 1 to 384, as said below
- out_degree: int32 [1024], P(('row', 'col')), may hold values from 1 to 8
- seed_ids: int32 [512, 16], P('seed'), may hold values from 0 to 1023
- prior: float32 [512, 1024], P('seed', ('row', 'col')), may hold values from -6 to 6
Outputs:
- risk: float32 [512, 1024], P('seed', ('row', 'col'))
The draws below stay inside these ranges and needn't reach their ends.
Inputs may be any that keep to these rules, and one draw needn't show every extreme that they name: `tile_count`: occupied slots of a device come first; some device has all 384 occupied in every draw. `tile_out`: on every device the output blocks named by the occupied slots never fall from one slot to the next; several occupied slots of one device may name the same output block, and the same pair of blocks.
All inputs are finite; a program needn't handle non-finite values.
Results may differ from the reference program's by a relative error of at most 0.0041.
Values may be sent and summed in bfloat16 or wider, within the bound.
No kernel may reach another device: no remote copies, remote signals or barrier semaphores. Data moves between devices by JAX's collectives and lax.ppermute only.
A program may use at most 64 MiB of HBM per device.

```python
import jax
import jax.numpy as jnp
from jax import lax

VERTEX_DEV = 128
TILE_SLOTS = 384
TILE_EDGE = 128
SEED_COUNT = 16
ITERATIONS = 2
SEED_SETS = 512
VERTICES = 1024
OUT_BLOCKS = 2
IN_BLOCKS = 4
N_ROW = 2
N_COL = 4


def count_table(key):
    first_key, second_key, third_key = jax.random.split(jax.random.fold_in(key, 7), 3)
    device_total = N_ROW * N_COL
    divisor = 1 + jax.random.randint(first_key, (device_total,), 0, 4)
    lowered = jax.random.randint(second_key, (device_total,), 1, 32)
    counts = jnp.maximum(TILE_SLOTS // divisor - lowered, 1)
    chosen = jax.random.randint(third_key, (), 0, device_total)
    counts = counts.at[chosen].set(TILE_SLOTS)
    return counts.astype(jnp.int32)


def draw_tile_count(key, part):
    return count_table(key).reshape(N_ROW, N_COL)


def draw_tile_out(key, part):
    counts = count_table(key).reshape(N_ROW * N_COL, 1)
    raw_blocks = jax.random.randint(jax.random.fold_in(key, 11), (N_ROW * N_COL, TILE_SLOTS), 0, OUT_BLOCKS)
    slot_order = jnp.arange(TILE_SLOTS, dtype=jnp.int32)[None, :]
    keyed = jnp.where(slot_order < counts, raw_blocks, raw_blocks + OUT_BLOCKS)
    ordered = jnp.sort(keyed, axis=1)
    ordered = jnp.where(ordered >= OUT_BLOCKS, ordered - OUT_BLOCKS, ordered)
    return ordered.reshape(N_ROW, N_COL, TILE_SLOTS).astype(jnp.int32)


def touch_ends(drawn, stream_key, least, largest):
    longest = drawn.shape.index(max(drawn.shape))
    spots = []
    for shift in (0, 1):
        where = [jax.random.randint(jax.random.fold_in(stream_key, axis), (), 0, length) for axis, length in enumerate(drawn.shape)]
        where[longest] = (where[longest] + shift) % drawn.shape[longest]
        spots.append(tuple(where))
    return drawn.at[spots[0]].set(least).at[spots[1]].set(largest)


def block_scale(key, dims, cuts, smallest, high):
    def one(dim, shards_of):
        draws = jax.random.uniform(jax.random.fold_in(jax.random.fold_in(key, 6), dim), (shards_of,), jnp.float32, smallest / len(cuts), high / len(cuts))
        return jnp.repeat(jnp.exp(draws), dims[dim] // shards_of).reshape((-1,) + (1,) * (len(dims) - dim - 1))

    factor_of = one(*cuts[0])
    for cut in cuts[1:]:
        factor_of = factor_of * one(*cut)
    return factor_of


def normal_values(rng, extent, spread, reach, cuts=(), held_as=jnp.bfloat16):
    values = spread * jax.random.normal(rng, extent, jnp.float32)
    if cuts:
        values = values * block_scale(rng, extent, cuts, -0.22, 0.18)
    return jnp.clip(values, -reach, reach).astype(held_as)


def setup_inputs(seed: int = 0) -> dict:
    seeds = jax.random.split(jax.random.key(seed), 8)
    return {
        "tiles": normal_values(seeds[0], (N_ROW, N_COL, TILE_SLOTS, TILE_EDGE, TILE_EDGE), (TILE_EDGE * TILE_EDGE * TILE_SLOTS // (2 * VERTEX_DEV)) ** -0.5, 0.0390625, ((0, 2), (1, 4))),
        "tile_out": draw_tile_out(jax.random.fold_in(seeds[7], 71), 0),
        "tile_in": touch_ends(jax.random.randint(seeds[2], (N_ROW, N_COL, TILE_SLOTS), 0, IN_BLOCKS), jax.random.fold_in(seeds[2], 1), 0, IN_BLOCKS - 1).astype(jnp.int32),
        "tile_count": draw_tile_count(jax.random.fold_in(seeds[7], 71), 0),
        "out_degree": touch_ends(jax.random.randint(seeds[4], (VERTICES,), 1, 9), jax.random.fold_in(seeds[4], 1), 1, 8).astype(jnp.int32),
        "seed_ids": touch_ends(jax.random.randint(seeds[5], (SEED_SETS, SEED_COUNT), 0, VERTICES), jax.random.fold_in(seeds[5], 1), 0, VERTICES - 1).astype(jnp.int32),
        "prior": normal_values(seeds[6], (SEED_SETS, VERTICES), 1.0, 6.0, ((0, 4), (1, 8)), jnp.float32),
    }


damping = 0.85


def reference(tiles, tile_out, tile_in, tile_count, out_degree, seed_ids, prior):
    set_rows = jnp.broadcast_to(jnp.arange(SEED_SETS, dtype=jnp.int32)[:, None], seed_ids.shape)
    restart = jnp.zeros((SEED_SETS, VERTICES), jnp.float32).at[set_rows, seed_ids].add(1.0)
    degree = out_degree.astype(jnp.float32)
    slot_index = jnp.arange(TILE_SLOTS, dtype=jnp.int32)
    row_order = jnp.arange(N_ROW, dtype=jnp.int32)
    risk_now = prior
    for round_index in range(ITERATIONS):
        scaled = (risk_now / degree[None, :]).astype(jnp.bfloat16)
        inputs = scaled.reshape(SEED_SETS, N_ROW, IN_BLOCKS, TILE_EDGE)
        columns = []
        for col_index in range(N_COL):
            def add_device(panel_sum, row_index):
                block_in = inputs[:, row_index]
                gathered = jnp.take(block_in, tile_in[row_index, col_index], axis=1).astype(jnp.float32)
                weights = tiles[row_index, col_index].astype(jnp.float32)
                product = jnp.einsum("stk,tkj->stj", gathered, weights)
                valid_mask = (slot_index < tile_count[row_index, col_index]).astype(jnp.float32)
                product = product * valid_mask[None, :, None]
                return panel_sum.at[:, tile_out[row_index, col_index], :].add(product), None

            zero_panel = jnp.zeros((SEED_SETS, OUT_BLOCKS, TILE_EDGE), jnp.float32)
            panel_sum, _ = lax.scan(add_device, zero_panel, row_order)
            columns.append(panel_sum.reshape(SEED_SETS, N_ROW, VERTEX_DEV))
        incoming = jnp.stack(columns, axis=2).reshape(SEED_SETS, VERTICES)
        risk_now = (1.0 - damping) * restart + damping * incoming
    return risk_now
```

```python
import functools
import math

import jax
import jax.numpy as jnp
from jax import lax
from jax.experimental import pallas as pl
from jax.experimental.pallas import tpu as pltpu
from jax.sharding import PartitionSpec as P

ITERATIONS = 2


damping = 0.85

VMEM = pl.BlockSpec(memory_space=pltpu.VMEM)
SMEM = pl.BlockSpec(memory_space=pltpu.SMEM)
HBM = pl.BlockSpec(memory_space=pl.ANY)

UNROLL = 4
FIELD_BITS = 8
FIELD_MASK = (1 << FIELD_BITS) - 1
WORD_FIELDS = 4


def partner(index, offset, extent):
    if extent & (extent - 1) == 0:
        return index ^ offset
    return (index + offset) % extent


def send_to(value, axes, extents, offsets):
    pairs = []
    for flat in range(math.prod(extents)):
        rest, source = flat, []
        for extent in reversed(extents):
            source.insert(0, rest % extent)
            rest //= extent
        origin = [partner(place, offset, extent) for place, offset, extent in zip(source, offsets, extents)]
        origin_flat = 0
        for place, extent in zip(origin, extents):
            origin_flat = origin_flat * extent + place
        pairs.append((origin_flat, flat))
    return lax.ppermute(value, axes, pairs)


def scale_kernel(prior_ref, degree_ref, scaled_ref):
    scaled_ref[...] = (prior_ref[...] / degree_ref[...].astype(jnp.float32)).astype(jnp.bfloat16)


def sum_kernel(rows, cols, owned_blocks, tiles_ref, out_ref, in_ref, count_ref, seeds_ref, *rest):
    weight_refs, restart_ref = rest[:rows], rest[rows]
    buffer, total, listed, arrived = rest[rows + 1:]
    in_blocks, out_blocks = cols * owned_blocks, rows * owned_blocks
    slots, edge = tiles_ref.shape[2], tiles_ref.shape[3]
    group = slots // arrived.shape[0]
    reach = group + UNROLL
    row, col = lax.axis_index("row"), lax.axis_index("col")

    def arrival(index):
        span = pl.ds(index * group, group)
        return pltpu.make_async_copy(tiles_ref.at[0, 0, span], buffer.at[span], arrived.at[index])

    for index in range(slots // group):
        arrival(index).start()

    buffer[slots] = jnp.zeros((edge, edge), jnp.bfloat16)
    total[...] = jnp.zeros(total.shape, jnp.float32)

    seed_total, sets = seeds_ref.shape
    owned = owned_blocks * edge
    vertex = lax.broadcasted_iota(jnp.int32, (owned, sets), 0) + (row * cols + col) * owned
    restart = jnp.zeros((owned, sets), jnp.float32)
    for seed in range(seed_total):
        restart += (seeds_ref[seed:seed + 1, :] == vertex).astype(jnp.float32)
    restart_ref[...] = (1.0 - damping) * restart.T

    occupied = count_ref[0, 0]

    def add_group(index, carry):
        first = index * group
        end = jnp.minimum(first + group, occupied)
        lowest = out_ref[0, 0, first]
        highest = out_ref[0, 0, jnp.maximum(end - 1, first)]

        def add_target(target, carry):
            def scan(step, words):
                words = list(words)
                for inner in range(8):
                    slot = first + step * 8 + inner
                    source = in_ref[0, 0, slot]
                    valid = (out_ref[0, 0, slot] == target) & (slot < occupied)
                    shift = (source % WORD_FIELDS) * FIELD_BITS
                    word = words[0]
                    for other in range(1, len(words)):
                        word = jnp.where(source // WORD_FIELDS == other, words[other], word)
                    place = (word >> shift) & FIELD_MASK
                    listed[source * reach + place] = slot
                    grown = jnp.where(valid, jnp.int32(1) << shift, 0)
                    if len(words) == 1:
                        words[0] = words[0] + grown
                    else:
                        for other in range(len(words)):
                            words[other] += jnp.where(source // WORD_FIELDS == other, grown, 0)
                return tuple(words)

            word_total = -(-in_blocks // WORD_FIELDS)
            words = lax.fori_loop(0, group // 8, scan, (jnp.int32(0),) * word_total)

            @pl.when(target == lowest)
            def _():
                arrival(index).wait()

            for source in range(in_blocks):
                held = (words[source // WORD_FIELDS] >> (source % WORD_FIELDS * FIELD_BITS)) & FIELD_MASK
                base = source * reach
                for pad in range(UNROLL - 1):
                    listed[base + held + pad] = slots
                pair = target * in_blocks + source

                def add_tiles(step, value):
                    at = base + step * UNROLL
                    parts = [buffer[listed[at + inner]].astype(jnp.float32) for inner in range(UNROLL)]
                    while len(parts) > 1:
                        parts = [a + b for a, b in zip(parts[::2], parts[1::2])]
                    return value + parts[0]

                total[pair] = lax.fori_loop(0, (held + UNROLL - 1) // UNROLL, add_tiles, total[pair])
            return carry

        return lax.fori_loop(lowest, jnp.maximum(highest, lowest) + 1, add_target, carry)

    lax.fori_loop(0, slots // group, add_group, 0)

    for offset in range(rows):
        owner = partner(row, offset, rows)
        for block in range(owned_blocks):
            for source in range(in_blocks):
                pair = (owner * owned_blocks + block) * in_blocks + source
                weight_refs[offset][
                    source * edge:(source + 1) * edge, block * edge:(block + 1) * edge
                ] = total[pair].astype(jnp.bfloat16)


def round_kernel(rows, cols, relative, last, *refs):
    block_total = rows * cols if relative else 1
    blocks, weights = refs[:block_total], refs[block_total:block_total + rows]
    restart_ref, degree_ref, result_ref = refs[block_total + rows:]
    row, col = lax.axis_index("row"), lax.axis_index("col")
    owned = restart_ref.shape[1]
    incoming = jnp.zeros(restart_ref.shape, jnp.float32)
    for row_offset in range(rows):
        for col_offset in range(cols):
            column = partner(col, col_offset, cols)
            if relative:
                scaled = blocks[row_offset * cols + col_offset][...]
            else:
                scaled = blocks[0][partner(row, row_offset, rows) * cols + column]
            weight = weights[row_offset][pl.ds(pl.multiple_of(column * owned, owned), owned), :]
            incoming += jnp.dot(scaled, weight, preferred_element_type=jnp.float32)
    risk = restart_ref[...] + damping * incoming
    if last:
        result_ref[...] = risk
    else:
        result_ref[...] = (risk / degree_ref[...].astype(jnp.float32)).astype(jnp.bfloat16)


def local(tiles, tile_out, tile_in, tile_count, out_degree, seed_ids, prior):
    rows, cols = lax.axis_size("row"), lax.axis_size("col")
    sets, owned = prior.shape
    slots, edge = tiles.shape[2], tiles.shape[3]
    owned_blocks = owned // edge
    in_blocks, out_blocks = cols * owned_blocks, rows * owned_blocks
    group = math.gcd(slots, 64)
    relative = rows * cols <= 8
    degree = out_degree.reshape(1, owned)

    scaled = pl.pallas_call(
        scale_kernel,
        out_shape=jax.ShapeDtypeStruct((sets, owned), jnp.bfloat16),
        in_specs=[VMEM, VMEM],
        out_specs=VMEM,
        cost_estimate=pl.CostEstimate(flops=sets * owned, bytes_accessed=6 * sets * owned, transcendentals=0),
        name="scale",
    )(prior, degree)

    def spread(value):
        if not relative:
            return [lax.all_gather(value, ("row", "col"), axis=0)]
        blocks = []
        for row_offset in range(rows):
            for col_offset in range(cols):
                if row_offset or col_offset:
                    blocks.append(send_to(value, ("row", "col"), (rows, cols), (row_offset, col_offset)))
                else:
                    blocks.append(value)
        return blocks

    blocks = spread(scaled)

    *weights, restart = pl.pallas_call(
        functools.partial(sum_kernel, rows, cols, owned_blocks),
        out_shape=[jax.ShapeDtypeStruct((in_blocks * edge, owned), jnp.bfloat16)] * rows
        + [jax.ShapeDtypeStruct((sets, owned), jnp.float32)],
        in_specs=[HBM, SMEM, SMEM, SMEM, VMEM],
        out_specs=[VMEM] * (rows + 1),
        scratch_shapes=[
            pltpu.VMEM((slots + 1, edge, edge), jnp.bfloat16),
            pltpu.VMEM((out_blocks * in_blocks, edge, edge), jnp.float32),
            pltpu.SMEM((in_blocks * (group + UNROLL),), jnp.int32),
            pltpu.SemaphoreType.DMA((slots // group,)),
        ],
        compiler_params=pltpu.CompilerParams(vmem_limit_bytes=32 * 1024 * 1024),
        cost_estimate=pl.CostEstimate(
            flops=slots * edge * edge, bytes_accessed=2 * slots * edge * edge, transcendentals=0
        ),
        name="sum_tiles",
    )(tiles, tile_out, tile_in, tile_count, seed_ids.T)

    weights = [weights[0]] + [
        send_to(weights[offset], ("row",), (rows,), (offset,)) for offset in range(1, rows)
    ]

    for round_index in range(ITERATIONS):
        last = round_index == ITERATIONS - 1
        value = pl.pallas_call(
            functools.partial(round_kernel, rows, cols, relative, last),
            out_shape=jax.ShapeDtypeStruct((sets, owned), jnp.float32 if last else jnp.bfloat16),
            in_specs=[VMEM] * (len(blocks) + rows + 2),
            out_specs=VMEM,
            compiler_params=pltpu.CompilerParams(vmem_limit_bytes=32 * 1024 * 1024),
            cost_estimate=pl.CostEstimate(
                flops=2 * sets * rows * cols * owned * owned,
                bytes_accessed=2 * rows * cols * owned * (sets + owned),
                transcendentals=0,
            ),
            name="last_round" if last else "first_round",
        )(*blocks, *weights, restart, degree)
        if not last:
            blocks = spread(value)
    return value


def solution(mesh):
    placed = (
        P("row", "col", None, None, None),
        P("row", "col", None),
        P("row", "col", None),
        P("row", "col"),
        P(("row", "col")),
        P("seed", None),
        P("seed", ("row", "col")),
    )
    return jax.shard_map(
        local, mesh=mesh, in_specs=placed, out_specs=P("seed", ("row", "col")), check_vma=False
    )
```

```python
import functools
import math

import jax
import jax.numpy as jnp
from jax import lax
from jax.experimental import pallas as pl
from jax.experimental.pallas import tpu as pltpu
from jax.sharding import PartitionSpec as P

ITERATIONS = 2


damping = 0.85

VMEM = pl.BlockSpec(memory_space=pltpu.VMEM)
HBM = pl.BlockSpec(memory_space=pltpu.HBM)

TILES_VMEM = 50 * 1024 * 1024
SMALL_VMEM = 8 * 1024 * 1024
UNROLL = 4
FIELD_BITS = 8
FIELD_MASK = (1 << FIELD_BITS) - 1
WORD_FIELDS = 4


def partner(index, offset, extent):
    if extent & (extent - 1) == 0:
        return index ^ offset
    return (index + offset) % extent


def send_to(value, axes, extents, offsets):
    pairs = []
    for flat in range(math.prod(extents)):
        rest, source = flat, []
        for extent in reversed(extents):
            source.insert(0, rest % extent)
            rest //= extent
        origin = [partner(place, offset, extent) for place, offset, extent in zip(source, offsets, extents)]
        origin_flat = 0
        for place, extent in zip(origin, extents):
            origin_flat = origin_flat * extent + place
        pairs.append((origin_flat, flat))
    return lax.ppermute(value, axes, pairs)


def in_hbm(*arrays):
    return [pltpu.with_memory_space_constraint(array, pltpu.HBM) for array in arrays]


def scale_kernel(prior_hbm, degree_hbm, scaled_ref, prior_ref, degree_ref, arrived):
    copies = [
        pltpu.make_async_copy(source, place, arrived.at[index])
        for index, (source, place) in enumerate(((prior_hbm, prior_ref), (degree_hbm, degree_ref)))
    ]
    for copy in copies:
        copy.start()
    for copy in copies:
        copy.wait()
    scaled = (prior_ref[...] / degree_ref[...].astype(jnp.float32)).astype(jnp.bfloat16)
    for place in range(scaled_ref.shape[0]):
        scaled_ref[place] = scaled


def sum_kernel(rows, cols, owned_blocks, scaled_ref, count_ref, tiles_ref, out_hbm, in_hbm, seeds_hbm, *rest):
    weight_refs, restart_ref = rest[:rows], rest[rows]
    buffer, total, listed, out_ref, in_ref, seeds_ref, arrived, small = rest[rows + 1:]
    in_blocks, out_blocks = cols * owned_blocks, rows * owned_blocks
    slots, edge = tiles_ref.shape[2], tiles_ref.shape[3]
    group = slots // arrived.shape[0]
    reach = group + UNROLL
    row, col = lax.axis_index("row"), lax.axis_index("col")

    def arrival(index):
        span = pl.ds(index * group, group)
        return pltpu.make_async_copy(tiles_ref.at[0, 0, span], buffer.at[span], arrived.at[index])

    copies = [
        pltpu.make_async_copy(source, place, small.at[index])
        for index, (source, place) in enumerate(
            ((out_hbm, out_ref), (in_hbm, in_ref), (seeds_hbm, seeds_ref))
        )
    ]
    for copy in copies:
        copy.start()
    for index in range(slots // group):
        arrival(index).start()

    buffer[slots] = jnp.zeros((edge, edge), jnp.bfloat16)
    total[...] = jnp.zeros(total.shape, jnp.float32)

    for copy in copies:
        copy.wait()
    seed_total, sets = seeds_ref.shape
    owned = owned_blocks * edge
    vertex = lax.broadcasted_iota(jnp.int32, (owned, sets), 0) + (row * cols + col) * owned
    restart = jnp.zeros((owned, sets), jnp.float32)
    for seed in range(seed_total):
        restart += (seeds_ref[seed:seed + 1, :] == vertex).astype(jnp.float32)
    restart_ref[...] = (1.0 - damping) * restart.T

    occupied = count_ref[0, 0]

    def add_group(index, carry):
        first = index * group
        end = jnp.minimum(first + group, occupied)
        lowest = out_ref[0, 0, first]
        highest = out_ref[0, 0, jnp.maximum(end - 1, first)]

        def add_target(target, carry):
            def scan(step, words):
                words = list(words)
                for inner in range(8):
                    slot = first + step * 8 + inner
                    source = in_ref[0, 0, slot]
                    valid = (out_ref[0, 0, slot] == target) & (slot < occupied)
                    shift = (source % WORD_FIELDS) * FIELD_BITS
                    word = words[0]
                    for other in range(1, len(words)):
                        word = jnp.where(source // WORD_FIELDS == other, words[other], word)
                    place = (word >> shift) & FIELD_MASK
                    listed[source * reach + place] = slot
                    grown = jnp.where(valid, jnp.int32(1) << shift, 0)
                    if len(words) == 1:
                        words[0] = words[0] + grown
                    else:
                        for other in range(len(words)):
                            words[other] += jnp.where(source // WORD_FIELDS == other, grown, 0)
                return tuple(words)

            word_total = -(-in_blocks // WORD_FIELDS)
            words = lax.fori_loop(0, group // 8, scan, (jnp.int32(0),) * word_total)

            @pl.when(target == lowest)
            def _():
                arrival(index).wait()

            for source in range(in_blocks):
                held = (words[source // WORD_FIELDS] >> (source % WORD_FIELDS * FIELD_BITS)) & FIELD_MASK
                base = source * reach
                for pad in range(UNROLL - 1):
                    listed[base + held + pad] = slots
                pair = target * in_blocks + source

                def add_tiles(step, value):
                    at = base + step * UNROLL
                    parts = [buffer[listed[at + inner]].astype(jnp.float32) for inner in range(UNROLL)]
                    while len(parts) > 1:
                        parts = [a + b for a, b in zip(parts[::2], parts[1::2])]
                    return value + parts[0]

                total[pair] = lax.fori_loop(0, (held + UNROLL - 1) // UNROLL, add_tiles, total[pair])
            return carry

        return lax.fori_loop(lowest, jnp.maximum(highest, lowest) + 1, add_target, carry)

    lax.fori_loop(0, slots // group, add_group, 0)

    for offset in range(rows):
        owner = partner(row, offset, rows)
        for block in range(owned_blocks):
            for source in range(in_blocks):
                pair = (owner * owned_blocks + block) * in_blocks + source
                weight_refs[offset][
                    source * edge:(source + 1) * edge, block * edge:(block + 1) * edge
                ] = total[pair].astype(jnp.bfloat16)


def round_kernel(rows, cols, last, blocks_ref, *refs):
    weights, (restart_ref, degree_ref, result_ref) = refs[:rows], refs[rows:]
    row, col = lax.axis_index("row"), lax.axis_index("col")
    owned = restart_ref.shape[1]
    incoming = jnp.zeros(restart_ref.shape, jnp.float32)
    for row_offset in range(rows):
        first = partner(row, row_offset, rows) * cols
        for column in range(cols):
            weight = weights[row_offset][column * owned:(column + 1) * owned, :]
            incoming += jnp.dot(blocks_ref[first + column], weight, preferred_element_type=jnp.float32)
    risk = restart_ref[...] + damping * incoming
    if last:
        result_ref[...] = risk
    else:
        scaled = (risk / degree_ref[...].astype(jnp.float32)).astype(jnp.bfloat16)
        for place in range(result_ref.shape[0]):
            result_ref[place] = scaled


def local(tiles, tile_out, tile_in, tile_count, out_degree, seed_ids, prior):
    rows, cols = lax.axis_size("row"), lax.axis_size("col")
    sets, owned = prior.shape
    slots, edge = tiles.shape[2], tiles.shape[3]
    owned_blocks = owned // edge
    in_blocks, out_blocks = cols * owned_blocks, rows * owned_blocks
    group = math.gcd(slots, 64)
    everyone = rows * cols
    degree = out_degree.reshape(1, owned)

    scaled = pl.pallas_call(
        scale_kernel,
        out_shape=jax.ShapeDtypeStruct((everyone, sets, owned), jnp.bfloat16),
        in_specs=[HBM, HBM],
        out_specs=VMEM,
        scratch_shapes=[
            pltpu.VMEM((sets, owned), jnp.float32),
            pltpu.VMEM((1, owned), jnp.int32),
            pltpu.SemaphoreType.DMA((2,)),
        ],
        compiler_params=pltpu.CompilerParams(vmem_limit_bytes=SMALL_VMEM),
        cost_estimate=pl.CostEstimate(flops=sets * owned, bytes_accessed=6 * sets * owned, transcendentals=0),
        name="scale",
    )(*in_hbm(prior, degree))

    def spread(copies):
        return lax.all_to_all(copies, ("row", "col"), split_axis=0, concat_axis=0, tiled=True)

    blocks = spread(scaled)

    *weights, restart = pl.pallas_call(
        functools.partial(sum_kernel, rows, cols, owned_blocks),
        out_shape=[jax.ShapeDtypeStruct((in_blocks * edge, owned), jnp.bfloat16)] * rows
        + [jax.ShapeDtypeStruct((sets, owned), jnp.float32)],
        in_specs=[pl.BlockSpec(memory_space=pl.ANY), pl.BlockSpec(memory_space=pltpu.SMEM)] + [HBM] * 4,
        out_specs=[VMEM] * (rows + 1),
        scratch_shapes=[
            pltpu.VMEM((slots + 1, edge, edge), jnp.bfloat16),
            pltpu.VMEM((out_blocks * in_blocks, edge, edge), jnp.float32),
            pltpu.SMEM((in_blocks * (group + UNROLL),), jnp.int32),
            pltpu.SMEM(tile_out.shape, jnp.int32),
            pltpu.SMEM(tile_in.shape, jnp.int32),
            pltpu.VMEM((seed_ids.shape[1], sets), jnp.int32),
            pltpu.SemaphoreType.DMA((slots // group,)),
            pltpu.SemaphoreType.DMA((3,)),
        ],
        compiler_params=pltpu.CompilerParams(vmem_limit_bytes=TILES_VMEM),
        cost_estimate=pl.CostEstimate(
            flops=slots * edge * edge, bytes_accessed=2 * slots * edge * edge, transcendentals=0
        ),
        name="sum_tiles",
    )(scaled, tile_count, *in_hbm(tiles, tile_out, tile_in, seed_ids.T))

    weights = [weights[0]] + [
        send_to(weights[offset], ("row",), (rows,), (offset,)) for offset in range(1, rows)
    ]

    for round_index in range(ITERATIONS):
        last = round_index == ITERATIONS - 1
        shape = (sets, owned) if last else (everyone, sets, owned)
        value = pl.pallas_call(
            functools.partial(round_kernel, rows, cols, last),
            out_shape=jax.ShapeDtypeStruct(shape, jnp.float32 if last else jnp.bfloat16),
            in_specs=[VMEM] * (rows + 3),
            out_specs=VMEM,
            compiler_params=pltpu.CompilerParams(vmem_limit_bytes=SMALL_VMEM),
            cost_estimate=pl.CostEstimate(
                flops=2 * sets * everyone * owned * owned,
                bytes_accessed=2 * everyone * owned * (sets + owned),
                transcendentals=0,
            ),
            name="last_round" if last else "first_round",
        )(blocks, *weights, restart, degree)
        if not last:
            blocks = spread(value)
    return value


def solution(mesh):
    placed = (
        P("row", "col", None, None, None),
        P("row", "col", None),
        P("row", "col", None),
        P("row", "col"),
        P(("row", "col")),
        P("seed", None),
        P("seed", ("row", "col")),
    )
    return jax.shard_map(
        local, mesh=mesh, in_specs=placed, out_specs=P("seed", ("row", "col")), check_vma=False
    )
```

```python
import functools
import math

import jax
import jax.numpy as jnp
from jax import lax
from jax.experimental import pallas as pl
from jax.experimental.pallas import tpu as pltpu
from jax.sharding import PartitionSpec as P

ITERATIONS = 2


damping = 0.85

VMEM = pl.BlockSpec(memory_space=pltpu.VMEM)
SMEM = pl.BlockSpec(memory_space=pltpu.SMEM)
HBM = pl.BlockSpec(memory_space=pltpu.HBM)
ANY = pl.BlockSpec(memory_space=pl.ANY)

TILES_VMEM = 50 * 1024 * 1024
SMALL_VMEM = 8 * 1024 * 1024
LANES = 4
FLIGHT = 6


def in_hbm(*arrays):
    return [pltpu.with_memory_space_constraint(array, pltpu.HBM) for array in arrays]


def call(kernel, out_shape, name, **options):
    return pl.pallas_call(
        kernel,
        out_shape=out_shape,
        compiler_params=pltpu.CompilerParams(vmem_limit_bytes=options.pop("vmem", SMALL_VMEM)),
        cost_estimate=pl.CostEstimate(
            flops=options.pop("flops", 0), bytes_accessed=options.pop("size", 0), transcendentals=0
        ),
        name=name,
        **options,
    )


def bit_orders(cols):
    bits = list(range(cols.bit_length() - 1))
    return bits[::-1], bits


def column_masks(cols):
    return [
        [sum((block >> step & 1) << bit for step, bit in enumerate(order)) for block in range(cols)]
        for order in bit_orders(cols)
    ]


def exchange(value, rows, cols, step):
    pairs = []
    for row in range(rows):
        flip = 1 << bit_orders(cols)[row % 2][step]
        pairs += [(row * cols + (col ^ flip), row * cols + col) for col in range(cols)]
    return lax.ppermute(value, ("row", "col"), pairs)


def swap_rows(value):
    return lax.ppermute(value, "row", [(0, 1), (1, 0)])


def scale_kernel(prior_hbm, degree_hbm, scaled_ref, prior_ref, degree_ref, arrived):
    copies = [
        pltpu.make_async_copy(source, place, arrived.at[index])
        for index, (source, place) in enumerate(((prior_hbm, prior_ref), (degree_hbm, degree_ref)))
    ]
    for copy in copies:
        copy.start()
    for copy in copies:
        copy.wait()
    scaled_ref[0] = (prior_ref[...] / degree_ref[...].astype(jnp.float32)).astype(jnp.bfloat16)


def join_kernel(held_ref, received_ref, joined_ref):
    count = held_ref.shape[0]
    joined_ref[:count] = held_ref[...]
    joined_ref[count:] = received_ref[...]


def sum_kernel(
    rows, cols, owned_blocks, scaled_ref, count_ref, tiles_ref, out_hbm, in_hbm, seeds_hbm,
    weight_ref, restart_ref, buffer, total, out_ref, in_ref, seeds_ref, arrived, small,
):
    in_blocks, out_blocks = cols * owned_blocks, rows * owned_blocks
    slots, edge = tiles_ref.shape[2], tiles_ref.shape[3]
    group_total = arrived.shape[0]
    group = slots // group_total
    row, col = lax.axis_index("row"), lax.axis_index("col")

    def arrival(index):
        span = pl.ds(index * group, group)
        return pltpu.make_async_copy(tiles_ref.at[0, 0, span], buffer.at[span], arrived.at[index])

    copies = [
        pltpu.make_async_copy(source, place, small.at[index])
        for index, (source, place) in enumerate(
            ((out_hbm, out_ref), (in_hbm, in_ref), (seeds_hbm, seeds_ref))
        )
    ]
    for copy in copies:
        copy.start()
    for index in range(min(FLIGHT, group_total)):
        arrival(index).start()

    buffer[slots] = jnp.zeros((edge, edge), jnp.bfloat16)
    total[...] = jnp.zeros(total.shape, jnp.float32)

    for copy in copies:
        copy.wait()
    seed_total, sets = seeds_ref.shape
    owned = owned_blocks * edge
    vertex = lax.broadcasted_iota(jnp.int32, (owned, sets), 0) + (row * cols + col) * owned
    restart = jnp.zeros((owned, sets), jnp.float32)
    for seed in range(seed_total):
        restart += (seeds_ref[seed:seed + 1, :] == vertex).astype(jnp.float32)
    restart_ref[...] = (1.0 - damping) * restart.T

    occupied = count_ref[0, 0]

    def add_group(index, carry):
        arrival(index).wait()

        @pl.when(index + FLIGHT < group_total)
        def _():
            arrival(index + FLIGHT).start()

        first = index * group

        def add_tiles(step, carry):
            at = first + step * LANES
            for start in range(0, LANES, 2):
                sums = []
                for lane in range(start, start + 2):
                    slot = at + lane
                    pair = out_ref[0, 0, slot] * in_blocks + in_ref[0, 0, slot]
                    used = jnp.where(slot < occupied, slot, slots)
                    sums.append((lane, pair, total[lane, pair] + buffer[used].astype(jnp.float32)))
                for lane, pair, value in sums:
                    total[lane, pair] = value
            return carry

        here = jnp.clip(occupied - first, 0, group)
        return lax.fori_loop(0, (here + LANES - 1) // LANES, add_tiles, carry)

    lax.fori_loop(0, group_total, add_group, 0)

    for place in range(rows):
        owner = row ^ place if rows == 2 else place
        for block in range(owned_blocks):
            columns = slice(place * owned + block * edge, place * owned + (block + 1) * edge)
            for source in range(in_blocks):
                pair = (owner * owned_blocks + block) * in_blocks + source
                value = (total[0, pair] + total[1, pair]) + (total[2, pair] + total[3, pair])
                high = value.astype(jnp.bfloat16)
                low = (value - high.astype(jnp.float32)).astype(jnp.bfloat16)
                lines = source // owned_blocks, source % owned_blocks * edge
                weight_ref[lines[0], lines[1]:lines[1] + edge, columns] = high
                weight_ref[lines[0], owned + lines[1]:owned + lines[1] + edge, columns] = low


def product_kernel(rows, cols, *refs):
    parts, (weight_ref, *result_refs) = refs[:2], refs[2:]
    row, col = lax.axis_index("row"), lax.axis_index("col")
    even, odd = column_masks(cols)
    incoming = None
    for block in range(cols):
        half = cols // 2
        scaled = parts[block // half][block % half] if half else parts[0][0]
        column = col ^ jnp.where(row % 2 == 0, even[block], odd[block])
        term = jnp.dot(
            jnp.concatenate([scaled, scaled], axis=1), weight_ref[column], preferred_element_type=jnp.float32
        )
        incoming = term if incoming is None else incoming + term
    owned = incoming.shape[1] // rows
    if len(result_refs) == 1:
        for place in range(rows):
            result_refs[0][place] = incoming[:, place * owned:(place + 1) * owned]
    else:
        for place in range(rows):
            result_refs[place][...] = incoming[:, place * owned:(place + 1) * owned]


def finish_kernel(last, *refs):
    *incoming_refs, restart_ref, degree_ref, result_ref = refs
    incoming = sum(ref[...] for ref in incoming_refs)
    risk = restart_ref[...] + damping * incoming
    if last:
        result_ref[...] = risk
    else:
        result_ref[0] = (risk / degree_ref[...].astype(jnp.float32)).astype(jnp.bfloat16)


def local(tiles, tile_out, tile_in, tile_count, out_degree, seed_ids, prior):
    rows, cols = lax.axis_size("row"), lax.axis_size("col")
    sets, owned = prior.shape
    slots, edge = tiles.shape[2], tiles.shape[3]
    owned_blocks = owned // edge
    in_blocks, out_blocks = cols * owned_blocks, rows * owned_blocks
    group = math.gcd(slots, 32)
    degree = out_degree.reshape(1, owned)
    low = jnp.bfloat16

    scaled = call(
        scale_kernel,
        jax.ShapeDtypeStruct((1, sets, owned), low),
        "scale",
        in_specs=[HBM, HBM],
        out_specs=VMEM,
        scratch_shapes=[
            pltpu.VMEM((sets, owned), jnp.float32),
            pltpu.VMEM((1, owned), jnp.int32),
            pltpu.SemaphoreType.DMA((2,)),
        ],
        size=6 * sets * owned,
    )(*in_hbm(prior, degree))

    def spread(held):
        received = None
        for step in range(cols.bit_length() - 1):
            if received is not None:
                held = call(
                    join_kernel,
                    jax.ShapeDtypeStruct((2 * held.shape[0],) + held.shape[1:], low),
                    "join",
                    in_specs=[VMEM, VMEM],
                    out_specs=VMEM,
                    size=8 * held.size,
                )(held, received)
            received = exchange(held, rows, cols, step)
        return held, received

    held, received = spread(scaled)

    weight, restart = call(
        functools.partial(sum_kernel, rows, cols, owned_blocks),
        [
            jax.ShapeDtypeStruct((cols, 2 * owned, rows * owned), low),
            jax.ShapeDtypeStruct((sets, owned), jnp.float32),
        ],
        "sum_tiles",
        in_specs=[ANY, SMEM] + [HBM] * 4,
        out_specs=[VMEM] * 2,
        scratch_shapes=[
            pltpu.VMEM((slots + 1, edge, edge), low),
            pltpu.VMEM((LANES, out_blocks * in_blocks, edge, edge), jnp.float32),
            pltpu.SMEM(tile_out.shape, jnp.int32),
            pltpu.SMEM(tile_in.shape, jnp.int32),
            pltpu.VMEM((seed_ids.shape[1], sets), jnp.int32),
            pltpu.SemaphoreType.DMA((slots // group,)),
            pltpu.SemaphoreType.DMA((3,)),
        ],
        vmem=TILES_VMEM,
        flops=slots * edge * edge,
        size=2 * slots * edge * edge,
    )(held, tile_count, *in_hbm(tiles, tile_out, tile_in, seed_ids.T))

    for round_index in range(ITERATIONS):
        last = round_index == ITERATIONS - 1
        piece = jax.ShapeDtypeStruct((sets, owned), jnp.float32)
        partial_value = call(
            functools.partial(product_kernel, rows, cols),
            [piece] * 2 if rows == 2 else jax.ShapeDtypeStruct((rows, sets, owned), jnp.float32),
            "product",
            in_specs=[VMEM] * 3,
            out_specs=[VMEM] * 2 if rows == 2 else VMEM,
            flops=4 * sets * cols * owned * rows * owned,
            size=2 * cols * owned * (sets + 2 * rows * owned),
        )(held, received, weight)
        if rows == 2:
            incoming = (partial_value[0], swap_rows(partial_value[1]))
        else:
            incoming = (lax.psum_scatter(partial_value, "row", scatter_dimension=0, tiled=False),)
        value = call(
            functools.partial(finish_kernel, last),
            piece if last else jax.ShapeDtypeStruct((1, sets, owned), low),
            "last" if last else "next",
            in_specs=[VMEM] * (len(incoming) + 2),
            out_specs=VMEM,
            size=12 * sets * owned,
        )(*incoming, restart, degree)
        if not last:
            held, received = spread(value)
    return value


def solution(mesh):
    placed = (
        P("row", "col", None, None, None),
        P("row", "col", None),
        P("row", "col", None),
        P("row", "col"),
        P(("row", "col")),
        P("seed", None),
        P("seed", ("row", "col")),
    )
    return jax.shard_map(
        local, mesh=mesh, in_specs=placed, out_specs=P("seed", ("row", "col")), check_vma=False
    )
```

```python
import functools
import math

import jax
import jax.numpy as jnp
from jax import lax
from jax.experimental import pallas as pl
from jax.experimental.pallas import tpu as pltpu
from jax.sharding import PartitionSpec as P

ITERATIONS = 2


damping = 0.85

VMEM = pl.BlockSpec(memory_space=pltpu.VMEM)
SMEM = pl.BlockSpec(memory_space=pltpu.SMEM)
HBM = pl.BlockSpec(memory_space=pltpu.HBM)
ANY = pl.BlockSpec(memory_space=pl.ANY)

TILES_VMEM = 50 * 1024 * 1024
SMALL_VMEM = 8 * 1024 * 1024
LANES = 4
UNROLL = 8
FLIGHT = 6


def in_hbm(*arrays):
    return [pltpu.with_memory_space_constraint(array, pltpu.HBM) for array in arrays]


def call(kernel, out_shape, name, **options):
    return pl.pallas_call(
        kernel,
        out_shape=out_shape,
        compiler_params=pltpu.CompilerParams(vmem_limit_bytes=options.pop("vmem", SMALL_VMEM)),
        cost_estimate=pl.CostEstimate(
            flops=options.pop("flops", 0), bytes_accessed=options.pop("size", 0), transcendentals=0
        ),
        name=name,
        **options,
    )


def partner(index, offset, extent):
    if extent & (extent - 1) == 0:
        return index ^ offset
    return (index + offset) % extent


def from_column(value, cols, offset):
    return lax.ppermute(value, "col", [(partner(col, offset, cols), col) for col in range(cols)])


def swap_rows(value):
    return lax.ppermute(value, "row", [(0, 1), (1, 0)])


def scale_kernel(prior_hbm, degree_hbm, scaled_ref, prior_ref, degree_ref, arrived):
    copies = [
        pltpu.make_async_copy(source, place, arrived.at[index])
        for index, (source, place) in enumerate(((prior_hbm, prior_ref), (degree_hbm, degree_ref)))
    ]
    for copy in copies:
        copy.start()
    for copy in copies:
        copy.wait()
    scaled_ref[...] = (prior_ref[...] / degree_ref[...].astype(jnp.float32)).astype(jnp.bfloat16)


def sum_kernel(
    rows, cols, owned_blocks, scaled_ref, count_ref, tiles_ref, out_hbm, in_hbm, seeds_hbm,
    weight_ref, restart_ref, buffer, total, out_ref, in_ref, seeds_ref, arrived, small,
):
    in_blocks, out_blocks = cols * owned_blocks, rows * owned_blocks
    slots, edge = tiles_ref.shape[2], tiles_ref.shape[3]
    group_total = arrived.shape[0]
    group = slots // group_total
    row, col = lax.axis_index("row"), lax.axis_index("col")

    def arrival(index):
        span = pl.ds(index * group, group)
        return pltpu.make_async_copy(tiles_ref.at[0, 0, span], buffer.at[span], arrived.at[index])

    copies = [
        pltpu.make_async_copy(source, place, small.at[index])
        for index, (source, place) in enumerate(
            ((out_hbm, out_ref), (in_hbm, in_ref), (seeds_hbm, seeds_ref))
        )
    ]
    for copy in copies:
        copy.start()
    for index in range(min(FLIGHT, group_total)):
        arrival(index).start()

    buffer[slots] = jnp.zeros((edge, edge), jnp.bfloat16)
    total[...] = jnp.zeros(total.shape, jnp.float32)

    for copy in copies:
        copy.wait()
    seed_total, sets = seeds_ref.shape
    owned = owned_blocks * edge
    vertex = lax.broadcasted_iota(jnp.int32, (owned, sets), 0) + (row * cols + col) * owned
    restart = jnp.zeros((owned, sets), jnp.float32)
    for seed in range(seed_total):
        restart += (seeds_ref[seed:seed + 1, :] == vertex).astype(jnp.float32)
    restart_ref[...] = (1.0 - damping) * restart.T

    occupied = count_ref[0, 0]

    def add_group(index, carry):
        arrival(index).wait()

        @pl.when(index + FLIGHT < group_total)
        def _():
            arrival(index + FLIGHT).start()

        first = index * group

        def add_tiles(step, carry):
            at = first + step * UNROLL
            places = []
            for lane in range(UNROLL):
                slot = at + lane
                pair = out_ref[0, 0, slot] * in_blocks + in_ref[0, 0, slot]
                places.append((lane % LANES, pair, jnp.where(slot < occupied, slot, slots)))
            for start in range(0, UNROLL, 2):
                sums = [
                    (lane, pair, total[lane, pair] + buffer[used].astype(jnp.float32))
                    for lane, pair, used in places[start:start + 2]
                ]
                for lane, pair, value in sums:
                    total[lane, pair] = value
            return carry

        here = jnp.clip(occupied - first, 0, group)
        return lax.fori_loop(0, (here + UNROLL - 1) // UNROLL, add_tiles, carry)

    lax.fori_loop(0, group_total, add_group, 0)

    for place in range(rows):
        owner = row ^ place if rows == 2 else place
        for block in range(owned_blocks):
            columns = slice(place * owned + block * edge, place * owned + (block + 1) * edge)
            for source in range(in_blocks):
                pair = (owner * owned_blocks + block) * in_blocks + source
                value = (total[0, pair] + total[1, pair]) + (total[2, pair] + total[3, pair])
                high = value.astype(jnp.bfloat16)
                low = (value - high.astype(jnp.float32)).astype(jnp.bfloat16)
                lines = source // owned_blocks, source % owned_blocks * edge
                weight_ref[lines[0], lines[1]:lines[1] + edge, columns] = high
                weight_ref[lines[0], owned + lines[1]:owned + lines[1] + edge, columns] = low


def product_kernel(rows, cols, *refs):
    parts, (weight_ref, *result_refs) = refs[:cols], refs[cols:]
    col = lax.axis_index("col")
    incoming = None
    for offset in range(cols):
        scaled = parts[offset][...]
        term = jnp.dot(
            jnp.concatenate([scaled, scaled], axis=1),
            weight_ref[partner(col, offset, cols)],
            preferred_element_type=jnp.float32,
        )
        incoming = term if incoming is None else incoming + term
    owned = incoming.shape[1] // rows
    if len(result_refs) == 1:
        for place in range(rows):
            result_refs[0][place] = incoming[:, place * owned:(place + 1) * owned]
    else:
        for place in range(rows):
            result_refs[place][...] = incoming[:, place * owned:(place + 1) * owned]


def finish_kernel(last, *refs):
    *incoming_refs, restart_ref, degree_ref, result_ref = refs
    incoming = sum(ref[...] for ref in incoming_refs)
    risk = restart_ref[...] + damping * incoming
    if last:
        result_ref[...] = risk
    else:
        result_ref[...] = (risk / degree_ref[...].astype(jnp.float32)).astype(jnp.bfloat16)


def local(tiles, tile_out, tile_in, tile_count, out_degree, seed_ids, prior):
    rows, cols = lax.axis_size("row"), lax.axis_size("col")
    sets, owned = prior.shape
    slots, edge = tiles.shape[2], tiles.shape[3]
    owned_blocks = owned // edge
    in_blocks, out_blocks = cols * owned_blocks, rows * owned_blocks
    group = math.gcd(slots, 32)
    degree = out_degree.reshape(1, owned)
    low = jnp.bfloat16

    scaled = call(
        scale_kernel,
        jax.ShapeDtypeStruct((sets, owned), low),
        "scale",
        in_specs=[HBM, HBM],
        out_specs=VMEM,
        scratch_shapes=[
            pltpu.VMEM((sets, owned), jnp.float32),
            pltpu.VMEM((1, owned), jnp.int32),
            pltpu.SemaphoreType.DMA((2,)),
        ],
        size=6 * sets * owned,
    )(*in_hbm(prior, degree))

    def spread(value):
        return [value] + [from_column(value, cols, offset) for offset in range(cols - 1, 0, -1)][::-1]

    parts = spread(scaled)

    weight, restart = call(
        functools.partial(sum_kernel, rows, cols, owned_blocks),
        [
            jax.ShapeDtypeStruct((cols, 2 * owned, rows * owned), low),
            jax.ShapeDtypeStruct((sets, owned), jnp.float32),
        ],
        "sum_tiles",
        in_specs=[ANY, SMEM] + [HBM] * 4,
        out_specs=[VMEM] * 2,
        scratch_shapes=[
            pltpu.VMEM((slots + 1, edge, edge), low),
            pltpu.VMEM((LANES, out_blocks * in_blocks, edge, edge), jnp.float32),
            pltpu.SMEM(tile_out.shape, jnp.int32),
            pltpu.SMEM(tile_in.shape, jnp.int32),
            pltpu.VMEM((seed_ids.shape[1], sets), jnp.int32),
            pltpu.SemaphoreType.DMA((slots // group,)),
            pltpu.SemaphoreType.DMA((3,)),
        ],
        vmem=TILES_VMEM,
        flops=slots * edge * edge,
        size=2 * slots * edge * edge,
    )(scaled, tile_count, *in_hbm(tiles, tile_out, tile_in, seed_ids.T))

    for round_index in range(ITERATIONS):
        last = round_index == ITERATIONS - 1
        piece = jax.ShapeDtypeStruct((sets, owned), jnp.float32)
        partial_value = call(
            functools.partial(product_kernel, rows, cols),
            [piece] * 2 if rows == 2 else jax.ShapeDtypeStruct((rows, sets, owned), jnp.float32),
            "product",
            in_specs=[VMEM] * (cols + 1),
            out_specs=[VMEM] * 2 if rows == 2 else VMEM,
            flops=4 * sets * cols * owned * rows * owned,
            size=2 * cols * owned * (sets + 2 * rows * owned),
        )(*parts, weight)
        if rows == 2:
            incoming = (partial_value[0], swap_rows(partial_value[1]))
        else:
            incoming = (lax.psum_scatter(partial_value, "row", scatter_dimension=0, tiled=False),)
        value = call(
            functools.partial(finish_kernel, last),
            piece if last else jax.ShapeDtypeStruct((sets, owned), low),
            "last" if last else "next",
            in_specs=[VMEM] * (len(incoming) + 2),
            out_specs=VMEM,
            size=12 * sets * owned,
        )(*incoming, restart, degree)
        if not last:
            parts = spread(value)
    return value


def solution(mesh):
    placed = (
        P("row", "col", None, None, None),
        P("row", "col", None),
        P("row", "col", None),
        P("row", "col"),
        P(("row", "col")),
        P("seed", None),
        P("seed", ("row", "col")),
    )
    return jax.shard_map(
        local, mesh=mesh, in_specs=placed, out_specs=P("seed", ("row", "col")), check_vma=False
    )
```

```python
import functools

import jax
import jax.numpy as jnp
from jax import lax
from jax.experimental import pallas as pl
from jax.experimental.pallas import tpu as pltpu
from jax.sharding import PartitionSpec as P

ITERATIONS = 2


damping = 0.85

VMEM = pl.BlockSpec(memory_space=pltpu.VMEM)
SMEM = pl.BlockSpec(memory_space=pltpu.SMEM)
HBM = pl.BlockSpec(memory_space=pltpu.HBM)
ANY = pl.BlockSpec(memory_space=pl.ANY)

TILES_VMEM = 32 * 1024 * 1024
SMALL_VMEM = 8 * 1024 * 1024
LANES = 4
UNROLL = 8


def in_hbm(*arrays):
    return [pltpu.with_memory_space_constraint(array, pltpu.HBM) for array in arrays]


def call(kernel, out_shape, name, **options):
    return pl.pallas_call(
        kernel,
        out_shape=out_shape,
        compiler_params=pltpu.CompilerParams(vmem_limit_bytes=options.pop("vmem", SMALL_VMEM)),
        cost_estimate=pl.CostEstimate(
            flops=options.pop("flops", 0), bytes_accessed=options.pop("size", 0), transcendentals=0
        ),
        name=name,
        **options,
    )


def partner(index, offset, extent):
    if extent & (extent - 1) == 0:
        return index ^ offset
    return (index + offset) % extent


def from_column(value, cols, offset):
    return lax.ppermute(value, "col", [(partner(col, offset, cols), col) for col in range(cols)])


def swap_rows(value):
    return lax.ppermute(value, "row", [(0, 1), (1, 0)])


def scale_kernel(
    prior_hbm, degree_hbm, out_hbm, in_hbm, seeds_hbm,
    scaled_ref, out_ref, in_ref, seeds_ref, prior_ref, degree_ref, arrived,
):
    moves = (
        (prior_hbm, prior_ref), (degree_hbm, degree_ref),
        (out_hbm, out_ref), (in_hbm, in_ref), (seeds_hbm, seeds_ref),
    )
    copies = [
        pltpu.make_async_copy(source, place, arrived.at[index])
        for index, (source, place) in enumerate(moves)
    ]
    for copy in copies:
        copy.start()
    for copy in copies[:2]:
        copy.wait()
    scaled_ref[...] = (prior_ref[...] / degree_ref[...].astype(jnp.float32)).astype(jnp.bfloat16)
    for copy in copies[2:]:
        copy.wait()


def sum_kernel(
    rows, cols, owned_blocks, scaled_ref, count_ref, out_ref, in_ref, tiles_ref, seeds_ref,
    weight_ref, restart_ref, total,
):
    in_blocks = cols * owned_blocks
    slots, edge = tiles_ref.shape[2], tiles_ref.shape[3]
    row, col = lax.axis_index("row"), lax.axis_index("col")

    total[...] = jnp.zeros(total.shape, jnp.float32)

    seed_total, sets = seeds_ref.shape
    owned = owned_blocks * edge
    vertex = lax.broadcasted_iota(jnp.int32, (owned, sets), 0) + (row * cols + col) * owned
    restart = jnp.zeros((owned, sets), jnp.float32)
    for seed in range(seed_total):
        restart += (seeds_ref[seed:seed + 1, :] == vertex).astype(jnp.float32)
    restart_ref[...] = (1.0 - damping) * restart.T

    occupied = count_ref[0, 0]
    spare = total.shape[1] - 1

    def add_tiles(step, carry):
        at = step * UNROLL
        places = []
        for lane in range(UNROLL):
            slot = at + lane
            pair = out_ref[0, 0, slot] * in_blocks + in_ref[0, 0, slot]
            places.append((lane % LANES, jnp.where(slot < occupied, pair, spare), slot))
        for start in range(0, UNROLL, 2):
            sums = [
                (lane, pair, total[lane, pair] + tiles_ref[0, 0, slot].astype(jnp.float32))
                for lane, pair, slot in places[start:start + 2]
            ]
            for lane, pair, value in sums:
                total[lane, pair] = value
        return carry

    lax.fori_loop(0, (occupied + UNROLL - 1) // UNROLL, add_tiles, 0)

    for place in range(rows):
        owner = row ^ place if rows == 2 else place
        for block in range(owned_blocks):
            columns = slice(place * owned + block * edge, place * owned + (block + 1) * edge)
            for source in range(in_blocks):
                pair = (owner * owned_blocks + block) * in_blocks + source
                value = (total[0, pair] + total[1, pair]) + (total[2, pair] + total[3, pair])
                high = value.astype(jnp.bfloat16)
                low = (value - high.astype(jnp.float32)).astype(jnp.bfloat16)
                lines = source // owned_blocks, source % owned_blocks * edge
                weight_ref[lines[0], lines[1]:lines[1] + edge, columns] = high
                weight_ref[lines[0], owned + lines[1]:owned + lines[1] + edge, columns] = low


def product_kernel(rows, cols, *refs):
    parts, (weight_ref, *result_refs) = refs[:cols], refs[cols:]
    col = lax.axis_index("col")
    incoming = None
    for offset in range(cols):
        scaled = parts[offset][...]
        term = jnp.dot(
            jnp.concatenate([scaled, scaled], axis=1),
            weight_ref[partner(col, offset, cols)],
            preferred_element_type=jnp.float32,
        )
        incoming = term if incoming is None else incoming + term
    owned = incoming.shape[1] // rows
    if len(result_refs) == 1:
        for place in range(rows):
            result_refs[0][place] = incoming[:, place * owned:(place + 1) * owned]
    else:
        for place in range(rows):
            result_refs[place][...] = incoming[:, place * owned:(place + 1) * owned]


def finish_kernel(last, *refs):
    *incoming_refs, restart_ref, degree_ref, result_ref = refs
    incoming = sum(ref[...] for ref in incoming_refs)
    risk = restart_ref[...] + damping * incoming
    if last:
        result_ref[...] = risk
    else:
        result_ref[...] = (risk / degree_ref[...].astype(jnp.float32)).astype(jnp.bfloat16)


def local(tiles, tile_out, tile_in, tile_count, out_degree, seed_ids, prior):
    rows, cols = lax.axis_size("row"), lax.axis_size("col")
    sets, owned = prior.shape
    slots, edge = tiles.shape[2], tiles.shape[3]
    owned_blocks = owned // edge
    in_blocks, out_blocks = cols * owned_blocks, rows * owned_blocks
    degree = out_degree.reshape(1, owned)
    low = jnp.bfloat16

    scaled, out_ids, in_ids, seeds = call(
        scale_kernel,
        [
            jax.ShapeDtypeStruct((sets, owned), low),
            pltpu.SMEM(tile_out.shape, jnp.int32),
            pltpu.SMEM(tile_in.shape, jnp.int32),
            jax.ShapeDtypeStruct((seed_ids.shape[1], sets), jnp.int32),
        ],
        "scale",
        in_specs=[HBM] * 5,
        out_specs=[VMEM, SMEM, SMEM, VMEM],
        scratch_shapes=[
            pltpu.VMEM((sets, owned), jnp.float32),
            pltpu.VMEM((1, owned), jnp.int32),
            pltpu.SemaphoreType.DMA((5,)),
        ],
        flops=16 * slots * edge**3,
        size=6 * sets * owned,
    )(*in_hbm(prior, degree, tile_out, tile_in, seed_ids.T))

    def spread(value):
        return [value] + [from_column(value, cols, offset) for offset in range(cols - 1, 0, -1)][::-1]

    parts = spread(scaled)

    weight, restart = call(
        functools.partial(sum_kernel, rows, cols, owned_blocks),
        [
            jax.ShapeDtypeStruct((cols, 2 * owned, rows * owned), low),
            jax.ShapeDtypeStruct((sets, owned), jnp.float32),
        ],
        "sum_tiles",
        in_specs=[ANY] + [SMEM] * 3 + [VMEM] * 2,
        out_specs=[VMEM] * 2,
        scratch_shapes=[pltpu.VMEM((LANES, out_blocks * in_blocks + 1, edge, edge), jnp.float32)],
        vmem=TILES_VMEM,
        flops=slots * edge * edge,
        size=2 * slots * edge * edge,
    )(
        scaled, tile_count, out_ids, in_ids,
        tiles, seeds,
    )

    for round_index in range(ITERATIONS):
        last = round_index == ITERATIONS - 1
        piece = jax.ShapeDtypeStruct((sets, owned), jnp.float32)
        partial_value = call(
            functools.partial(product_kernel, rows, cols),
            [piece] * 2 if rows == 2 else jax.ShapeDtypeStruct((rows, sets, owned), jnp.float32),
            "product",
            in_specs=[VMEM] * (cols + 1),
            out_specs=[VMEM] * 2 if rows == 2 else VMEM,
            flops=4 * sets * cols * owned * rows * owned,
            size=2 * cols * owned * (sets + 2 * rows * owned),
        )(*parts, weight)
        if rows == 2:
            incoming = (partial_value[0], swap_rows(partial_value[1]))
        else:
            incoming = (lax.psum_scatter(partial_value, "row", scatter_dimension=0, tiled=False),)
        value = call(
            functools.partial(finish_kernel, last),
            piece if last else jax.ShapeDtypeStruct((sets, owned), low),
            "last" if last else "next",
            in_specs=[VMEM] * (len(incoming) + 2),
            out_specs=VMEM,
            size=12 * sets * owned,
        )(*incoming, restart, degree)
        if not last:
            parts = spread(value)
    return value


def solution(mesh):
    placed = (
        P("row", "col", None, None, None),
        P("row", "col", None),
        P("row", "col", None),
        P("row", "col"),
        P(("row", "col")),
        P("seed", None),
        P("seed", ("row", "col")),
    )
    return jax.shard_map(
        local, mesh=mesh, in_specs=placed, out_specs=P("seed", ("row", "col")), check_vma=False
    )
```

```python
import functools
import math

import jax
import jax.numpy as jnp
from jax import lax
from jax.experimental import pallas as pl
from jax.experimental.pallas import tpu as pltpu
from jax.sharding import PartitionSpec as P

ITERATIONS = 2


damping = 0.85

VMEM = pl.BlockSpec(memory_space=pltpu.VMEM)
SMEM = pl.BlockSpec(memory_space=pltpu.SMEM)
HBM = pl.BlockSpec(memory_space=pltpu.HBM)
ANY = pl.BlockSpec(memory_space=pl.ANY)

TILES_VMEM = 32 * 1024 * 1024
SMALL_VMEM = 8 * 1024 * 1024
LANES = 4
UNROLL = 8


def in_hbm(*arrays):
    return [pltpu.with_memory_space_constraint(array, pltpu.HBM) for array in arrays]


def call(kernel, out_shape, name, **options):
    return pl.pallas_call(
        kernel,
        out_shape=out_shape,
        compiler_params=pltpu.CompilerParams(vmem_limit_bytes=options.pop("vmem", SMALL_VMEM)),
        cost_estimate=pl.CostEstimate(
            flops=options.pop("flops", 0), bytes_accessed=options.pop("size", 0), transcendentals=0
        ),
        name=name,
        **options,
    )


def partner(index, offset, extent):
    if extent & (extent - 1) == 0:
        return index ^ offset
    return (index + offset) % extent


def from_column(value, cols, offset):
    return lax.ppermute(value, "col", [(partner(col, offset, cols), col) for col in range(cols)])


def swap_rows(value):
    return lax.ppermute(value, "row", [(0, 1), (1, 0)])


def scale_kernel(
    prior_hbm, degree_hbm, out_hbm, in_hbm, seeds_hbm,
    scaled_ref, out_ref, in_ref, seeds_ref, prior_ref, degree_ref, arrived,
):
    moves = (
        (prior_hbm, prior_ref), (degree_hbm, degree_ref),
        (out_hbm, out_ref), (in_hbm, in_ref), (seeds_hbm, seeds_ref),
    )
    copies = [
        pltpu.make_async_copy(source, place, arrived.at[index])
        for index, (source, place) in enumerate(moves)
    ]
    for copy in copies:
        copy.start()
    for copy in copies[:2]:
        copy.wait()
    scaled_ref[...] = (prior_ref[...] / degree_ref[...].astype(jnp.float32)).astype(jnp.bfloat16)
    for copy in copies[2:]:
        copy.wait()


def first_at_least(ids_ref, block, end):
    def halve(step, bounds):
        low, high = bounds
        middle = (low + high) // 2
        below = ids_ref[0, 0, jnp.minimum(middle, ids_ref.shape[2] - 1)] < block
        searching = low < high
        return (
            jnp.where(searching & below, middle + 1, low),
            jnp.where(searching & ~below, middle, high),
        )

    return lax.fori_loop(0, ids_ref.shape[2].bit_length(), halve, (jnp.int32(0), end))[0]


def sum_kernel(
    rows, cols, owned_blocks, place, after_ref, count_ref, out_ref, in_ref, tiles_ref, weight_ref, total
):
    in_blocks = cols * owned_blocks
    slots, edge = tiles_ref.shape[2], tiles_ref.shape[3]
    owned = owned_blocks * edge
    spare = total.shape[1] - 1
    unroll = math.gcd(slots, UNROLL)

    total[...] = jnp.zeros(total.shape, jnp.float32)

    first_block, begin, end = 0, 0, count_ref[0, 0]
    if place is not None:
        first_block = partner(lax.axis_index("row"), place, rows) * owned_blocks
        begin = first_at_least(out_ref, first_block, end)
        end = first_at_least(out_ref, first_block + owned_blocks, end)

    def add_tiles(step, carry):
        at = step * unroll
        places = []
        for lane in range(unroll):
            slot = at + lane
            pair = (out_ref[0, 0, slot] - first_block) * in_blocks + in_ref[0, 0, slot]
            used = (slot >= begin) & (slot < end)
            places.append((lane % LANES, jnp.where(used, pair, spare), slot))
        for start in range(0, unroll, 2):
            sums = [
                (lane, pair, total[lane, pair] + tiles_ref[0, 0, slot].astype(jnp.float32))
                for lane, pair, slot in places[start:start + 2]
            ]
            for lane, pair, value in sums:
                total[lane, pair] = value
        return carry

    lax.fori_loop(begin // unroll, (end + unroll - 1) // unroll, add_tiles, 0)

    for block in range(spare // in_blocks):
        columns = slice(block * edge, (block + 1) * edge)
        for source in range(in_blocks):
            pair = block * in_blocks + source
            value = (total[0, pair] + total[1, pair]) + (total[2, pair] + total[3, pair])
            high = value.astype(jnp.bfloat16)
            low = (value - high.astype(jnp.float32)).astype(jnp.bfloat16)
            column, line = source // owned_blocks, source % owned_blocks * edge
            weight_ref[column, line:line + edge, columns] = high
            weight_ref[column, owned + line:owned + line + edge, columns] = low


def restart_kernel(rows, cols, after_ref, seeds_ref, restart_ref):
    seed_total, sets = seeds_ref.shape
    owned = restart_ref.shape[1]
    first = (lax.axis_index("row") * cols + lax.axis_index("col")) * owned
    vertex = lax.broadcasted_iota(jnp.int32, (owned, sets), 0) + first
    restart = jnp.zeros((owned, sets), jnp.float32)
    for seed in range(seed_total):
        restart += (seeds_ref[seed:seed + 1, :] == vertex).astype(jnp.float32)
    restart_ref[...] = (1.0 - damping) * restart.T


def product_kernel(cols, after, *refs):
    *parts, weight_ref, result_ref = refs[after:]
    col = lax.axis_index("col")
    incoming = None
    for offset in range(cols):
        scaled = parts[offset][...]
        term = jnp.dot(
            jnp.concatenate([scaled, scaled], axis=1),
            weight_ref[partner(col, offset, cols)],
            preferred_element_type=jnp.float32,
        )
        incoming = term if incoming is None else incoming + term
    if len(result_ref.shape) == 2:
        result_ref[...] = incoming
    else:
        owned = result_ref.shape[2]
        for place in range(result_ref.shape[0]):
            result_ref[place] = incoming[:, place * owned:(place + 1) * owned]


def finish_kernel(last, *refs):
    *incoming_refs, restart_ref, degree_ref, result_ref = refs
    incoming = sum(ref[...] for ref in incoming_refs)
    risk = restart_ref[...] + damping * incoming
    if last:
        result_ref[...] = risk
    else:
        result_ref[...] = (risk / degree_ref[...].astype(jnp.float32)).astype(jnp.bfloat16)


def local(tiles, tile_out, tile_in, tile_count, out_degree, seed_ids, prior):
    rows, cols = lax.axis_size("row"), lax.axis_size("col")
    sets, owned = prior.shape
    slots, edge = tiles.shape[2], tiles.shape[3]
    owned_blocks = owned // edge
    in_blocks, out_blocks = cols * owned_blocks, rows * owned_blocks
    degree = out_degree.reshape(1, owned)
    low = jnp.bfloat16

    scaled, out_ids, in_ids, seeds = call(
        scale_kernel,
        [
            jax.ShapeDtypeStruct((sets, owned), low),
            pltpu.SMEM(tile_out.shape, jnp.int32),
            pltpu.SMEM(tile_in.shape, jnp.int32),
            jax.ShapeDtypeStruct((seed_ids.shape[1], sets), jnp.int32),
        ],
        "scale",
        in_specs=[HBM] * 5,
        out_specs=[VMEM, SMEM, SMEM, VMEM],
        scratch_shapes=[
            pltpu.VMEM((sets, owned), jnp.float32),
            pltpu.VMEM((1, owned), jnp.int32),
            pltpu.SemaphoreType.DMA((5,)),
        ],
        flops=16 * slots * edge**3,
        size=6 * sets * owned,
    )(*in_hbm(prior, degree, tile_out, tile_in, seed_ids.T))

    def spread(value):
        return [value] + [from_column(value, cols, offset) for offset in range(cols - 1, 0, -1)][::-1]

    parts = spread(scaled)

    def add_up(place, after):
        pair_total = in_blocks * (owned_blocks if place is not None else out_blocks)
        return call(
            functools.partial(sum_kernel, rows, cols, owned_blocks, place),
            jax.ShapeDtypeStruct((cols, 2 * owned, pair_total // in_blocks * edge), low),
            "sum_tiles",
            in_specs=[ANY] + [SMEM] * 3 + [VMEM],
            out_specs=VMEM,
            scratch_shapes=[pltpu.VMEM((LANES, pair_total + 1, edge, edge), jnp.float32)],
            vmem=TILES_VMEM,
            flops=slots * edge * edge,
            size=2 * slots * edge * edge,
        )(after, tile_count, out_ids, in_ids, tiles)

    def multiply(parts, weight, after=()):
        shape = (sets, owned) if weight.shape[2] == owned else (rows, sets, owned)
        return call(
            functools.partial(product_kernel, cols, len(after)),
            jax.ShapeDtypeStruct(shape, jnp.float32),
            "product",
            in_specs=[ANY] * len(after) + [VMEM] * (cols + 1),
            out_specs=VMEM,
            flops=2 * sets * weight.size,
            size=2 * weight.size,
        )(*after, *parts, weight)

    def count_restart(after):
        return call(
            functools.partial(restart_kernel, rows, cols),
            jax.ShapeDtypeStruct((sets, owned), jnp.float32),
            "restart",
            in_specs=[ANY, VMEM],
            out_specs=VMEM,
            flops=2 * sets * owned * seed_ids.shape[1],
            size=4 * sets * owned,
        )(after, seeds)

    def finish(incoming, restart, last):
        return call(
            functools.partial(finish_kernel, last),
            jax.ShapeDtypeStruct((sets, owned), jnp.float32 if last else low),
            "last" if last else "next",
            in_specs=[VMEM] * (len(incoming) + 2),
            out_specs=VMEM,
            size=12 * sets * owned,
        )(*incoming, restart, degree)

    paired = rows == 2
    weight = add_up(1 if paired else None, scaled)
    for round_index in range(ITERATIONS):
        last = round_index == ITERATIONS - 1
        partial_value = multiply(parts, weight)
        if paired:
            received = swap_rows(partial_value)
            if not round_index:
                own_weight = add_up(0, partial_value)
                restart = count_restart(own_weight)
            incoming = (multiply(parts, own_weight, (partial_value,)), received)
        else:
            if not round_index:
                restart = count_restart(weight)
            incoming = (lax.psum_scatter(partial_value, "row", scatter_dimension=0, tiled=False),)
        value = finish(incoming, restart, last)
        if not last:
            parts = spread(value)
    return value


def solution(mesh):
    placed = (
        P("row", "col", None, None, None),
        P("row", "col", None),
        P("row", "col", None),
        P("row", "col"),
        P(("row", "col")),
        P("seed", None),
        P("seed", ("row", "col")),
    )
    return jax.shard_map(
        local, mesh=mesh, in_specs=placed, out_specs=P("seed", ("row", "col")), check_vma=False
    )
```

```python
import functools
import math

import jax
import jax.numpy as jnp
from jax import lax
from jax.experimental import pallas as pl
from jax.experimental.pallas import tpu as pltpu
from jax.sharding import PartitionSpec as P

ITERATIONS = 2


damping = 0.85

VMEM = pl.BlockSpec(memory_space=pltpu.VMEM)
SMEM = pl.BlockSpec(memory_space=pltpu.SMEM)
HBM = pl.BlockSpec(memory_space=pltpu.HBM)
ANY = pl.BlockSpec(memory_space=pl.ANY)

TILES_VMEM = 32 * 1024 * 1024
SMALL_VMEM = 8 * 1024 * 1024
LANES = 4
UNROLL = 8
DEGREE_LINES = 8


def in_hbm(*arrays):
    return [pltpu.with_memory_space_constraint(array, pltpu.HBM) for array in arrays]


def call(kernel, out_shape, name, **options):
    return pl.pallas_call(
        kernel,
        out_shape=out_shape,
        compiler_params=pltpu.CompilerParams(vmem_limit_bytes=options.pop("vmem", SMALL_VMEM)),
        cost_estimate=pl.CostEstimate(
            flops=options.pop("flops", 0), bytes_accessed=options.pop("size", 0), transcendentals=0
        ),
        name=name,
        **options,
    )


def partner(index, offset, extent):
    if extent & (extent - 1) == 0:
        return index ^ offset
    return (index + offset) % extent


def offsets(cols):
    return list(range(cols))


def from_column(value, cols, offset):
    return lax.ppermute(value, "col", [(partner(col, offset, cols), col) for col in range(cols)])


def swap_rows(value):
    return lax.ppermute(value, "row", [(0, 1), (1, 0)])


def scale_kernel(
    prior_hbm, degree_hbm, out_hbm, in_hbm, seeds_hbm,
    scaled_ref, out_ref, in_ref, seeds_ref, prior_ref, degree_ref, arrived,
):
    moves = (
        (prior_hbm, prior_ref), (degree_hbm, degree_ref),
        (out_hbm, out_ref), (in_hbm, in_ref), (seeds_hbm, seeds_ref),
    )
    copies = [
        pltpu.make_async_copy(source, place, arrived.at[index])
        for index, (source, place) in enumerate(moves)
    ]
    for copy in copies:
        copy.start()
    for copy in copies[:2]:
        copy.wait()
    scaled_ref[...] = (prior_ref[...] / degree_ref[...].astype(jnp.float32)).astype(jnp.bfloat16)
    for copy in copies[2:]:
        copy.wait()


def sum_kernel(
    rows, cols, owned_blocks, after_ref, count_ref, out_ref, in_ref, tiles_ref, *rest
):
    *weight_refs, total = rest
    in_blocks = cols * owned_blocks
    slots, edge = tiles_ref.shape[2], tiles_ref.shape[3]
    owned = owned_blocks * edge
    spare = total.shape[1] - 1
    unroll = math.gcd(slots, UNROLL)
    row = lax.axis_index("row")
    occupied = count_ref[0, 0]

    total[...] = jnp.zeros(total.shape, jnp.float32)

    def add_tiles(step, carry):
        at = step * unroll
        places = []
        for lane in range(unroll):
            slot = at + lane
            pair = out_ref[0, 0, slot] * in_blocks + in_ref[0, 0, slot]
            places.append((lane % LANES, jnp.where(slot < occupied, pair, spare), slot))
        for start in range(0, unroll, 2):
            sums = [
                (lane, pair, total[lane, pair] + tiles_ref[0, 0, slot].astype(jnp.float32))
                for lane, pair, slot in places[start:start + 2]
            ]
            for lane, pair, value in sums:
                total[lane, pair] = value
        return carry

    lax.fori_loop(0, (occupied + unroll - 1) // unroll, add_tiles, 0)

    for place in range(rows):
        owner = partner(row, place, rows) if rows == 2 else place
        for block in range(owned_blocks):
            columns = slice(block * edge, (block + 1) * edge)
            for source in range(in_blocks):
                pair = (owner * owned_blocks + block) * in_blocks + source
                value = (total[0, pair] + total[1, pair]) + (total[2, pair] + total[3, pair])
                high = value.astype(jnp.bfloat16)
                low = (value - high.astype(jnp.float32)).astype(jnp.bfloat16)
                column, line = source // owned_blocks, source % owned_blocks * edge
                weight_refs[place][column, line:line + edge, columns] = high
                weight_refs[place][column, owned + line:owned + line + edge, columns] = low


def restart_kernel(rows, cols, places, after_ref, seeds_ref, restart_ref):
    seed_total, sets = seeds_ref.shape
    owned = restart_ref.shape[2]
    for place in range(places):
        row = partner(lax.axis_index("row"), place, rows)
        first = (row * cols + lax.axis_index("col")) * owned
        vertex = lax.broadcasted_iota(jnp.int32, (owned, sets), 0) + first
        restart = jnp.zeros((owned, sets), jnp.float32)
        for seed in range(seed_total):
            restart += (seeds_ref[seed:seed + 1, :] == vertex).astype(jnp.float32)
        restart_ref[place] = (1.0 - damping) * restart.T


def times_weight(col, cols, parts, weight_ref):
    incoming = None
    for part, offset in zip(parts, offsets(cols)):
        term = jnp.dot(
            jnp.concatenate([part] * 2, axis=1),
            weight_ref[partner(col, offset, cols)],
            preferred_element_type=jnp.float32,
        )
        incoming = term if incoming is None else incoming + term
    return incoming


def product_kernel(rows, cols, *refs):
    part_refs, weight_refs, (degree_ref, result_ref) = refs[:cols], refs[cols:cols + rows], refs[cols + rows:]
    col = lax.axis_index("col")
    parts = [ref[...] for ref in part_refs]
    sets, owned = parts[0].shape
    for place in range(rows):
        result_ref[place, :sets] = times_weight(col, cols, parts, weight_refs[place])
        if result_ref.shape[1] > sets:
            result_ref[place, sets:] = jnp.broadcast_to(
                degree_ref[...].astype(jnp.float32), (result_ref.shape[1] - sets, owned)
            )


def both_kernel(mine_ref, theirs_ref, restart_ref, weight_ref, scaled_ref, leaving_ref):
    leaving_ref[...] = weight_ref[...]
    sets = restart_ref.shape[1]
    for place in range(2):
        incoming = mine_ref[place, :sets] + theirs_ref[1 - place, :sets]
        degree = (theirs_ref if place else mine_ref)[0, sets:sets + 1]
        risk = restart_ref[place] + damping * incoming
        scaled_ref[place] = (risk / degree).astype(jnp.bfloat16)


def result_kernel(cols, *refs):
    part_refs, weight_refs, (restart_ref, result_ref) = refs[:cols], refs[cols:cols + 2], refs[cols + 2:]
    col = lax.axis_index("col")
    incoming = [
        times_weight(col, cols, [ref[place] for ref in part_refs], weight_refs[place]) for place in range(2)
    ]
    result_ref[...] = restart_ref[0] + damping * (incoming[0] + incoming[1])


def finish_kernel(last, incoming_ref, restart_ref, degree_ref, result_ref):
    risk = restart_ref[0] + damping * incoming_ref[...]
    if last:
        result_ref[...] = risk
    else:
        result_ref[...] = (risk / degree_ref[...].astype(jnp.float32)).astype(jnp.bfloat16)


def local(tiles, tile_out, tile_in, tile_count, out_degree, seed_ids, prior):
    rows, cols = lax.axis_size("row"), lax.axis_size("col")
    sets, owned = prior.shape
    slots, edge = tiles.shape[2], tiles.shape[3]
    owned_blocks = owned // edge
    in_blocks, out_blocks = cols * owned_blocks, rows * owned_blocks
    degree = out_degree.reshape(1, owned)
    low = jnp.bfloat16

    scaled, out_ids, in_ids, seeds = call(
        scale_kernel,
        [
            jax.ShapeDtypeStruct((sets, owned), low),
            pltpu.SMEM(tile_out.shape, jnp.int32),
            pltpu.SMEM(tile_in.shape, jnp.int32),
            jax.ShapeDtypeStruct((seed_ids.shape[1], sets), jnp.int32),
        ],
        "scale",
        in_specs=[HBM] * 5,
        out_specs=[VMEM, SMEM, SMEM, VMEM],
        scratch_shapes=[
            pltpu.VMEM((sets, owned), jnp.float32),
            pltpu.VMEM((1, owned), jnp.int32),
            pltpu.SemaphoreType.DMA((5,)),
        ],
        flops=16 * slots * edge**3,
        size=6 * sets * owned,
    )(*in_hbm(prior, degree, tile_out, tile_in, seed_ids.T))

    def spread(value):
        return [from_column(value, cols, offset) if offset else value for offset in offsets(cols)]

    parts = spread(scaled)

    weights = call(
        functools.partial(sum_kernel, rows, cols, owned_blocks),
        [jax.ShapeDtypeStruct((cols, 2 * owned, owned), low)] * rows,
        "sum_tiles",
        in_specs=[ANY] + [SMEM] * 3 + [VMEM],
        out_specs=[VMEM] * rows,
        scratch_shapes=[pltpu.VMEM((LANES, out_blocks * in_blocks + 1, edge, edge), jnp.float32)],
        vmem=TILES_VMEM,
        flops=slots * edge * edge,
        size=2 * slots * edge * edge,
    )(scaled, tile_count, out_ids, in_ids, tiles)

    def multiply(parts, lines):
        return call(
            functools.partial(product_kernel, rows, cols),
            jax.ShapeDtypeStruct((rows, lines, owned), jnp.float32),
            "product",
            in_specs=[VMEM] * (cols + rows + 1),
            out_specs=VMEM,
            flops=4 * sets * rows * cols * owned * owned,
            size=4 * rows * cols * owned * owned,
        )(*parts, *weights, degree)

    def count_restart(places, after):
        return call(
            functools.partial(restart_kernel, rows, cols, places),
            jax.ShapeDtypeStruct((places, sets, owned), jnp.float32),
            "restart",
            in_specs=[ANY, VMEM],
            out_specs=VMEM,
            flops=2 * places * sets * owned * seed_ids.shape[1],
            size=4 * places * sets * owned,
        )(after, seeds)

    if rows == 2 and ITERATIONS == 2:
        mine = multiply(parts, sets + DEGREE_LINES)
        theirs = swap_rows(mine)
        restart = count_restart(2, mine)
        both, leaving = call(
            both_kernel,
            [jax.ShapeDtypeStruct((2, sets, owned), low), jax.ShapeDtypeStruct(weights[1].shape, low)],
            "both",
            in_specs=[VMEM] * 4,
            out_specs=[VMEM] * 2,
            size=24 * sets * owned,
        )(mine, theirs, restart, weights[1])
        parts = spread(both)
        other_weight = swap_rows(leaving)
        return call(
            functools.partial(result_kernel, cols),
            jax.ShapeDtypeStruct((sets, owned), jnp.float32),
            "result",
            in_specs=[VMEM] * (cols + 3),
            out_specs=VMEM,
            flops=8 * sets * cols * owned * owned,
            size=8 * cols * owned * owned,
        )(*parts, weights[0], other_weight, restart)

    restart = count_restart(1, scaled)
    for round_index in range(ITERATIONS):
        last = round_index == ITERATIONS - 1
        partial_value = multiply(parts, sets)
        incoming = lax.psum_scatter(partial_value, "row", scatter_dimension=0, tiled=False)
        value = call(
            functools.partial(finish_kernel, last),
            jax.ShapeDtypeStruct((sets, owned), jnp.float32 if last else low),
            "last" if last else "next",
            in_specs=[VMEM] * 3,
            out_specs=VMEM,
            size=12 * sets * owned,
        )(incoming, restart, degree)
        if not last:
            parts = spread(value)
    return value


def solution(mesh):
    placed = (
        P("row", "col", None, None, None),
        P("row", "col", None),
        P("row", "col", None),
        P("row", "col"),
        P(("row", "col")),
        P("seed", None),
        P("seed", ("row", "col")),
    )
    return jax.shard_map(
        local, mesh=mesh, in_specs=placed, out_specs=P("seed", ("row", "col")), check_vma=False
    )
```

```python
import functools
import math

import jax
import jax.numpy as jnp
from jax import lax
from jax.experimental import pallas as pl
from jax.experimental.pallas import tpu as pltpu
from jax.sharding import PartitionSpec as P

ITERATIONS = 2


damping = 0.85

VMEM = pl.BlockSpec(memory_space=pltpu.VMEM)
SMEM = pl.BlockSpec(memory_space=pltpu.SMEM)
HBM = pl.BlockSpec(memory_space=pltpu.HBM)
ANY = pl.BlockSpec(memory_space=pl.ANY)

TILES_VMEM = 32 * 1024 * 1024
SMALL_VMEM = 8 * 1024 * 1024
LANES = 4
UNROLL = 8
DEGREE_LINES = 8


def in_hbm(*arrays):
    return [pltpu.with_memory_space_constraint(array, pltpu.HBM) for array in arrays]


def call(kernel, out_shape, name, **options):
    return pl.pallas_call(
        kernel,
        out_shape=out_shape,
        compiler_params=pltpu.CompilerParams(vmem_limit_bytes=options.pop("vmem", SMALL_VMEM)),
        cost_estimate=pl.CostEstimate(
            flops=options.pop("flops", 0), bytes_accessed=options.pop("size", 0), transcendentals=0
        ),
        name=name,
        **options,
    )


def partner(index, offset, extent):
    if extent & (extent - 1) == 0:
        return index ^ offset
    return (index + offset) % extent


def from_column(value, cols, offset):
    return lax.ppermute(value, "col", [(partner(col, offset, cols), col) for col in range(cols)])


def swap_rows(value):
    return lax.ppermute(value, "row", [(0, 1), (1, 0)])


def scale_kernel(
    prior_hbm, degree_hbm, out_hbm, in_hbm, seeds_hbm,
    scaled_ref, out_ref, in_ref, seeds_ref, prior_ref, degree_ref, arrived,
):
    moves = (
        (prior_hbm, prior_ref), (degree_hbm, degree_ref),
        (out_hbm, out_ref), (in_hbm, in_ref), (seeds_hbm, seeds_ref),
    )
    copies = [
        pltpu.make_async_copy(source, place, arrived.at[index])
        for index, (source, place) in enumerate(moves)
    ]
    for copy in copies:
        copy.start()
    for copy in copies[:2]:
        copy.wait()
    scaled = (prior_ref[...] / degree_ref[...].astype(jnp.float32)).astype(jnp.bfloat16)
    for place in range(scaled_ref.shape[0]):
        scaled_ref[place] = scaled
    for copy in copies[2:]:
        copy.wait()


def sum_kernel(
    rows, cols, owned_blocks, after_ref, count_ref, out_ref, in_ref, tiles_ref, *rest
):
    *weight_refs, total = rest
    in_blocks = cols * owned_blocks
    slots, edge = tiles_ref.shape[2], tiles_ref.shape[3]
    owned = owned_blocks * edge
    spare = total.shape[1] - 1
    unroll = math.gcd(slots, UNROLL)
    row = lax.axis_index("row")
    occupied = count_ref[0, 0]

    total[...] = jnp.zeros(total.shape, jnp.float32)

    def add_tiles(step, carry):
        at = step * unroll
        places = []
        for lane in range(unroll):
            slot = at + lane
            pair = out_ref[0, 0, slot] * in_blocks + in_ref[0, 0, slot]
            places.append((lane % LANES, jnp.where(slot < occupied, pair, spare), slot))
        for start in range(0, unroll, 2):
            sums = [
                (lane, pair, total[lane, pair] + tiles_ref[0, 0, slot].astype(jnp.float32))
                for lane, pair, slot in places[start:start + 2]
            ]
            for lane, pair, value in sums:
                total[lane, pair] = value
        return carry

    lax.fori_loop(0, (occupied + unroll - 1) // unroll, add_tiles, 0)

    for place in range(rows):
        owner = partner(row, place, rows) if rows == 2 else place
        for block in range(owned_blocks):
            columns = slice(block * edge, (block + 1) * edge)
            for source in range(in_blocks):
                pair = (owner * owned_blocks + block) * in_blocks + source
                value = (total[0, pair] + total[1, pair]) + (total[2, pair] + total[3, pair])
                high = value.astype(jnp.bfloat16)
                low = (value - high.astype(jnp.float32)).astype(jnp.bfloat16)
                column, line = source // owned_blocks, source % owned_blocks * edge
                lines = slice(line, line + edge)
                weight_refs[place][column, lines, columns] = high
                weight_refs[place][column, lines, owned + block * edge:owned + (block + 1) * edge] = low


def restart_kernel(rows, cols, places, after_ref, seeds_ref, restart_ref):
    seed_total, sets = seeds_ref.shape
    owned = restart_ref.shape[2]
    for place in range(places):
        row = partner(lax.axis_index("row"), place, rows)
        first = (row * cols + lax.axis_index("col")) * owned
        vertex = lax.broadcasted_iota(jnp.int32, (owned, sets), 0) + first
        restart = jnp.zeros((owned, sets), jnp.float32)
        for seed in range(seed_total):
            restart += (seeds_ref[seed:seed + 1, :] == vertex).astype(jnp.float32)
        restart_ref[place] = (1.0 - damping) * restart.T


def times_weight(parts, weights):
    incoming = None
    for start in range(0, len(parts), 2):
        term = jnp.dot(
            jnp.concatenate(parts[start:start + 2], axis=1),
            jnp.concatenate(weights[start:start + 2], axis=0),
            preferred_element_type=jnp.float32,
        )
        incoming = term if incoming is None else incoming + term
    owned = incoming.shape[1] // 2
    return incoming[:, :owned] + incoming[:, owned:]


def product_kernel(rows, cols, gathered, *refs):
    part_count = 1 if gathered else cols
    part_refs, weight_refs = refs[:part_count], refs[part_count:part_count + rows]
    degree_ref, result_ref = refs[part_count + rows:]
    col = lax.axis_index("col")
    if gathered:
        parts, columns = [part_refs[0][column] for column in range(cols)], range(cols)
    else:
        parts, columns = [ref[...] for ref in part_refs], [partner(col, offset, cols) for offset in range(cols)]
    sets, owned = parts[0].shape
    for place in range(rows):
        weights = [weight_refs[place][column] for column in columns]
        result_ref[place, :sets] = times_weight(parts, weights)
        if result_ref.shape[1] > sets:
            result_ref[place, sets:] = jnp.broadcast_to(
                degree_ref[...].astype(jnp.float32), (result_ref.shape[1] - sets, owned)
            )


def both_kernel(mine_ref, theirs_ref, restart_ref, weight_ref, scaled_ref, leaving_ref):
    leaving_ref[...] = weight_ref[...]
    sets = restart_ref.shape[1]
    for place in range(2):
        incoming = mine_ref[place, :sets] + theirs_ref[1 - place, :sets]
        degree = (theirs_ref if place else mine_ref)[0, sets:sets + 1]
        risk = restart_ref[place] + damping * incoming
        scaled_ref[place] = (risk / degree).astype(jnp.bfloat16)


def result_kernel(cols, *refs):
    part_refs, weight_refs, (restart_ref, result_ref) = refs[:cols], refs[cols:cols + 2], refs[cols + 2:]
    col = lax.axis_index("col")
    parts = [ref[place] for place in range(2) for ref in part_refs]
    weights = [
        weight_refs[place][partner(col, offset, cols)] for place in range(2) for offset in range(cols)
    ]
    result_ref[...] = restart_ref[0] + damping * times_weight(parts, weights)


def finish_kernel(last, incoming_ref, restart_ref, degree_ref, result_ref):
    risk = restart_ref[0] + damping * incoming_ref[...]
    if last:
        result_ref[...] = risk
    else:
        result_ref[...] = (risk / degree_ref[...].astype(jnp.float32)).astype(jnp.bfloat16)


def local(tiles, tile_out, tile_in, tile_count, out_degree, seed_ids, prior):
    rows, cols = lax.axis_size("row"), lax.axis_size("col")
    sets, owned = prior.shape
    slots, edge = tiles.shape[2], tiles.shape[3]
    owned_blocks = owned // edge
    in_blocks, out_blocks = cols * owned_blocks, rows * owned_blocks
    degree = out_degree.reshape(1, owned)
    low = jnp.bfloat16

    scaled, out_ids, in_ids, seeds = call(
        scale_kernel,
        [
            jax.ShapeDtypeStruct((cols, sets, owned), low),
            pltpu.SMEM(tile_out.shape, jnp.int32),
            pltpu.SMEM(tile_in.shape, jnp.int32),
            jax.ShapeDtypeStruct((seed_ids.shape[1], sets), jnp.int32),
        ],
        "scale",
        in_specs=[HBM] * 5,
        out_specs=[VMEM, SMEM, SMEM, VMEM],
        scratch_shapes=[
            pltpu.VMEM((sets, owned), jnp.float32),
            pltpu.VMEM((1, owned), jnp.int32),
            pltpu.SemaphoreType.DMA((5,)),
        ],
        flops=16 * slots * edge**3,
        size=6 * sets * owned,
    )(*in_hbm(prior, degree, tile_out, tile_in, seed_ids.T))

    def spread(value):
        return [from_column(value, cols, offset) if offset else value for offset in range(cols)]

    gathered = lax.all_to_all(scaled, "col", split_axis=0, concat_axis=0, tiled=True)

    weights = call(
        functools.partial(sum_kernel, rows, cols, owned_blocks),
        [jax.ShapeDtypeStruct((cols, owned, 2 * owned), low)] * rows,
        "sum_tiles",
        in_specs=[ANY] + [SMEM] * 3 + [VMEM],
        out_specs=[VMEM] * rows,
        scratch_shapes=[pltpu.VMEM((LANES, out_blocks * in_blocks + 1, edge, edge), jnp.float32)],
        vmem=TILES_VMEM,
        flops=slots * edge * edge,
        size=2 * slots * edge * edge,
    )(scaled, tile_count, out_ids, in_ids, tiles)

    def multiply(parts, lines):
        return call(
            functools.partial(product_kernel, rows, cols, len(parts) == 1),
            jax.ShapeDtypeStruct((rows, lines, owned), jnp.float32),
            "product",
            in_specs=[VMEM] * (len(parts) + rows + 1),
            out_specs=VMEM,
            flops=4 * sets * rows * cols * owned * owned,
            size=4 * rows * cols * owned * owned,
        )(*parts, *weights, degree)

    def count_restart(places, after):
        return call(
            functools.partial(restart_kernel, rows, cols, places),
            jax.ShapeDtypeStruct((places, sets, owned), jnp.float32),
            "restart",
            in_specs=[ANY, VMEM],
            out_specs=VMEM,
            flops=2 * places * sets * owned * seed_ids.shape[1],
            size=4 * places * sets * owned,
        )(after, seeds)

    if rows == 2 and ITERATIONS == 2:
        mine = multiply([gathered], sets + DEGREE_LINES)
        theirs = swap_rows(mine)
        restart = count_restart(2, mine)
        both, leaving = call(
            both_kernel,
            [jax.ShapeDtypeStruct((2, sets, owned), low), jax.ShapeDtypeStruct(weights[1].shape, low)],
            "both",
            in_specs=[VMEM] * 4,
            out_specs=[VMEM] * 2,
            size=24 * sets * owned,
        )(mine, theirs, restart, weights[1])
        parts = spread(both)
        other_weight = swap_rows(leaving)
        return call(
            functools.partial(result_kernel, cols),
            jax.ShapeDtypeStruct((sets, owned), jnp.float32),
            "result",
            in_specs=[VMEM] * (cols + 3),
            out_specs=VMEM,
            flops=8 * sets * cols * owned * owned,
            size=8 * cols * owned * owned,
        )(*parts, weights[0], other_weight, restart)

    restart = count_restart(1, scaled)
    parts = [gathered]
    for round_index in range(ITERATIONS):
        last = round_index == ITERATIONS - 1
        partial_value = multiply(parts, sets)
        incoming = lax.psum_scatter(partial_value, "row", scatter_dimension=0, tiled=False)
        value = call(
            functools.partial(finish_kernel, last),
            jax.ShapeDtypeStruct((sets, owned), jnp.float32 if last else low),
            "last" if last else "next",
            in_specs=[VMEM] * 3,
            out_specs=VMEM,
            size=12 * sets * owned,
        )(incoming, restart, degree)
        if not last:
            parts = spread(value)
    return value


def solution(mesh):
    placed = (
        P("row", "col", None, None, None),
        P("row", "col", None),
        P("row", "col", None),
        P("row", "col"),
        P(("row", "col")),
        P("seed", None),
        P("seed", ("row", "col")),
    )
    return jax.shard_map(
        local, mesh=mesh, in_specs=placed, out_specs=P("seed", ("row", "col")), check_vma=False
    )
```

```python
import functools
import math

import jax
import jax.numpy as jnp
from jax import lax
from jax.experimental import pallas as pl
from jax.experimental.pallas import tpu as pltpu
from jax.sharding import PartitionSpec as P

ITERATIONS = 2


damping = 0.85

VMEM = pl.BlockSpec(memory_space=pltpu.VMEM)
SMEM = pl.BlockSpec(memory_space=pltpu.SMEM)
HBM = pl.BlockSpec(memory_space=pltpu.HBM)
ANY = pl.BlockSpec(memory_space=pl.ANY)

TILES_VMEM = 32 * 1024 * 1024
SMALL_VMEM = 8 * 1024 * 1024
LANES = 4
UNROLL = 8
DEGREE_LINES = 16


def in_hbm(*arrays):
    return [pltpu.with_memory_space_constraint(array, pltpu.HBM) for array in arrays]


def call(kernel, out_shape, name, **options):
    return pl.pallas_call(
        kernel,
        out_shape=out_shape,
        compiler_params=pltpu.CompilerParams(vmem_limit_bytes=options.pop("vmem", SMALL_VMEM)),
        cost_estimate=pl.CostEstimate(
            flops=options.pop("flops", 0), bytes_accessed=options.pop("size", 0), transcendentals=0
        ),
        name=name,
        **options,
    )


def partner(index, offset, extent):
    if extent & (extent - 1) == 0:
        return index ^ offset
    return (index + offset) % extent


def from_column(value, rows, cols, offset):
    pairs = [
        (row * cols + partner(col, offset, cols), row * cols + col) for row in rows for col in range(cols)
    ]
    return lax.ppermute(value, ("row", "col"), pairs)


def scale_kernel(
    prior_hbm, degree_hbm, out_hbm, in_hbm, seeds_hbm,
    scaled_ref, out_ref, in_ref, seeds_ref, prior_ref, degree_ref, arrived,
):
    moves = (
        (prior_hbm, prior_ref), (degree_hbm, degree_ref),
        (out_hbm, out_ref), (in_hbm, in_ref), (seeds_hbm, seeds_ref),
    )
    copies = [
        pltpu.make_async_copy(source, place, arrived.at[index])
        for index, (source, place) in enumerate(moves)
    ]
    for copy in copies:
        copy.start()
    for copy in copies[:2]:
        copy.wait()
    degree = degree_ref[...].astype(jnp.float32)
    sets, owned = prior_ref.shape
    scaled_ref[:sets] = (prior_ref[...] / degree).astype(jnp.bfloat16)
    extra = scaled_ref.shape[0] - sets
    if extra:
        scaled_ref[sets:] = jnp.broadcast_to(degree, (extra, owned)).astype(jnp.bfloat16)
    for copy in copies[2:]:
        copy.wait()


def join_kernel(count_ref, mine_ref, theirs_ref, joined_ref, degree_ref):
    sets = joined_ref.shape[1]
    for place, ref in enumerate((mine_ref, theirs_ref)):
        joined_ref[place] = ref[:sets]
        degree_ref[place] = ref[sets:].astype(jnp.float32)


def sum_kernel(
    rows, cols, owned_blocks, after_ref, count_ref, out_ref, in_ref, tiles_ref, *rest
):
    weight_ref, total = rest
    in_blocks = cols * owned_blocks
    slots, edge = tiles_ref.shape[2], tiles_ref.shape[3]
    owned = owned_blocks * edge
    spare = total.shape[1] - 1
    unroll = math.gcd(slots, UNROLL)
    row = lax.axis_index("row")
    occupied = count_ref[0, 0]

    total[...] = jnp.zeros(total.shape, jnp.float32)

    def add_tiles(step, carry):
        at = step * unroll
        places = []
        for lane in range(unroll):
            slot = at + lane
            pair = out_ref[0, 0, slot] * in_blocks + in_ref[0, 0, slot]
            places.append((lane % LANES, jnp.where(slot < occupied, pair, spare), slot))
        for start in range(0, unroll, 2):
            sums = [
                (lane, pair, total[lane, pair] + tiles_ref[0, 0, slot].astype(jnp.float32))
                for lane, pair, slot in places[start:start + 2]
            ]
            for lane, pair, value in sums:
                total[lane, pair] = value
        return carry

    lax.fori_loop(0, (occupied + unroll - 1) // unroll, add_tiles, 0)

    for place in range(rows):
        owner = partner(row, place, rows) if rows == 2 else place
        for block in range(owned_blocks):
            columns = slice(block * edge, (block + 1) * edge)
            for source in range(in_blocks):
                pair = (owner * owned_blocks + block) * in_blocks + source
                value = (total[0, pair] + total[1, pair]) + (total[2, pair] + total[3, pair])
                high = value.astype(jnp.bfloat16)
                low = (value - high.astype(jnp.float32)).astype(jnp.bfloat16)
                column, line = source // owned_blocks, source % owned_blocks * edge
                lines = slice(line, line + edge)
                weight_ref[place, column, lines, columns] = high
                weight_ref[place, column, lines, owned + block * edge:owned + (block + 1) * edge] = low


def leave_kernel(after, *refs):
    source_ref, leaving_ref = refs[after:]
    leaving_ref[...] = source_ref[...]


def restart_kernel(rows, cols, places, after_ref, seeds_ref, restart_ref):
    seed_total, sets = seeds_ref.shape
    owned = restart_ref.shape[2]
    for place in range(places):
        row = partner(lax.axis_index("row"), place, rows)
        first = (row * cols + lax.axis_index("col")) * owned
        vertex = lax.broadcasted_iota(jnp.int32, (owned, sets), 0) + first
        restart = jnp.zeros((owned, sets), jnp.float32)
        for seed in range(seed_total):
            restart += (seeds_ref[seed:seed + 1, :] == vertex).astype(jnp.float32)
        restart_ref[place] = (1.0 - damping) * restart.T


def times_weight(parts, weights):
    incoming = None
    for start in range(0, len(parts), 2):
        term = jnp.dot(
            jnp.concatenate(parts[start:start + 2], axis=1),
            jnp.concatenate(weights[start:start + 2], axis=0),
            preferred_element_type=jnp.float32,
        )
        incoming = term if incoming is None else incoming + term
    owned = incoming.shape[1] // 2
    return incoming[:, :owned] + incoming[:, owned:]


def round_kernel(cols, last, *refs):
    part_refs, (mine_ref, theirs_ref, restart_ref, degree_ref, *result_refs) = refs[:cols], refs[cols:]
    col = lax.axis_index("col")
    columns = [partner(col, offset, cols) for offset in range(cols)]
    parts = [ref[place] for place in range(2) for ref in part_refs]
    for block in range(2):
        weights = [mine_ref[block, column] for column in columns]
        weights += [theirs_ref[1 - block, column] for column in columns]
        risk = restart_ref[block] + damping * times_weight(parts, weights)
        if last:
            result_refs[block][...] = risk
        else:
            result_refs[0][block] = (risk / jnp.maximum(degree_ref[block, :1], 1.0)).astype(jnp.bfloat16)


def result_kernel(mine_ref, received_ref, result_ref):
    result_ref[...] = jnp.where(lax.axis_index("row") == 1, mine_ref[...], received_ref[...])


def product_kernel(rows, cols, *refs):
    part_refs, (weight_ref, result_ref) = refs[:cols], refs[cols:]
    col = lax.axis_index("col")
    parts = [ref[...] for ref in part_refs]
    for place in range(rows):
        weights = [weight_ref[place, partner(col, offset, cols)] for offset in range(cols)]
        result_ref[place] = times_weight(parts, weights)


def finish_kernel(last, incoming_ref, restart_ref, degree_ref, result_ref):
    risk = restart_ref[0] + damping * incoming_ref[...]
    if last:
        result_ref[...] = risk
    else:
        result_ref[...] = (risk / degree_ref[...].astype(jnp.float32)).astype(jnp.bfloat16)


def local(tiles, tile_out, tile_in, tile_count, out_degree, seed_ids, prior):
    rows, cols = lax.axis_size("row"), lax.axis_size("col")
    sets, owned = prior.shape
    slots, edge = tiles.shape[2], tiles.shape[3]
    owned_blocks = owned // edge
    in_blocks, out_blocks = cols * owned_blocks, rows * owned_blocks
    degree = out_degree.reshape(1, owned)
    low = jnp.bfloat16
    paired = rows == 2

    scaled, out_ids, in_ids, seeds = call(
        scale_kernel,
        [
            jax.ShapeDtypeStruct((sets + DEGREE_LINES if paired else sets, owned), low),
            pltpu.SMEM(tile_out.shape, jnp.int32),
            pltpu.SMEM(tile_in.shape, jnp.int32),
            jax.ShapeDtypeStruct((seed_ids.shape[1], sets), jnp.int32),
        ],
        "scale",
        in_specs=[HBM] * 5,
        out_specs=[VMEM, SMEM, SMEM, VMEM],
        scratch_shapes=[
            pltpu.VMEM((sets, owned), jnp.float32),
            pltpu.VMEM((1, owned), jnp.int32),
            pltpu.SemaphoreType.DMA((5,)),
        ],
        flops=16 * slots * edge**3,
        size=6 * sets * owned,
    )(*in_hbm(prior, degree, tile_out, tile_in, seed_ids.T))

    def spread(value):
        talking = [1] if paired else range(rows)
        return [from_column(value, talking, cols, offset) if offset else value for offset in range(cols)]

    if paired:
        scaled, degrees = call(
            join_kernel,
            [
                jax.ShapeDtypeStruct((2, sets, owned), low),
                jax.ShapeDtypeStruct((2, DEGREE_LINES, owned), jnp.float32),
            ],
            "join",
            in_specs=[SMEM] + [VMEM] * 2,
            out_specs=[VMEM] * 2,
            size=8 * sets * owned,
        )(tile_count, scaled, lax.ppermute(scaled, "row", [(0, 1)]))
    parts = spread(scaled)

    weight = call(
        functools.partial(sum_kernel, rows, cols, owned_blocks),
        jax.ShapeDtypeStruct((rows, cols, owned, 2 * owned), low),
        "sum_tiles",
        in_specs=[ANY] + [SMEM] * 3 + [VMEM],
        out_specs=VMEM,
        scratch_shapes=[pltpu.VMEM((LANES, out_blocks * in_blocks + 1, edge, edge), jnp.float32)],
        vmem=TILES_VMEM,
        flops=slots * edge * edge,
        size=2 * slots * edge * edge,
    )(scaled, tile_count, out_ids, in_ids, tiles)

    def count_restart(places, after):
        return call(
            functools.partial(restart_kernel, rows, cols, places),
            jax.ShapeDtypeStruct((places, sets, owned), jnp.float32),
            "restart",
            in_specs=[ANY, VMEM],
            out_specs=VMEM,
            flops=2 * places * sets * owned * seed_ids.shape[1],
            size=4 * places * sets * owned,
        )(after, seeds)

    for round_index in range(ITERATIONS):
        last = round_index == ITERATIONS - 1
        if not round_index and paired:
            leaving = call(
                functools.partial(leave_kernel, cols),
                jax.ShapeDtypeStruct(weight.shape, low),
                "leave",
                in_specs=[ANY] * cols + [VMEM],
                out_specs=VMEM,
                size=4 * weight.size,
            )(*parts, weight)
            other_weight = lax.ppermute(leaving, "row", [(0, 1)])
            restart = count_restart(2, leaving)
        elif not round_index:
            restart = count_restart(1, weight)
        if paired:
            value = call(
                functools.partial(round_kernel, cols, last),
                [jax.ShapeDtypeStruct((sets, owned), jnp.float32)] * 2
                if last
                else jax.ShapeDtypeStruct((2, sets, owned), low),
                "last" if last else "next",
                in_specs=[VMEM] * (cols + 4),
                out_specs=[VMEM] * 2 if last else VMEM,
                flops=16 * sets * cols * owned * owned,
                size=16 * cols * owned * owned,
            )(*parts, weight, other_weight, restart, degrees)
            if last:
                value = call(
                    result_kernel,
                    jax.ShapeDtypeStruct((sets, owned), jnp.float32),
                    "result",
                    in_specs=[VMEM] * 2,
                    out_specs=VMEM,
                    size=12 * sets * owned,
                )(value[0], lax.ppermute(value[1], "row", [(1, 0)]))
        else:
            partial_value = call(
                functools.partial(product_kernel, rows, cols),
                jax.ShapeDtypeStruct((rows, sets, owned), jnp.float32),
                "product",
                in_specs=[VMEM] * (cols + 1),
                out_specs=VMEM,
                flops=4 * sets * rows * cols * owned * owned,
                size=4 * rows * cols * owned * owned,
            )(*parts, weight)
            incoming = lax.psum_scatter(partial_value, "row", scatter_dimension=0, tiled=False)
            value = call(
                functools.partial(finish_kernel, last),
                jax.ShapeDtypeStruct((sets, owned), jnp.float32 if last else low),
                "last" if last else "next",
                in_specs=[VMEM] * 3,
                out_specs=VMEM,
                size=12 * sets * owned,
            )(incoming, restart, degree)
        if not last:
            parts = spread(value)
    return value


def solution(mesh):
    placed = (
        P("row", "col", None, None, None),
        P("row", "col", None),
        P("row", "col", None),
        P("row", "col"),
        P(("row", "col")),
        P("seed", None),
        P("seed", ("row", "col")),
    )
    return jax.shard_map(
        local, mesh=mesh, in_specs=placed, out_specs=P("seed", ("row", "col")), check_vma=False
    )
```

```python
import functools
import math

import jax
import jax.numpy as jnp
from jax import lax
from jax.experimental import pallas as pl
from jax.experimental.pallas import tpu as pltpu
from jax.sharding import PartitionSpec as P

ITERATIONS = 2


damping = 0.85

VMEM = pl.BlockSpec(memory_space=pltpu.VMEM)
SMEM = pl.BlockSpec(memory_space=pltpu.SMEM)
HBM = pl.BlockSpec(memory_space=pltpu.HBM)
ANY = pl.BlockSpec(memory_space=pl.ANY)

TILES_VMEM = 32 * 1024 * 1024
SMALL_VMEM = 8 * 1024 * 1024
LANES = 4
UNROLL = 8


def in_hbm(*arrays):
    return [pltpu.with_memory_space_constraint(array, pltpu.HBM) for array in arrays]


def call(kernel, out_shape, name, **options):
    return pl.pallas_call(
        kernel,
        out_shape=out_shape,
        compiler_params=pltpu.CompilerParams(vmem_limit_bytes=options.pop("vmem", SMALL_VMEM)),
        cost_estimate=pl.CostEstimate(
            flops=options.pop("flops", 0), bytes_accessed=options.pop("size", 0), transcendentals=0
        ),
        name=name,
        **options,
    )


def partner(index, offset, extent):
    if extent & (extent - 1) == 0:
        return index ^ offset
    return (index + offset) % extent


def from_column(value, cols, offset):
    return lax.ppermute(value, "col", [(partner(col, offset, cols), col) for col in range(cols)])


def swap_rows(value):
    return lax.ppermute(value, "row", [(0, 1), (1, 0)])


def scale_kernel(
    prior_hbm, degree_hbm, out_hbm, in_hbm, seeds_hbm,
    scaled_ref, out_ref, in_ref, seeds_ref, prior_ref, degree_ref, arrived,
):
    moves = (
        (prior_hbm, prior_ref), (degree_hbm, degree_ref),
        (out_hbm, out_ref), (in_hbm, in_ref), (seeds_hbm, seeds_ref),
    )
    copies = [
        pltpu.make_async_copy(source, place, arrived.at[index])
        for index, (source, place) in enumerate(moves)
    ]
    for copy in copies:
        copy.start()
    for copy in copies[:2]:
        copy.wait()
    scaled = (prior_ref[...] / degree_ref[...].astype(jnp.float32)).astype(jnp.bfloat16)
    scaled_ref[...] = scaled
    for copy in copies[2:]:
        copy.wait()


def sum_kernel(
    rows, cols, owned_blocks, after_ref, count_ref, out_ref, in_ref, tiles_ref, *rest
):
    *weight_refs, total = rest
    in_blocks = cols * owned_blocks
    slots, edge = tiles_ref.shape[2], tiles_ref.shape[3]
    owned = owned_blocks * edge
    spare = total.shape[1] - 1
    unroll = math.gcd(slots, UNROLL)
    row = lax.axis_index("row")
    occupied = count_ref[0, 0]

    total[...] = jnp.zeros(total.shape, jnp.float32)

    def add_tiles(step, carry):
        at = step * unroll
        places = []
        for lane in range(unroll):
            slot = at + lane
            pair = out_ref[0, 0, slot] * in_blocks + in_ref[0, 0, slot]
            places.append((lane % LANES, jnp.where(slot < occupied, pair, spare), slot))
        for start in range(0, unroll, 2):
            sums = [
                (lane, pair, total[lane, pair] + tiles_ref[0, 0, slot].astype(jnp.float32))
                for lane, pair, slot in places[start:start + 2]
            ]
            for lane, pair, value in sums:
                total[lane, pair] = value
        return carry

    lax.fori_loop(0, (occupied + unroll - 1) // unroll, add_tiles, 0)

    for place in range(rows):
        owner = partner(row, place, rows) if rows == 2 else place
        for block in range(owned_blocks):
            columns = slice(block * edge, (block + 1) * edge)
            for source in range(in_blocks):
                pair = (owner * owned_blocks + block) * in_blocks + source
                value = (total[0, pair] + total[1, pair]) + (total[2, pair] + total[3, pair])
                high = value.astype(jnp.bfloat16)
                low = (value - high.astype(jnp.float32)).astype(jnp.bfloat16)
                column, line = source // owned_blocks, source % owned_blocks * edge
                lines = slice(line, line + edge)
                weight_refs[place][column, lines, columns] = high
                weight_refs[place][column, lines, owned + block * edge:owned + (block + 1) * edge] = low


def times_weight(parts, weights):
    incoming = None
    for start in range(0, len(parts), 2):
        term = jnp.dot(
            jnp.concatenate(parts[start:start + 2], axis=1),
            jnp.concatenate(weights[start:start + 2], axis=0),
            preferred_element_type=jnp.float32,
        )
        incoming = term if incoming is None else incoming + term
    owned = incoming.shape[1] // 2
    return incoming[:, :owned] + incoming[:, owned:]


def product_kernel(rows, cols, after, *refs):
    part_refs, refs = refs[after:after + cols], refs[after + cols:]
    weight_refs, result_refs = refs[:len(refs) // 2], refs[len(refs) // 2:]
    col = lax.axis_index("col")
    parts = [ref[...] for ref in part_refs]
    for weight_ref, result_ref in zip(weight_refs, result_refs):
        weights = [weight_ref[partner(col, offset, cols)] for offset in range(cols)]
        result_ref[...] = times_weight(parts, weights)


def restart_kernel(rows, cols, after_ref, seeds_ref, restart_ref):
    seed_total, sets = seeds_ref.shape
    owned = restart_ref.shape[1]
    first = (lax.axis_index("row") * cols + lax.axis_index("col")) * owned
    vertex = lax.broadcasted_iota(jnp.int32, (owned, sets), 0) + first
    restart = jnp.zeros((owned, sets), jnp.float32)
    for seed in range(seed_total):
        restart += (seeds_ref[seed:seed + 1, :] == vertex).astype(jnp.float32)
    restart_ref[...] = (1.0 - damping) * restart.T


def finish_kernel(last, *refs):
    *incoming_refs, restart_ref, degree_ref, result_ref = refs
    risk = restart_ref[...] + damping * sum(ref[...] for ref in incoming_refs)
    if last:
        result_ref[...] = risk
    else:
        result_ref[...] = (risk / degree_ref[...].astype(jnp.float32)).astype(jnp.bfloat16)


def local(tiles, tile_out, tile_in, tile_count, out_degree, seed_ids, prior):
    rows, cols = lax.axis_size("row"), lax.axis_size("col")
    sets, owned = prior.shape
    slots, edge = tiles.shape[2], tiles.shape[3]
    owned_blocks = owned // edge
    in_blocks, out_blocks = cols * owned_blocks, rows * owned_blocks
    degree = out_degree.reshape(1, owned)
    low = jnp.bfloat16

    scaled, out_ids, in_ids, seeds = call(
        scale_kernel,
        [
            jax.ShapeDtypeStruct((sets, owned), low),
            pltpu.SMEM(tile_out.shape, jnp.int32),
            pltpu.SMEM(tile_in.shape, jnp.int32),
            jax.ShapeDtypeStruct((seed_ids.shape[1], sets), jnp.int32),
        ],
        "scale",
        in_specs=[HBM] * 5,
        out_specs=[VMEM, SMEM, SMEM, VMEM],
        scratch_shapes=[
            pltpu.VMEM((sets, owned), jnp.float32),
            pltpu.VMEM((1, owned), jnp.int32),
            pltpu.SemaphoreType.DMA((5,)),
        ],
        flops=16 * slots * edge**3,
        size=6 * sets * owned,
    )(*in_hbm(prior, degree, tile_out, tile_in, seed_ids.T))

    def spread(value):
        return [from_column(value, cols, offset) if offset else value for offset in range(cols)]

    parts = spread(scaled)

    weights = call(
        functools.partial(sum_kernel, rows, cols, owned_blocks),
        [jax.ShapeDtypeStruct((cols, owned, 2 * owned), low)] * rows,
        "sum_tiles",
        in_specs=[ANY] + [SMEM] * 3 + [VMEM],
        out_specs=[VMEM] * rows,
        scratch_shapes=[pltpu.VMEM((LANES, out_blocks * in_blocks + 1, edge, edge), jnp.float32)],
        vmem=TILES_VMEM,
        flops=slots * edge * edge,
        size=2 * slots * edge * edge,
    )(scaled, tile_count, out_ids, in_ids, tiles)

    piece = jax.ShapeDtypeStruct((sets, owned), jnp.float32)

    def multiply(parts, weights, after=()):
        return call(
            functools.partial(product_kernel, rows, cols, len(after)),
            [piece] * len(weights),
            "product",
            in_specs=[ANY] * len(after) + [VMEM] * (cols + len(weights)),
            out_specs=[VMEM] * len(weights),
            flops=4 * sets * len(weights) * cols * owned * owned,
            size=4 * len(weights) * cols * owned * owned,
        )(*after, *parts, *weights)

    for round_index in range(ITERATIONS):
        last = round_index == ITERATIONS - 1
        if rows == 2:
            leaving, = multiply(parts, weights[1:])
            received = swap_rows(leaving)
            staying, = multiply(parts, weights[:1], (leaving,))
            incoming = (staying, received)
        else:
            leaving = jnp.stack(multiply(parts, weights))
            incoming = (lax.psum_scatter(leaving, "row", scatter_dimension=0, tiled=False),)
        if not round_index:
            restart = call(
                functools.partial(restart_kernel, rows, cols),
                piece,
                "restart",
                in_specs=[ANY, VMEM],
                out_specs=VMEM,
                flops=2 * sets * owned * seed_ids.shape[1],
                size=4 * sets * owned,
            )(leaving, seeds)
        value = call(
            functools.partial(finish_kernel, last),
            piece if last else jax.ShapeDtypeStruct((sets, owned), low),
            "last" if last else "next",
            in_specs=[VMEM] * (len(incoming) + 2),
            out_specs=VMEM,
            size=12 * sets * owned,
        )(*incoming, restart, degree)
        if not last:
            parts = spread(value)
    return value


def solution(mesh):
    placed = (
        P("row", "col", None, None, None),
        P("row", "col", None),
        P("row", "col", None),
        P("row", "col"),
        P(("row", "col")),
        P("seed", None),
        P("seed", ("row", "col")),
    )
    return jax.shard_map(
        local, mesh=mesh, in_specs=placed, out_specs=P("seed", ("row", "col")), check_vma=False
    )
```

```python
import functools
import math

import jax
import jax.numpy as jnp
from jax import lax
from jax.experimental import pallas as pl
from jax.experimental.pallas import tpu as pltpu
from jax.sharding import PartitionSpec as P

ITERATIONS = 2


damping = 0.85

VMEM = pl.BlockSpec(memory_space=pltpu.VMEM)
SMEM = pl.BlockSpec(memory_space=pltpu.SMEM)
HBM = pl.BlockSpec(memory_space=pltpu.HBM)
ANY = pl.BlockSpec(memory_space=pl.ANY)

TILES_VMEM = 32 * 1024 * 1024
SMALL_VMEM = 8 * 1024 * 1024
LANES = 4
UNROLL = 8
DEGREE_LINES = 8


def in_hbm(*arrays):
    return [pltpu.with_memory_space_constraint(array, pltpu.HBM) for array in arrays]


def call(kernel, out_shape, name, **options):
    return pl.pallas_call(
        kernel,
        out_shape=out_shape,
        compiler_params=pltpu.CompilerParams(vmem_limit_bytes=options.pop("vmem", SMALL_VMEM)),
        cost_estimate=pl.CostEstimate(
            flops=options.pop("flops", 0), bytes_accessed=options.pop("size", 0), transcendentals=0
        ),
        name=name,
        **options,
    )


def partner(index, offset, extent):
    if extent & (extent - 1) == 0:
        return index ^ offset
    return (index + offset) % extent


def from_column(value, cols, offset):
    return lax.ppermute(value, "col", [(partner(col, offset, cols), col) for col in range(cols)])


def hop(row):
    return row + 1


def from_hop(value, cols):
    pairs = [(row * cols + (col ^ hop(row)), row * cols + col) for row in range(2) for col in range(cols)]
    return lax.ppermute(value, ("row", "col"), pairs)


def swap_rows(value):
    return lax.ppermute(value, "row", [(0, 1), (1, 0)])


def scale_kernel(
    prior_hbm, degree_hbm, out_hbm, in_hbm, seeds_hbm,
    scaled_ref, out_ref, in_ref, seeds_ref, prior_ref, degree_ref, arrived,
):
    moves = (
        (prior_hbm, prior_ref), (degree_hbm, degree_ref),
        (out_hbm, out_ref), (in_hbm, in_ref), (seeds_hbm, seeds_ref),
    )
    copies = [
        pltpu.make_async_copy(source, place, arrived.at[index])
        for index, (source, place) in enumerate(moves)
    ]
    for copy in copies:
        copy.start()
    for copy in copies[:2]:
        copy.wait()
    scaled = (prior_ref[...] / degree_ref[...].astype(jnp.float32)).astype(jnp.bfloat16)
    scaled_ref[...] = scaled
    for copy in copies[2:]:
        copy.wait()


def sum_kernel(
    rows, cols, owned_blocks, after_ref, count_ref, out_ref, in_ref, tiles_ref, *rest
):
    *weight_refs, total = rest
    in_blocks = cols * owned_blocks
    slots, edge = tiles_ref.shape[2], tiles_ref.shape[3]
    owned = owned_blocks * edge
    spare = total.shape[1] - 1
    unroll = math.gcd(slots, UNROLL)
    row = lax.axis_index("row")
    occupied = count_ref[0, 0]

    total[...] = jnp.zeros(total.shape, jnp.float32)

    def add_tiles(step, carry):
        at = step * unroll
        places = []
        for lane in range(unroll):
            slot = at + lane
            pair = out_ref[0, 0, slot] * in_blocks + in_ref[0, 0, slot]
            places.append((lane % LANES, jnp.where(slot < occupied, pair, spare), slot))
        for start in range(0, unroll, 2):
            sums = [
                (lane, pair, total[lane, pair] + tiles_ref[0, 0, slot].astype(jnp.float32))
                for lane, pair, slot in places[start:start + 2]
            ]
            for lane, pair, value in sums:
                total[lane, pair] = value
        return carry

    lax.fori_loop(0, (occupied + unroll - 1) // unroll, add_tiles, 0)

    for place in range(rows):
        owner = partner(row, place, rows) if rows == 2 else place
        for block in range(owned_blocks):
            columns = slice(block * edge, (block + 1) * edge)
            for source in range(in_blocks):
                pair = (owner * owned_blocks + block) * in_blocks + source
                value = (total[0, pair] + total[1, pair]) + (total[2, pair] + total[3, pair])
                high = value.astype(jnp.bfloat16)
                low = (value - high.astype(jnp.float32)).astype(jnp.bfloat16)
                column, line = source // owned_blocks, source % owned_blocks * edge
                lines = slice(line, line + edge)
                weight_refs[place][column, lines, columns] = high
                weight_refs[place][column, lines, owned + block * edge:owned + (block + 1) * edge] = low


def times_weight(parts, weights):
    incoming = None
    for start in range(0, len(parts), 2):
        term = jnp.dot(
            jnp.concatenate(parts[start:start + 2], axis=1),
            jnp.concatenate(weights[start:start + 2], axis=0),
            preferred_element_type=jnp.float32,
        )
        incoming = term if incoming is None else incoming + term
    owned = incoming.shape[1] // 2
    return incoming[:, :owned] + incoming[:, owned:]


def product_kernel(rows, cols, after, *refs):
    part_refs, refs = refs[after:after + cols], refs[after + cols:]
    weight_refs, result_refs = refs[:len(refs) // 2], refs[len(refs) // 2:]
    col = lax.axis_index("col")
    parts = [ref[...] for ref in part_refs]
    for weight_ref, result_ref in zip(weight_refs, result_refs):
        weights = [weight_ref[partner(col, offset, cols)] for offset in range(cols)]
        result_ref[...] = times_weight(parts, weights)


def restart_kernel(rows, cols, after_ref, seeds_ref, restart_ref):
    seed_total, sets = seeds_ref.shape
    places, _, owned = restart_ref.shape
    for place in range(places):
        row = partner(lax.axis_index("row"), place, rows)
        first = (row * cols + lax.axis_index("col")) * owned
        vertex = lax.broadcasted_iota(jnp.int32, (owned, sets), 0) + first
        restart = jnp.zeros((owned, sets), jnp.float32)
        for seed in range(seed_total):
            restart += (seeds_ref[seed:seed + 1, :] == vertex).astype(jnp.float32)
        restart_ref[place] = (1.0 - damping) * restart.T


def first_kernel(cols, *refs):
    part_refs, (own_ref, other_ref, degree_ref, given_ref) = refs[:cols], refs[cols:]
    row, col = lax.axis_index("row"), lax.axis_index("col")
    parts = [ref[...] for ref in part_refs]
    sets, owned = parts[0].shape
    columns = [partner(col, offset, cols) for offset in range(cols)]
    wanted = col ^ hop(1 - row)
    for place, weight_ref in enumerate((own_ref, other_ref)):
        given_ref[place, :sets] = times_weight(parts, [weight_ref[column] for column in columns])
        given_ref[place, sets:sets + owned] = weight_ref[wanted, :, :owned].astype(
            jnp.float32
        ) + weight_ref[wanted, :, owned:].astype(jnp.float32)
        given_ref[place, sets + owned:] = jnp.broadcast_to(
            degree_ref[...].astype(jnp.float32), (given_ref.shape[1] - sets - owned, owned)
        )


def both_kernel(mine_ref, theirs_ref, restart_ref, own_ref, scaled_ref):
    _, sets, owned = restart_ref.shape
    for place in range(2):
        incoming = mine_ref[place, :sets] + theirs_ref[1 - place, :sets]
        degree = (theirs_ref if place else mine_ref)[0, sets + owned:sets + owned + 1]
        risk = restart_ref[place] + damping * incoming
        scaled = (risk / degree).astype(jnp.bfloat16)
        scaled_ref[place] = scaled
        if not place:
            own_ref[...] = scaled


def foreign_kernel(after_ref, theirs_ref, weight_ref):
    _, owned, double = weight_ref.shape
    sets = theirs_ref.shape[1] - owned - DEGREE_LINES
    for place in range(2):
        value = theirs_ref[1 - place, sets:sets + owned]
        high = value.astype(jnp.bfloat16)
        weight_ref[place, :, :owned] = high
        weight_ref[place, :, owned:] = (value - high.astype(jnp.float32)).astype(jnp.bfloat16)


def second_kernel(place, after, *refs):
    own_ref, hop_ref, far_ref, weight_ref, foreign_ref, result_ref = refs[after:]
    row, col = lax.axis_index("row"), lax.axis_index("col")
    parts = [own_ref[...], far_ref[...], hop_ref[0], hop_ref[1]]
    weights = [weight_ref[col], weight_ref[col ^ 3], weight_ref[col ^ hop(row)], foreign_ref[place]]
    result_ref[...] = times_weight(parts, weights)


def finish_kernel(last, *refs):
    *incoming_refs, restart_ref, degree_ref, result_ref = refs
    risk = restart_ref[0] + damping * sum(ref[...] for ref in incoming_refs)
    if last:
        result_ref[...] = risk
    else:
        result_ref[...] = (risk / degree_ref[...].astype(jnp.float32)).astype(jnp.bfloat16)


def local(tiles, tile_out, tile_in, tile_count, out_degree, seed_ids, prior):
    rows, cols = lax.axis_size("row"), lax.axis_size("col")
    sets, owned = prior.shape
    slots, edge = tiles.shape[2], tiles.shape[3]
    owned_blocks = owned // edge
    in_blocks, out_blocks = cols * owned_blocks, rows * owned_blocks
    degree = out_degree.reshape(1, owned)
    low = jnp.bfloat16

    scaled, out_ids, in_ids, seeds = call(
        scale_kernel,
        [
            jax.ShapeDtypeStruct((sets, owned), low),
            pltpu.SMEM(tile_out.shape, jnp.int32),
            pltpu.SMEM(tile_in.shape, jnp.int32),
            jax.ShapeDtypeStruct((seed_ids.shape[1], sets), jnp.int32),
        ],
        "scale",
        in_specs=[HBM] * 5,
        out_specs=[VMEM, SMEM, SMEM, VMEM],
        scratch_shapes=[
            pltpu.VMEM((sets, owned), jnp.float32),
            pltpu.VMEM((1, owned), jnp.int32),
            pltpu.SemaphoreType.DMA((5,)),
        ],
        flops=16 * slots * edge**3,
        size=6 * sets * owned,
    )(*in_hbm(prior, degree, tile_out, tile_in, seed_ids.T))

    def spread(value):
        return [from_column(value, cols, offset) if offset else value for offset in range(cols)]

    parts = spread(scaled)

    weights = call(
        functools.partial(sum_kernel, rows, cols, owned_blocks),
        [jax.ShapeDtypeStruct((cols, owned, 2 * owned), low)] * rows,
        "sum_tiles",
        in_specs=[ANY] + [SMEM] * 3 + [VMEM],
        out_specs=[VMEM] * rows,
        scratch_shapes=[pltpu.VMEM((LANES, out_blocks * in_blocks + 1, edge, edge), jnp.float32)],
        vmem=TILES_VMEM,
        flops=slots * edge * edge,
        size=2 * slots * edge * edge,
    )(scaled, tile_count, out_ids, in_ids, tiles)

    piece = jax.ShapeDtypeStruct((sets, owned), jnp.float32)

    def multiply(parts, weights, after=()):
        return call(
            functools.partial(product_kernel, rows, cols, len(after)),
            [piece] * len(weights),
            "product",
            in_specs=[ANY] * len(after) + [VMEM] * (cols + len(weights)),
            out_specs=[VMEM] * len(weights),
            flops=4 * sets * len(weights) * cols * owned * owned,
            size=4 * len(weights) * cols * owned * owned,
        )(*after, *parts, *weights)

    def count_restart(places, after):
        return call(
            functools.partial(restart_kernel, rows, cols),
            jax.ShapeDtypeStruct((places, sets, owned), jnp.float32),
            "restart",
            in_specs=[ANY, VMEM],
            out_specs=VMEM,
            flops=2 * places * sets * owned * seed_ids.shape[1],
            size=4 * places * sets * owned,
        )(after, seeds)

    def finish(incoming, restart, last):
        return call(
            functools.partial(finish_kernel, last),
            piece if last else jax.ShapeDtypeStruct((sets, owned), low),
            "last" if last else "next",
            in_specs=[VMEM] * (len(incoming) + 2),
            out_specs=VMEM,
            size=12 * sets * owned,
        )(*incoming, restart, degree)

    if (rows, cols, ITERATIONS) == (2, 4, 2):
        mine = call(
            functools.partial(first_kernel, cols),
            jax.ShapeDtypeStruct((2, sets + owned + DEGREE_LINES, owned), jnp.float32),
            "first",
            in_specs=[VMEM] * (cols + 3),
            out_specs=VMEM,
            flops=8 * sets * cols * owned * owned,
            size=8 * cols * owned * owned,
        )(*parts, *weights, degree)
        theirs = swap_rows(mine)
        restart = count_restart(2, mine)
        own, both = call(
            both_kernel,
            [jax.ShapeDtypeStruct((sets, owned), low), jax.ShapeDtypeStruct((2, sets, owned), low)],
            "both",
            in_specs=[VMEM] * 3,
            out_specs=[VMEM] * 2,
            size=24 * sets * owned,
        )(mine, theirs, restart)
        far = from_column(own, cols, 3)
        near = from_hop(both, cols)
        foreign = call(
            foreign_kernel,
            jax.ShapeDtypeStruct((2, owned, 2 * owned), low),
            "foreign",
            in_specs=[ANY, VMEM],
            out_specs=VMEM,
            size=16 * owned * owned,
        )(own, theirs)

        def second(place, *after):
            return call(
                functools.partial(second_kernel, place, len(after)),
                piece,
                "second",
                in_specs=[ANY] * len(after) + [VMEM] * 5,
                out_specs=VMEM,
                flops=4 * sets * cols * owned * owned,
                size=4 * cols * owned * owned,
            )(*after, own, near, far, weights[place], foreign)

        leaving = second(1)
        received = swap_rows(leaving)
        return finish((second(0, leaving), received), restart, True)

    for round_index in range(ITERATIONS):
        last = round_index == ITERATIONS - 1
        if rows == 2:
            leaving, = multiply(parts, weights[1:])
            received = swap_rows(leaving)
            staying, = multiply(parts, weights[:1], (leaving,))
            incoming = (staying, received)
        else:
            leaving = jnp.stack(multiply(parts, weights))
            incoming = (lax.psum_scatter(leaving, "row", scatter_dimension=0, tiled=False),)
        if not round_index:
            restart = count_restart(1, leaving)
        value = finish(incoming, restart, last)
        if not last:
            parts = spread(value)
    return value


def solution(mesh):
    placed = (
        P("row", "col", None, None, None),
        P("row", "col", None),
        P("row", "col", None),
        P("row", "col"),
        P(("row", "col")),
        P("seed", None),
        P("seed", ("row", "col")),
    )
    return jax.shard_map(
        local, mesh=mesh, in_specs=placed, out_specs=P("seed", ("row", "col")), check_vma=False
    )
```

```python
import functools
import math

import jax
import jax.numpy as jnp
from jax import lax
from jax.experimental import pallas as pl
from jax.experimental.pallas import tpu as pltpu
from jax.sharding import PartitionSpec as P

ITERATIONS = 2


damping = 0.85

VMEM = pl.BlockSpec(memory_space=pltpu.VMEM)
SMEM = pl.BlockSpec(memory_space=pltpu.SMEM)
HBM = pl.BlockSpec(memory_space=pltpu.HBM)
ANY = pl.BlockSpec(memory_space=pl.ANY)

TILES_VMEM = 32 * 1024 * 1024
SMALL_VMEM = 8 * 1024 * 1024
LANES = 4
UNROLL = 8
DEGREE_LINES = 8


def in_hbm(*arrays):
    return [pltpu.with_memory_space_constraint(array, pltpu.HBM) for array in arrays]


def call(kernel, out_shape, name, **options):
    return pl.pallas_call(
        kernel,
        out_shape=out_shape,
        compiler_params=pltpu.CompilerParams(vmem_limit_bytes=options.pop("vmem", SMALL_VMEM)),
        cost_estimate=pl.CostEstimate(
            flops=options.pop("flops", 0), bytes_accessed=options.pop("size", 0), transcendentals=0
        ),
        name=name,
        **options,
    )


def partner(index, offset, extent):
    if extent & (extent - 1) == 0:
        return index ^ offset
    return (index + offset) % extent


def from_column(value, cols, offset):
    return lax.ppermute(value, "col", [(partner(col, offset, cols), col) for col in range(cols)])


def hop(row):
    return row + 2


def from_hop(value, cols):
    pairs = [(row * cols + (col ^ hop(row)), row * cols + col) for row in range(2) for col in range(cols)]
    return lax.ppermute(value, ("row", "col"), pairs)


def swap_rows(value):
    return lax.ppermute(value, "row", [(0, 1), (1, 0)])


def scale_kernel(
    prior_hbm, degree_hbm, out_hbm, in_hbm, seeds_hbm,
    scaled_ref, out_ref, in_ref, seeds_ref, prior_ref, degree_ref, arrived,
):
    moves = (
        (prior_hbm, prior_ref), (degree_hbm, degree_ref),
        (out_hbm, out_ref), (in_hbm, in_ref), (seeds_hbm, seeds_ref),
    )
    copies = [
        pltpu.make_async_copy(source, place, arrived.at[index])
        for index, (source, place) in enumerate(moves)
    ]
    for copy in copies:
        copy.start()
    for copy in copies[:2]:
        copy.wait()
    scaled = (prior_ref[...] / degree_ref[...].astype(jnp.float32)).astype(jnp.bfloat16)
    scaled_ref[...] = scaled
    for copy in copies[2:]:
        copy.wait()


def sum_kernel(
    rows, cols, owned_blocks, after_ref, count_ref, out_ref, in_ref, tiles_ref, *rest
):
    *weight_refs, total = rest
    in_blocks = cols * owned_blocks
    slots, edge = tiles_ref.shape[2], tiles_ref.shape[3]
    owned = owned_blocks * edge
    spare = total.shape[1] - 1
    unroll = math.gcd(slots, UNROLL)
    row = lax.axis_index("row")
    occupied = count_ref[0, 0]

    total[...] = jnp.zeros(total.shape, jnp.float32)

    def add_tiles(step, carry):
        at = step * unroll
        places = []
        for lane in range(unroll):
            slot = at + lane
            pair = out_ref[0, 0, slot] * in_blocks + in_ref[0, 0, slot]
            places.append((lane % LANES, jnp.where(slot < occupied, pair, spare), slot))
        for start in range(0, unroll, 2):
            sums = [
                (lane, pair, total[lane, pair] + tiles_ref[0, 0, slot].astype(jnp.float32))
                for lane, pair, slot in places[start:start + 2]
            ]
            for lane, pair, value in sums:
                total[lane, pair] = value
        return carry

    lax.fori_loop(0, (occupied + unroll - 1) // unroll, add_tiles, 0)

    for place in range(rows):
        owner = partner(row, place, rows) if rows == 2 else place
        for block in range(owned_blocks):
            columns = slice(block * edge, (block + 1) * edge)
            for source in range(in_blocks):
                pair = (owner * owned_blocks + block) * in_blocks + source
                value = (total[0, pair] + total[1, pair]) + (total[2, pair] + total[3, pair])
                high = value.astype(jnp.bfloat16)
                low = (value - high.astype(jnp.float32)).astype(jnp.bfloat16)
                column, line = source // owned_blocks, source % owned_blocks * edge
                lines = slice(line, line + edge)
                weight_refs[place][column, lines, columns] = high
                weight_refs[place][column, lines, owned + block * edge:owned + (block + 1) * edge] = low


def times_weight(parts, weights):
    incoming = None
    for start in range(0, len(parts), 2):
        term = jnp.dot(
            jnp.concatenate(parts[start:start + 2], axis=1),
            jnp.concatenate(weights[start:start + 2], axis=0),
            preferred_element_type=jnp.float32,
        )
        incoming = term if incoming is None else incoming + term
    owned = incoming.shape[1] // 2
    return incoming[:, :owned] + incoming[:, owned:]


def product_kernel(rows, cols, after, *refs):
    part_refs, refs = refs[after:after + cols], refs[after + cols:]
    weight_refs, result_refs = refs[:len(refs) // 2], refs[len(refs) // 2:]
    col = lax.axis_index("col")
    parts = [ref[...] for ref in part_refs]
    for weight_ref, result_ref in zip(weight_refs, result_refs):
        weights = [weight_ref[partner(col, offset, cols)] for offset in range(cols)]
        result_ref[...] = times_weight(parts, weights)


def restart_kernel(rows, cols, after_ref, seeds_ref, restart_ref):
    seed_total, sets = seeds_ref.shape
    places, _, owned = restart_ref.shape
    for place in range(places):
        row = partner(lax.axis_index("row"), place, rows)
        first = (row * cols + lax.axis_index("col")) * owned
        vertex = lax.broadcasted_iota(jnp.int32, (owned, sets), 0) + first
        restart = jnp.zeros((owned, sets), jnp.float32)
        for seed in range(seed_total):
            restart += (seeds_ref[seed:seed + 1, :] == vertex).astype(jnp.float32)
        restart_ref[place] = (1.0 - damping) * restart.T


def first_kernel(cols, *refs):
    part_refs, (own_ref, other_ref, degree_ref, given_ref) = refs[:cols], refs[cols:]
    row, col = lax.axis_index("row"), lax.axis_index("col")
    parts = [ref[...] for ref in part_refs]
    sets, owned = parts[0].shape
    columns = [partner(col, offset, cols) for offset in range(cols)]
    wanted = col ^ hop(1 - row)
    for place, weight_ref in enumerate((own_ref, other_ref)):
        given_ref[place, :sets] = times_weight(parts, [weight_ref[column] for column in columns])
        given_ref[place, sets:sets + owned] = weight_ref[wanted, :, :owned].astype(
            jnp.float32
        ) + weight_ref[wanted, :, owned:].astype(jnp.float32)
        given_ref[place, sets + owned:] = jnp.broadcast_to(
            degree_ref[...].astype(jnp.float32), (given_ref.shape[1] - sets - owned, owned)
        )


def both_kernel(mine_ref, theirs_ref, restart_ref, own_ref, scaled_ref):
    _, sets, owned = restart_ref.shape
    for place in range(2):
        incoming = mine_ref[place, :sets] + theirs_ref[1 - place, :sets]
        degree = (theirs_ref if place else mine_ref)[0, sets + owned:sets + owned + 1]
        risk = restart_ref[place] + damping * incoming
        scaled = (risk / degree).astype(jnp.bfloat16)
        scaled_ref[place] = scaled
        if not place:
            own_ref[...] = scaled


def foreign_kernel(after_ref, theirs_ref, weight_ref):
    _, owned, double = weight_ref.shape
    sets = theirs_ref.shape[1] - owned - DEGREE_LINES
    for place in range(2):
        value = theirs_ref[1 - place, sets:sets + owned]
        high = value.astype(jnp.bfloat16)
        weight_ref[place, :, :owned] = high
        weight_ref[place, :, owned:] = (value - high.astype(jnp.float32)).astype(jnp.bfloat16)


def second_kernel(place, after, *refs):
    own_ref, side_ref, hop_ref, weight_ref, foreign_ref, result_ref = refs[after:]
    row, col = lax.axis_index("row"), lax.axis_index("col")
    parts = [own_ref[...], side_ref[...], hop_ref[0], hop_ref[1]]
    weights = [weight_ref[col], weight_ref[col ^ 1], weight_ref[col ^ hop(row)], foreign_ref[place]]
    result_ref[...] = times_weight(parts, weights)


def finish_kernel(last, *refs):
    *incoming_refs, restart_ref, degree_ref, result_ref = refs
    risk = restart_ref[0] + damping * sum(ref[...] for ref in incoming_refs)
    if last:
        result_ref[...] = risk
    else:
        result_ref[...] = (risk / degree_ref[...].astype(jnp.float32)).astype(jnp.bfloat16)


def local(tiles, tile_out, tile_in, tile_count, out_degree, seed_ids, prior):
    rows, cols = lax.axis_size("row"), lax.axis_size("col")
    sets, owned = prior.shape
    slots, edge = tiles.shape[2], tiles.shape[3]
    owned_blocks = owned // edge
    in_blocks, out_blocks = cols * owned_blocks, rows * owned_blocks
    degree = out_degree.reshape(1, owned)
    low = jnp.bfloat16

    scaled, out_ids, in_ids, seeds = call(
        scale_kernel,
        [
            jax.ShapeDtypeStruct((sets, owned), low),
            pltpu.SMEM(tile_out.shape, jnp.int32),
            pltpu.SMEM(tile_in.shape, jnp.int32),
            jax.ShapeDtypeStruct((seed_ids.shape[1], sets), jnp.int32),
        ],
        "scale",
        in_specs=[HBM] * 5,
        out_specs=[VMEM, SMEM, SMEM, VMEM],
        scratch_shapes=[
            pltpu.VMEM((sets, owned), jnp.float32),
            pltpu.VMEM((1, owned), jnp.int32),
            pltpu.SemaphoreType.DMA((5,)),
        ],
        flops=16 * slots * edge**3,
        size=6 * sets * owned,
    )(*in_hbm(prior, degree, tile_out, tile_in, seed_ids.T))

    def spread(value):
        return [from_column(value, cols, offset) if offset else value for offset in range(cols)]

    parts = spread(scaled)

    weights = call(
        functools.partial(sum_kernel, rows, cols, owned_blocks),
        [jax.ShapeDtypeStruct((cols, owned, 2 * owned), low)] * rows,
        "sum_tiles",
        in_specs=[ANY] + [SMEM] * 3 + [VMEM],
        out_specs=[VMEM] * rows,
        scratch_shapes=[pltpu.VMEM((LANES, out_blocks * in_blocks + 1, edge, edge), jnp.float32)],
        vmem=TILES_VMEM,
        flops=slots * edge * edge,
        size=2 * slots * edge * edge,
    )(scaled, tile_count, out_ids, in_ids, tiles)

    piece = jax.ShapeDtypeStruct((sets, owned), jnp.float32)

    def multiply(parts, weights, after=()):
        return call(
            functools.partial(product_kernel, rows, cols, len(after)),
            [piece] * len(weights),
            "product",
            in_specs=[ANY] * len(after) + [VMEM] * (cols + len(weights)),
            out_specs=[VMEM] * len(weights),
            flops=4 * sets * len(weights) * cols * owned * owned,
            size=4 * len(weights) * cols * owned * owned,
        )(*after, *parts, *weights)

    def count_restart(places, after):
        return call(
            functools.partial(restart_kernel, rows, cols),
            jax.ShapeDtypeStruct((places, sets, owned), jnp.float32),
            "restart",
            in_specs=[ANY, VMEM],
            out_specs=VMEM,
            flops=2 * places * sets * owned * seed_ids.shape[1],
            size=4 * places * sets * owned,
        )(after, seeds)

    def finish(incoming, restart, last):
        return call(
            functools.partial(finish_kernel, last),
            piece if last else jax.ShapeDtypeStruct((sets, owned), low),
            "last" if last else "next",
            in_specs=[VMEM] * (len(incoming) + 2),
            out_specs=VMEM,
            size=12 * sets * owned,
        )(*incoming, restart, degree)

    if (rows, cols, ITERATIONS) == (2, 4, 2):
        mine = call(
            functools.partial(first_kernel, cols),
            jax.ShapeDtypeStruct((2, sets + owned + DEGREE_LINES, owned), jnp.float32),
            "first",
            in_specs=[VMEM] * (cols + 3),
            out_specs=VMEM,
            flops=8 * sets * cols * owned * owned,
            size=8 * cols * owned * owned,
        )(*parts, *weights, degree)
        theirs = swap_rows(mine)
        restart = count_restart(2, mine)
        own, both = call(
            both_kernel,
            [jax.ShapeDtypeStruct((sets, owned), low), jax.ShapeDtypeStruct((2, sets, owned), low)],
            "both",
            in_specs=[VMEM] * 3,
            out_specs=[VMEM] * 2,
            size=24 * sets * owned,
        )(mine, theirs, restart)
        side = from_column(own, cols, 1)
        near = from_hop(both, cols)
        foreign = call(
            foreign_kernel,
            jax.ShapeDtypeStruct((2, owned, 2 * owned), low),
            "foreign",
            in_specs=[ANY, VMEM],
            out_specs=VMEM,
            size=16 * owned * owned,
        )(own, theirs)

        def second(place, *after):
            return call(
                functools.partial(second_kernel, place, len(after)),
                piece,
                "second",
                in_specs=[ANY] * len(after) + [VMEM] * 5,
                out_specs=VMEM,
                flops=4 * sets * cols * owned * owned,
                size=4 * cols * owned * owned,
            )(*after, own, side, near, weights[place], foreign)

        leaving = second(1)
        received = swap_rows(leaving)
        return finish((second(0, leaving), received), restart, True)

    for round_index in range(ITERATIONS):
        last = round_index == ITERATIONS - 1
        if rows == 2:
            leaving, = multiply(parts, weights[1:])
            received = swap_rows(leaving)
            staying, = multiply(parts, weights[:1], (leaving,))
            incoming = (staying, received)
        else:
            leaving = jnp.stack(multiply(parts, weights))
            incoming = (lax.psum_scatter(leaving, "row", scatter_dimension=0, tiled=False),)
        if not round_index:
            restart = count_restart(1, leaving)
        value = finish(incoming, restart, last)
        if not last:
            parts = spread(value)
    return value


def solution(mesh):
    placed = (
        P("row", "col", None, None, None),
        P("row", "col", None),
        P("row", "col", None),
        P("row", "col"),
        P(("row", "col")),
        P("seed", None),
        P("seed", ("row", "col")),
    )
    return jax.shard_map(
        local, mesh=mesh, in_specs=placed, out_specs=P("seed", ("row", "col")), check_vma=False
    )
```

```python
import functools
import math

import jax
import jax.numpy as jnp
from jax import lax
from jax.experimental import pallas as pl
from jax.experimental.pallas import tpu as pltpu
from jax.sharding import PartitionSpec as P

ITERATIONS = 2


damping = 0.85

VMEM = pl.BlockSpec(memory_space=pltpu.VMEM)
SMEM = pl.BlockSpec(memory_space=pltpu.SMEM)
HBM = pl.BlockSpec(memory_space=pltpu.HBM)
ANY = pl.BlockSpec(memory_space=pl.ANY)

TILES_VMEM = 32 * 1024 * 1024
SMALL_VMEM = 8 * 1024 * 1024
STRIPS = 4
UNROLL = 8
DEGREE_LINES = 8


def in_hbm(*arrays):
    return [pltpu.with_memory_space_constraint(array, pltpu.HBM) for array in arrays]


def call(kernel, out_shape, name, **options):
    return pl.pallas_call(
        kernel,
        out_shape=out_shape,
        compiler_params=pltpu.CompilerParams(vmem_limit_bytes=options.pop("vmem", SMALL_VMEM)),
        cost_estimate=pl.CostEstimate(
            flops=options.pop("flops", 0), bytes_accessed=options.pop("size", 0), transcendentals=0
        ),
        name=name,
        **options,
    )


def partner(index, offset, extent):
    if extent & (extent - 1) == 0:
        return index ^ offset
    return (index + offset) % extent


def from_column(value, cols, offset):
    return lax.ppermute(value, "col", [(partner(col, offset, cols), col) for col in range(cols)])


def hop(row):
    return row + 2


def from_hop(value, cols):
    pairs = [(row * cols + (col ^ hop(row)), row * cols + col) for row in range(2) for col in range(cols)]
    return lax.ppermute(value, ("row", "col"), pairs)


def swap_rows(value):
    return lax.ppermute(value, "row", [(0, 1), (1, 0)])


def scale_kernel(
    prior_hbm, degree_hbm, out_hbm, in_hbm, seeds_hbm,
    scaled_ref, out_ref, in_ref, seeds_ref, prior_ref, degree_ref, arrived,
):
    moves = (
        (prior_hbm, prior_ref), (degree_hbm, degree_ref),
        (out_hbm, out_ref), (in_hbm, in_ref), (seeds_hbm, seeds_ref),
    )
    copies = [
        pltpu.make_async_copy(source, place, arrived.at[index])
        for index, (source, place) in enumerate(moves)
    ]
    for copy in copies:
        copy.start()
    for copy in copies[:2]:
        copy.wait()
    scaled = (prior_ref[...] / degree_ref[...].astype(jnp.float32)).astype(jnp.bfloat16)
    scaled_ref[...] = scaled
    for copy in copies[2:]:
        copy.wait()


def sum_kernel(
    rows, cols, owned_blocks, after_ref, count_ref, out_ref, in_ref, tiles_ref, *rest
):
    weight_refs, totals = rest[:rows], rest[rows:]
    in_blocks = cols * owned_blocks
    slots, edge = tiles_ref.shape[2], tiles_ref.shape[3]
    owned = owned_blocks * edge
    spare, strip = totals[0].shape[0] - 1, totals[0].shape[1]
    unroll = math.gcd(slots, UNROLL)
    row = lax.axis_index("row")
    occupied = count_ref[0, 0]

    for total in totals:
        total[...] = jnp.zeros(total.shape, jnp.float32)

    def add_tiles(step, carry):
        at = step * unroll
        places = []
        for lane in range(unroll):
            slot = at + lane
            pair = out_ref[0, 0, slot] * in_blocks + in_ref[0, 0, slot]
            places.append((slot, jnp.where(slot < occupied, pair, spare)))
        for slot, pair in places:
            for index, total in enumerate(totals):
                lines = slice(index * strip, (index + 1) * strip)
                total[pair] += tiles_ref[0, 0, slot, lines].astype(jnp.float32)
        return carry

    lax.fori_loop(0, (occupied + unroll - 1) // unroll, add_tiles, 0)

    for place in range(rows):
        owner = partner(row, place, rows) if rows == 2 else place
        for block in range(owned_blocks):
            columns = slice(block * edge, (block + 1) * edge)
            for source in range(in_blocks):
                pair = (owner * owned_blocks + block) * in_blocks + source
                for index, total in enumerate(totals):
                    value = total[pair]
                    high = value.astype(jnp.bfloat16)
                    low = (value - high.astype(jnp.float32)).astype(jnp.bfloat16)
                    column, line = source // owned_blocks, source % owned_blocks * edge + index * strip
                    lines = slice(line, line + strip)
                    weight_refs[place][column, lines, columns] = high
                    weight_refs[place][column, lines, owned + block * edge:owned + (block + 1) * edge] = low


def times_weight(parts, weights):
    incoming = None
    for start in range(0, len(parts), 2):
        term = jnp.dot(
            jnp.concatenate(parts[start:start + 2], axis=1),
            jnp.concatenate(weights[start:start + 2], axis=0),
            preferred_element_type=jnp.float32,
        )
        incoming = term if incoming is None else incoming + term
    owned = incoming.shape[1] // 2
    return incoming[:, :owned] + incoming[:, owned:]


def product_kernel(rows, cols, after, *refs):
    part_refs, refs = refs[after:after + cols], refs[after + cols:]
    weight_refs, result_refs = refs[:len(refs) // 2], refs[len(refs) // 2:]
    col = lax.axis_index("col")
    parts = [ref[...] for ref in part_refs]
    for weight_ref, result_ref in zip(weight_refs, result_refs):
        weights = [weight_ref[partner(col, offset, cols)] for offset in range(cols)]
        result_ref[...] = times_weight(parts, weights)


def restart_kernel(rows, cols, after_ref, seeds_ref, restart_ref):
    seed_total, sets = seeds_ref.shape
    places, _, owned = restart_ref.shape
    for place in range(places):
        row = partner(lax.axis_index("row"), place, rows)
        first = (row * cols + lax.axis_index("col")) * owned
        vertex = lax.broadcasted_iota(jnp.int32, (owned, sets), 0) + first
        restart = jnp.zeros((owned, sets), jnp.float32)
        for seed in range(seed_total):
            restart += (seeds_ref[seed:seed + 1, :] == vertex).astype(jnp.float32)
        restart_ref[place] = (1.0 - damping) * restart.T


def first_kernel(cols, *refs):
    part_refs, (own_ref, other_ref, degree_ref, given_ref) = refs[:cols], refs[cols:]
    row, col = lax.axis_index("row"), lax.axis_index("col")
    parts = [ref[...] for ref in part_refs]
    sets, owned = parts[0].shape
    columns = [partner(col, offset, cols) for offset in range(cols)]
    wanted = col ^ hop(1 - row)
    for place, weight_ref in enumerate((own_ref, other_ref)):
        given_ref[place, :sets] = times_weight(parts, [weight_ref[column] for column in columns])
        given_ref[place, sets:sets + owned] = weight_ref[wanted, :, :owned].astype(
            jnp.float32
        ) + weight_ref[wanted, :, owned:].astype(jnp.float32)
        given_ref[place, sets + owned:] = jnp.broadcast_to(
            degree_ref[...].astype(jnp.float32), (given_ref.shape[1] - sets - owned, owned)
        )


def both_kernel(mine_ref, theirs_ref, restart_ref, own_ref, scaled_ref):
    _, sets, owned = restart_ref.shape
    for place in range(2):
        incoming = mine_ref[place, :sets] + theirs_ref[1 - place, :sets]
        degree = (theirs_ref if place else mine_ref)[0, sets + owned:sets + owned + 1]
        risk = restart_ref[place] + damping * incoming
        scaled = (risk / degree).astype(jnp.bfloat16)
        scaled_ref[place] = scaled
        if not place:
            own_ref[...] = scaled


def foreign_kernel(after_ref, theirs_ref, weight_ref):
    _, owned, double = weight_ref.shape
    sets = theirs_ref.shape[1] - owned - DEGREE_LINES
    for place in range(2):
        value = theirs_ref[1 - place, sets:sets + owned]
        high = value.astype(jnp.bfloat16)
        weight_ref[place, :, :owned] = high
        weight_ref[place, :, owned:] = (value - high.astype(jnp.float32)).astype(jnp.bfloat16)


def second_kernel(place, after, *refs):
    own_ref, side_ref, hop_ref, weight_ref, foreign_ref, result_ref = refs[after:]
    row, col = lax.axis_index("row"), lax.axis_index("col")
    parts = [own_ref[...], side_ref[...], hop_ref[0], hop_ref[1]]
    weights = [weight_ref[col], weight_ref[col ^ 1], weight_ref[col ^ hop(row)], foreign_ref[place]]
    result_ref[...] = times_weight(parts, weights)


def finish_kernel(last, *refs):
    *incoming_refs, restart_ref, degree_ref, result_ref = refs
    risk = restart_ref[0] + damping * sum(ref[...] for ref in incoming_refs)
    if last:
        result_ref[...] = risk
    else:
        result_ref[...] = (risk / degree_ref[...].astype(jnp.float32)).astype(jnp.bfloat16)


def local(tiles, tile_out, tile_in, tile_count, out_degree, seed_ids, prior):
    rows, cols = lax.axis_size("row"), lax.axis_size("col")
    sets, owned = prior.shape
    slots, edge = tiles.shape[2], tiles.shape[3]
    owned_blocks = owned // edge
    in_blocks, out_blocks = cols * owned_blocks, rows * owned_blocks
    degree = out_degree.reshape(1, owned)
    low = jnp.bfloat16

    scaled, out_ids, in_ids, seeds = call(
        scale_kernel,
        [
            jax.ShapeDtypeStruct((sets, owned), low),
            pltpu.SMEM(tile_out.shape, jnp.int32),
            pltpu.SMEM(tile_in.shape, jnp.int32),
            jax.ShapeDtypeStruct((seed_ids.shape[1], sets), jnp.int32),
        ],
        "scale",
        in_specs=[HBM] * 5,
        out_specs=[VMEM, SMEM, SMEM, VMEM],
        scratch_shapes=[
            pltpu.VMEM((sets, owned), jnp.float32),
            pltpu.VMEM((1, owned), jnp.int32),
            pltpu.SemaphoreType.DMA((5,)),
        ],
        flops=16 * slots * edge**3,
        size=6 * sets * owned,
    )(*in_hbm(prior, degree, tile_out, tile_in, seed_ids.T))

    def spread(value):
        return [from_column(value, cols, offset) if offset else value for offset in range(cols)]

    parts = spread(scaled)

    weights = call(
        functools.partial(sum_kernel, rows, cols, owned_blocks),
        [jax.ShapeDtypeStruct((cols, owned, 2 * owned), low)] * rows,
        "sum_tiles",
        in_specs=[ANY] + [SMEM] * 3 + [VMEM],
        out_specs=[VMEM] * rows,
        scratch_shapes=[pltpu.VMEM((out_blocks * in_blocks + 1, edge // STRIPS, edge), jnp.float32)] * STRIPS,
        vmem=TILES_VMEM,
        flops=slots * edge * edge,
        size=2 * slots * edge * edge,
    )(scaled, tile_count, out_ids, in_ids, tiles)

    piece = jax.ShapeDtypeStruct((sets, owned), jnp.float32)

    def multiply(parts, weights, after=()):
        return call(
            functools.partial(product_kernel, rows, cols, len(after)),
            [piece] * len(weights),
            "product",
            in_specs=[ANY] * len(after) + [VMEM] * (cols + len(weights)),
            out_specs=[VMEM] * len(weights),
            flops=4 * sets * len(weights) * cols * owned * owned,
            size=4 * len(weights) * cols * owned * owned,
        )(*after, *parts, *weights)

    def count_restart(places, after):
        return call(
            functools.partial(restart_kernel, rows, cols),
            jax.ShapeDtypeStruct((places, sets, owned), jnp.float32),
            "restart",
            in_specs=[ANY, VMEM],
            out_specs=VMEM,
            flops=2 * places * sets * owned * seed_ids.shape[1],
            size=4 * places * sets * owned,
        )(after, seeds)

    def finish(incoming, restart, last):
        return call(
            functools.partial(finish_kernel, last),
            piece if last else jax.ShapeDtypeStruct((sets, owned), low),
            "last" if last else "next",
            in_specs=[VMEM] * (len(incoming) + 2),
            out_specs=VMEM,
            size=12 * sets * owned,
        )(*incoming, restart, degree)

    if (rows, cols, ITERATIONS) == (2, 4, 2):
        mine = call(
            functools.partial(first_kernel, cols),
            jax.ShapeDtypeStruct((2, sets + owned + DEGREE_LINES, owned), jnp.float32),
            "first",
            in_specs=[VMEM] * (cols + 3),
            out_specs=VMEM,
            flops=8 * sets * cols * owned * owned,
            size=8 * cols * owned * owned,
        )(*parts, *weights, degree)
        theirs = swap_rows(mine)
        restart = count_restart(2, mine)
        own, both = call(
            both_kernel,
            [jax.ShapeDtypeStruct((sets, owned), low), jax.ShapeDtypeStruct((2, sets, owned), low)],
            "both",
            in_specs=[VMEM] * 3,
            out_specs=[VMEM] * 2,
            size=24 * sets * owned,
        )(mine, theirs, restart)
        side = from_column(own, cols, 1)
        near = from_hop(both, cols)
        foreign = call(
            foreign_kernel,
            jax.ShapeDtypeStruct((2, owned, 2 * owned), low),
            "foreign",
            in_specs=[ANY, VMEM],
            out_specs=VMEM,
            size=16 * owned * owned,
        )(own, theirs)

        def second(place, *after):
            return call(
                functools.partial(second_kernel, place, len(after)),
                piece,
                "second",
                in_specs=[ANY] * len(after) + [VMEM] * 5,
                out_specs=VMEM,
                flops=4 * sets * cols * owned * owned,
                size=4 * cols * owned * owned,
            )(*after, own, side, near, weights[place], foreign)

        leaving = second(1)
        received = swap_rows(leaving)
        return finish((second(0, leaving), received), restart, True)

    for round_index in range(ITERATIONS):
        last = round_index == ITERATIONS - 1
        if rows == 2:
            leaving, = multiply(parts, weights[1:])
            received = swap_rows(leaving)
            staying, = multiply(parts, weights[:1], (leaving,))
            incoming = (staying, received)
        else:
            leaving = jnp.stack(multiply(parts, weights))
            incoming = (lax.psum_scatter(leaving, "row", scatter_dimension=0, tiled=False),)
        if not round_index:
            restart = count_restart(1, leaving)
        value = finish(incoming, restart, last)
        if not last:
            parts = spread(value)
    return value


def solution(mesh):
    placed = (
        P("row", "col", None, None, None),
        P("row", "col", None),
        P("row", "col", None),
        P("row", "col"),
        P(("row", "col")),
        P("seed", None),
        P("seed", ("row", "col")),
    )
    return jax.shard_map(
        local, mesh=mesh, in_specs=placed, out_specs=P("seed", ("row", "col")), check_vma=False
    )
```

```python
import functools
import math

import jax
import jax.numpy as jnp
from jax import lax
from jax.experimental import pallas as pl
from jax.experimental.pallas import tpu as pltpu
from jax.sharding import PartitionSpec as P

ITERATIONS = 2


damping = 0.85

VMEM = pl.BlockSpec(memory_space=pltpu.VMEM)
SMEM = pl.BlockSpec(memory_space=pltpu.SMEM)
HBM = pl.BlockSpec(memory_space=pltpu.HBM)
ANY = pl.BlockSpec(memory_space=pl.ANY)

TILES_VMEM = 32 * 1024 * 1024
SMALL_VMEM = 8 * 1024 * 1024
STRIPS = 4
UNROLL = 32
DEGREE_LINES = 8


def in_hbm(*arrays):
    return [pltpu.with_memory_space_constraint(array, pltpu.HBM) for array in arrays]


def call(kernel, out_shape, name, **options):
    return pl.pallas_call(
        kernel,
        out_shape=out_shape,
        compiler_params=pltpu.CompilerParams(vmem_limit_bytes=options.pop("vmem", SMALL_VMEM)),
        cost_estimate=pl.CostEstimate(
            flops=options.pop("flops", 0), bytes_accessed=options.pop("size", 0), transcendentals=0
        ),
        name=name,
        **options,
    )


def partner(index, offset, extent):
    if extent & (extent - 1) == 0:
        return index ^ offset
    return (index + offset) % extent


def from_column(value, cols, offset):
    return lax.ppermute(value, "col", [(partner(col, offset, cols), col) for col in range(cols)])


def hop(row):
    return row + 2


def from_hop(value, cols):
    pairs = [(row * cols + (col ^ hop(row)), row * cols + col) for row in range(2) for col in range(cols)]
    return lax.ppermute(value, ("row", "col"), pairs)


def from_side(value, cols):
    pairs = [((1 - row) * cols + (col ^ 1), row * cols + col) for row in range(2) for col in range(cols)]
    return lax.ppermute(value, ("row", "col"), pairs)


def swap_rows(value):
    return lax.ppermute(value, "row", [(0, 1), (1, 0)])


def scale_kernel(prior_hbm, degree_hbm, scaled_ref, prior_ref, degree_ref, arrived):
    copies = [
        pltpu.make_async_copy(source, place, arrived.at[index])
        for index, (source, place) in enumerate(((prior_hbm, prior_ref), (degree_hbm, degree_ref)))
    ]
    for copy in copies:
        copy.start()
    for copy in copies:
        copy.wait()
    scaled_ref[...] = (prior_ref[...] / degree_ref[...].astype(jnp.float32)).astype(jnp.bfloat16)


def sum_kernel(
    rows, cols, owned_blocks, after_ref, count_ref, out_ref, in_ref, tiles_ref, *rest
):
    weight_refs, totals = rest[:rows], rest[rows:]
    in_blocks = cols * owned_blocks
    slots, edge = tiles_ref.shape[2], tiles_ref.shape[3]
    owned = owned_blocks * edge
    spare, strip = totals[0].shape[0] - 1, totals[0].shape[1]
    unroll = math.gcd(slots, UNROLL)
    row = lax.axis_index("row")
    occupied = count_ref[0, 0]

    for total in totals:
        total[...] = jnp.zeros(total.shape, jnp.float32)

    def add_tiles(step, carry):
        at = step * unroll
        places = []
        for lane in range(unroll):
            slot = at + lane
            pair = out_ref[0, 0, slot] * in_blocks + in_ref[0, 0, slot]
            places.append((slot, jnp.where(slot < occupied, pair, spare)))
        for slot, pair in places:
            for index, total in enumerate(totals):
                lines = slice(index * strip, (index + 1) * strip)
                total[pair] += tiles_ref[0, 0, slot, lines].astype(jnp.float32)
        return carry

    lax.fori_loop(0, (occupied + unroll - 1) // unroll, add_tiles, 0)

    for place in range(rows):
        owner = partner(row, place, rows) if rows == 2 else place
        for block in range(owned_blocks):
            columns = slice(block * edge, (block + 1) * edge)
            for source in range(in_blocks):
                pair = (owner * owned_blocks + block) * in_blocks + source
                for index, total in enumerate(totals):
                    value = total[pair]
                    high = value.astype(jnp.bfloat16)
                    low = (value - high.astype(jnp.float32)).astype(jnp.bfloat16)
                    column, line = source // owned_blocks, source % owned_blocks * edge + index * strip
                    lines = slice(line, line + strip)
                    weight_refs[place][column, lines, columns] = high
                    weight_refs[place][column, lines, owned + block * edge:owned + (block + 1) * edge] = low


def times_weight(parts, weights):
    incoming = None
    for start in range(0, len(parts), 2):
        term = jnp.dot(
            jnp.concatenate(parts[start:start + 2], axis=1),
            jnp.concatenate(weights[start:start + 2], axis=0),
            preferred_element_type=jnp.float32,
        )
        incoming = term if incoming is None else incoming + term
    owned = incoming.shape[1] // 2
    return incoming[:, :owned] + incoming[:, owned:]


def product_kernel(rows, cols, after, *refs):
    part_refs, refs = refs[after:after + cols], refs[after + cols:]
    weight_refs, result_refs = refs[:len(refs) // 2], refs[len(refs) // 2:]
    col = lax.axis_index("col")
    parts = [ref[...] for ref in part_refs]
    for weight_ref, result_ref in zip(weight_refs, result_refs):
        weights = [weight_ref[partner(col, offset, cols)] for offset in range(cols)]
        result_ref[...] = times_weight(parts, weights)


def restart_kernel(rows, cols, after_ref, seeds_ref, restart_ref):
    seed_total, sets = seeds_ref.shape
    places, _, owned = restart_ref.shape
    for place in range(places):
        row = partner(lax.axis_index("row"), place, rows)
        first = (row * cols + lax.axis_index("col")) * owned
        vertex = lax.broadcasted_iota(jnp.int32, (owned, sets), 0) + first
        restart = jnp.zeros((owned, sets), jnp.float32)
        for seed in range(seed_total):
            restart += (seeds_ref[seed:seed + 1, :] == vertex).astype(jnp.float32)
        restart_ref[place] = (1.0 - damping) * restart.T


def first_kernel(cols, *refs):
    part_refs, (own_ref, other_ref, degree_ref, given_ref) = refs[:cols], refs[cols:]
    row, col = lax.axis_index("row"), lax.axis_index("col")
    parts = [ref[...] for ref in part_refs]
    sets, owned = parts[0].shape
    columns = [partner(col, offset, cols) for offset in range(cols)]
    wanted = col ^ hop(1 - row)
    for place, weight_ref in enumerate((own_ref, other_ref)):
        given_ref[place, :sets] = times_weight(parts, [weight_ref[column] for column in columns])
        given_ref[place, sets:sets + owned] = weight_ref[wanted, :, :owned].astype(
            jnp.float32
        ) + weight_ref[wanted, :, owned:].astype(jnp.float32)
        given_ref[place, sets + owned:] = jnp.broadcast_to(
            degree_ref[...].astype(jnp.float32), (given_ref.shape[1] - sets - owned, owned)
        )


def both_kernel(mine_ref, theirs_ref, restart_ref, other_ref, scaled_ref):
    _, sets, owned = restart_ref.shape
    for place in range(2):
        incoming = mine_ref[place, :sets] + theirs_ref[1 - place, :sets]
        degree = (theirs_ref if place else mine_ref)[0, sets + owned:sets + owned + 1]
        risk = restart_ref[place] + damping * incoming
        scaled = (risk / degree).astype(jnp.bfloat16)
        scaled_ref[place] = scaled
        if place:
            other_ref[...] = scaled


def foreign_kernel(after_ref, theirs_ref, weight_ref):
    _, owned, double = weight_ref.shape
    sets = theirs_ref.shape[1] - owned - DEGREE_LINES
    for place in range(2):
        value = theirs_ref[1 - place, sets:sets + owned]
        high = value.astype(jnp.bfloat16)
        weight_ref[place, :, :owned] = high
        weight_ref[place, :, owned:] = (value - high.astype(jnp.float32)).astype(jnp.bfloat16)


def second_kernel(place, after, *refs):
    both_ref, side_ref, hop_ref, weight_ref, foreign_ref, result_ref = refs[after:]
    row, col = lax.axis_index("row"), lax.axis_index("col")
    parts = [both_ref[0], side_ref[...], hop_ref[0], hop_ref[1]]
    weights = [weight_ref[col], weight_ref[col ^ 1], weight_ref[col ^ hop(row)], foreign_ref[place]]
    result_ref[...] = times_weight(parts, weights)


def finish_kernel(last, *refs):
    *incoming_refs, restart_ref, degree_ref, result_ref = refs
    risk = restart_ref[0] + damping * sum(ref[...] for ref in incoming_refs)
    if last:
        result_ref[...] = risk
    else:
        result_ref[...] = (risk / degree_ref[...].astype(jnp.float32)).astype(jnp.bfloat16)


def local(tiles, tile_out, tile_in, tile_count, out_degree, seed_ids, prior):
    rows, cols = lax.axis_size("row"), lax.axis_size("col")
    sets, owned = prior.shape
    slots, edge = tiles.shape[2], tiles.shape[3]
    owned_blocks = owned // edge
    in_blocks, out_blocks = cols * owned_blocks, rows * owned_blocks
    degree = out_degree.reshape(1, owned)
    low = jnp.bfloat16

    scaled = call(
        scale_kernel,
        jax.ShapeDtypeStruct((sets, owned), low),
        "scale",
        in_specs=[HBM] * 2,
        out_specs=VMEM,
        scratch_shapes=[
            pltpu.VMEM((sets, owned), jnp.float32),
            pltpu.VMEM((1, owned), jnp.int32),
            pltpu.SemaphoreType.DMA((2,)),
        ],
        flops=16 * slots * edge**3,
        size=6 * sets * owned,
    )(*in_hbm(prior, degree))

    def spread(value):
        return [from_column(value, cols, offset) if offset else value for offset in range(cols)]

    parts = spread(scaled)

    weights = call(
        functools.partial(sum_kernel, rows, cols, owned_blocks),
        [jax.ShapeDtypeStruct((cols, owned, 2 * owned), low)] * rows,
        "sum_tiles",
        in_specs=[ANY] + [SMEM] * 3 + [VMEM],
        out_specs=[VMEM] * rows,
        scratch_shapes=[pltpu.VMEM((out_blocks * in_blocks + 1, edge // STRIPS, edge), jnp.float32)] * STRIPS,
        vmem=TILES_VMEM,
        flops=slots * edge * edge,
        size=2 * slots * edge * edge,
    )(scaled, tile_count, tile_out, tile_in, tiles)

    piece = jax.ShapeDtypeStruct((sets, owned), jnp.float32)

    def multiply(parts, weights, after=()):
        return call(
            functools.partial(product_kernel, rows, cols, len(after)),
            [piece] * len(weights),
            "product",
            in_specs=[ANY] * len(after) + [VMEM] * (cols + len(weights)),
            out_specs=[VMEM] * len(weights),
            flops=4 * sets * len(weights) * cols * owned * owned,
            size=4 * len(weights) * cols * owned * owned,
        )(*after, *parts, *weights)

    def count_restart(places, after):
        return call(
            functools.partial(restart_kernel, rows, cols),
            jax.ShapeDtypeStruct((places, sets, owned), jnp.float32),
            "restart",
            in_specs=[ANY, VMEM],
            out_specs=VMEM,
            flops=2 * places * sets * owned * seed_ids.shape[1],
            size=4 * places * sets * owned,
        )(after, seed_ids.T)

    def finish(incoming, restart, last):
        return call(
            functools.partial(finish_kernel, last),
            piece if last else jax.ShapeDtypeStruct((sets, owned), low),
            "last" if last else "next",
            in_specs=[VMEM] * (len(incoming) + 2),
            out_specs=VMEM,
            size=12 * sets * owned,
        )(*incoming, restart, degree)

    if (rows, cols, ITERATIONS) == (2, 4, 2):
        mine = call(
            functools.partial(first_kernel, cols),
            jax.ShapeDtypeStruct((2, sets + owned + DEGREE_LINES, owned), jnp.float32),
            "first",
            in_specs=[VMEM] * (cols + 3),
            out_specs=VMEM,
            flops=8 * sets * cols * owned * owned,
            size=8 * cols * owned * owned,
        )(*parts, *weights, degree)
        theirs = swap_rows(mine)
        restart = count_restart(2, mine)
        other, both = call(
            both_kernel,
            [jax.ShapeDtypeStruct((sets, owned), low), jax.ShapeDtypeStruct((2, sets, owned), low)],
            "both",
            in_specs=[VMEM] * 3,
            out_specs=[VMEM] * 2,
            size=24 * sets * owned,
        )(mine, theirs, restart)
        side = from_side(other, cols)
        near = from_hop(both, cols)
        foreign = call(
            foreign_kernel,
            jax.ShapeDtypeStruct((2, owned, 2 * owned), low),
            "foreign",
            in_specs=[ANY, VMEM],
            out_specs=VMEM,
            size=16 * owned * owned,
        )(other, theirs)

        def second(place, *after):
            return call(
                functools.partial(second_kernel, place, len(after)),
                piece,
                "second",
                in_specs=[ANY] * len(after) + [VMEM] * 5,
                out_specs=VMEM,
                flops=4 * sets * cols * owned * owned,
                size=4 * cols * owned * owned,
            )(*after, both, side, near, weights[place], foreign)

        leaving = second(1)
        received = swap_rows(leaving)
        return finish((second(0, leaving), received), restart, True)

    for round_index in range(ITERATIONS):
        last = round_index == ITERATIONS - 1
        if rows == 2:
            leaving, = multiply(parts, weights[1:])
            received = swap_rows(leaving)
            staying, = multiply(parts, weights[:1], (leaving,))
            incoming = (staying, received)
        else:
            leaving = jnp.stack(multiply(parts, weights))
            incoming = (lax.psum_scatter(leaving, "row", scatter_dimension=0, tiled=False),)
        if not round_index:
            restart = count_restart(1, leaving)
        value = finish(incoming, restart, last)
        if not last:
            parts = spread(value)
    return value


def solution(mesh):
    placed = (
        P("row", "col", None, None, None),
        P("row", "col", None),
        P("row", "col", None),
        P("row", "col"),
        P(("row", "col")),
        P("seed", None),
        P("seed", ("row", "col")),
    )
    return jax.shard_map(
        local, mesh=mesh, in_specs=placed, out_specs=P("seed", ("row", "col")), check_vma=False
    )
```

```python
import functools
import math

import jax
import jax.numpy as jnp
from jax import lax
from jax.experimental import pallas as pl
from jax.experimental.pallas import tpu as pltpu
from jax.sharding import PartitionSpec as P

ITERATIONS = 2


damping = 0.85

VMEM = pl.BlockSpec(memory_space=pltpu.VMEM)
SMEM = pl.BlockSpec(memory_space=pltpu.SMEM)
HBM = pl.BlockSpec(memory_space=pltpu.HBM)
ANY = pl.BlockSpec(memory_space=pl.ANY)

TILES_VMEM = 32 * 1024 * 1024
SMALL_VMEM = 8 * 1024 * 1024
STRIPS = 4
UNROLL = 32
DEGREE_LINES = 8


def in_hbm(*arrays):
    return [pltpu.with_memory_space_constraint(array, pltpu.HBM) for array in arrays]


def call(kernel, out_shape, name, **options):
    return pl.pallas_call(
        kernel,
        out_shape=out_shape,
        compiler_params=pltpu.CompilerParams(vmem_limit_bytes=options.pop("vmem", SMALL_VMEM)),
        cost_estimate=pl.CostEstimate(
            flops=options.pop("flops", 0), bytes_accessed=options.pop("size", 0), transcendentals=0
        ),
        name=name,
        **options,
    )


def partner(index, offset, extent):
    if extent & (extent - 1) == 0:
        return index ^ offset
    return (index + offset) % extent


def from_column(value, cols, offset):
    return lax.ppermute(value, "col", [(partner(col, offset, cols), col) for col in range(cols)])


def hop(row):
    return row + 2


def from_hop(value, cols):
    pairs = [((1 - row) * cols + (col ^ hop(row)), row * cols + col) for row in range(2) for col in range(cols)]
    return lax.ppermute(value, ("row", "col"), pairs)


def from_side(value, cols):
    pairs = [((1 - row) * cols + (col ^ 1), row * cols + col) for row in range(2) for col in range(cols)]
    return lax.ppermute(value, ("row", "col"), pairs)


def swap_rows(value):
    return lax.ppermute(value, "row", [(0, 1), (1, 0)])


def scale_kernel(
    prior_hbm, degree_hbm, out_hbm, in_hbm, seeds_hbm,
    scaled_ref, out_ref, in_ref, seeds_ref, prior_ref, degree_ref, arrived,
):
    moves = (
        (prior_hbm, prior_ref), (degree_hbm, degree_ref),
        (out_hbm, out_ref), (in_hbm, in_ref), (seeds_hbm, seeds_ref),
    )
    copies = [
        pltpu.make_async_copy(source, place, arrived.at[index])
        for index, (source, place) in enumerate(moves)
    ]
    for copy in copies:
        copy.start()
    for copy in copies[:2]:
        copy.wait()
    scaled = (prior_ref[...] / degree_ref[...].astype(jnp.float32)).astype(jnp.bfloat16)
    scaled_ref[...] = scaled
    for copy in copies[2:]:
        copy.wait()


def sum_kernel(
    rows, cols, owned_blocks, after_ref, count_ref, out_ref, in_ref, tiles_ref, *rest
):
    weight_refs, totals = rest[:rows], rest[rows:]
    in_blocks = cols * owned_blocks
    slots, edge = tiles_ref.shape[2], tiles_ref.shape[3]
    owned = owned_blocks * edge
    spare, strip = totals[0].shape[0] - 1, totals[0].shape[1]
    unroll = math.gcd(slots, UNROLL)
    row = lax.axis_index("row")
    occupied = count_ref[0, 0]

    for total in totals:
        total[...] = jnp.zeros(total.shape, jnp.float32)

    def add_tiles(step, carry):
        at = step * unroll
        places = []
        for lane in range(unroll):
            slot = at + lane
            pair = out_ref[0, 0, slot] * in_blocks + in_ref[0, 0, slot]
            places.append((slot, jnp.where(slot < occupied, pair, spare)))
        for slot, pair in places:
            for index, total in enumerate(totals):
                lines = slice(index * strip, (index + 1) * strip)
                total[pair] += tiles_ref[0, 0, slot, lines].astype(jnp.float32)
        return carry

    lax.fori_loop(0, (occupied + unroll - 1) // unroll, add_tiles, 0)

    for place in range(rows):
        owner = partner(row, place, rows) if rows == 2 else place
        for block in range(owned_blocks):
            columns = slice(block * edge, (block + 1) * edge)
            for source in range(in_blocks):
                pair = (owner * owned_blocks + block) * in_blocks + source
                for index, total in enumerate(totals):
                    value = total[pair]
                    high = value.astype(jnp.bfloat16)
                    low = (value - high.astype(jnp.float32)).astype(jnp.bfloat16)
                    column, line = source // owned_blocks, source % owned_blocks * edge + index * strip
                    lines = slice(line, line + strip)
                    weight_refs[place][column, lines, columns] = high
                    weight_refs[place][column, lines, owned + block * edge:owned + (block + 1) * edge] = low


def times_weight(parts, weights):
    incoming = None
    for start in range(0, len(parts), 2):
        term = jnp.dot(
            jnp.concatenate(parts[start:start + 2], axis=1),
            jnp.concatenate(weights[start:start + 2], axis=0),
            preferred_element_type=jnp.float32,
        )
        incoming = term if incoming is None else incoming + term
    owned = incoming.shape[1] // 2
    return incoming[:, :owned] + incoming[:, owned:]


def product_kernel(rows, cols, after, *refs):
    part_refs, refs = refs[after:after + cols], refs[after + cols:]
    weight_refs, result_refs = refs[:len(refs) // 2], refs[len(refs) // 2:]
    col = lax.axis_index("col")
    parts = [ref[...] for ref in part_refs]
    for weight_ref, result_ref in zip(weight_refs, result_refs):
        weights = [weight_ref[partner(col, offset, cols)] for offset in range(cols)]
        result_ref[...] = times_weight(parts, weights)


def restart_kernel(rows, cols, after_ref, seeds_ref, restart_ref):
    seed_total, sets = seeds_ref.shape
    places, _, owned = restart_ref.shape
    for place in range(places):
        row = partner(lax.axis_index("row"), place, rows)
        first = (row * cols + lax.axis_index("col")) * owned
        vertex = lax.broadcasted_iota(jnp.int32, (owned, sets), 0) + first
        restart = jnp.zeros((owned, sets), jnp.float32)
        for seed in range(seed_total):
            restart += (seeds_ref[seed:seed + 1, :] == vertex).astype(jnp.float32)
        restart_ref[place] = (1.0 - damping) * restart.T


def first_kernel(cols, *refs):
    part_refs, (own_ref, other_ref, degree_ref, given_ref) = refs[:cols], refs[cols:]
    row, col = lax.axis_index("row"), lax.axis_index("col")
    parts = [ref[...] for ref in part_refs]
    sets, owned = parts[0].shape
    columns = [partner(col, offset, cols) for offset in range(cols)]
    wanted = col ^ hop(1 - row)
    for place, weight_ref in enumerate((own_ref, other_ref)):
        given_ref[place, :sets] = times_weight(parts, [weight_ref[column] for column in columns])
        given_ref[place, sets:sets + owned] = weight_ref[wanted, :, :owned].astype(
            jnp.float32
        ) + weight_ref[wanted, :, owned:].astype(jnp.float32)
        given_ref[place, sets + owned:] = jnp.broadcast_to(
            degree_ref[...].astype(jnp.float32), (given_ref.shape[1] - sets - owned, owned)
        )


def both_kernel(mine_ref, theirs_ref, restart_ref, other_ref, scaled_ref):
    _, sets, owned = restart_ref.shape
    for place in range(2):
        incoming = mine_ref[place, :sets] + theirs_ref[1 - place, :sets]
        degree = (theirs_ref if place else mine_ref)[0, sets + owned:sets + owned + 1]
        risk = restart_ref[place] + damping * incoming
        scaled = (risk / degree).astype(jnp.bfloat16)
        scaled_ref[place] = scaled
        if place:
            other_ref[...] = scaled


def foreign_kernel(after_ref, theirs_ref, weight_ref):
    _, owned, double = weight_ref.shape
    sets = theirs_ref.shape[1] - owned - DEGREE_LINES
    for place in range(2):
        value = theirs_ref[1 - place, sets:sets + owned]
        high = value.astype(jnp.bfloat16)
        weight_ref[place, :, :owned] = high
        weight_ref[place, :, owned:] = (value - high.astype(jnp.float32)).astype(jnp.bfloat16)


def second_kernel(place, after, *refs):
    both_ref, side_ref, hop_ref, weight_ref, foreign_ref, result_ref = refs[after:]
    row, col = lax.axis_index("row"), lax.axis_index("col")
    parts = [both_ref[0], side_ref[...], hop_ref[1], hop_ref[0]]
    weights = [weight_ref[col], weight_ref[col ^ 1], weight_ref[col ^ hop(row)], foreign_ref[place]]
    result_ref[...] = times_weight(parts, weights)


def finish_kernel(last, *refs):
    *incoming_refs, restart_ref, degree_ref, result_ref = refs
    risk = restart_ref[0] + damping * sum(ref[...] for ref in incoming_refs)
    if last:
        result_ref[...] = risk
    else:
        result_ref[...] = (risk / degree_ref[...].astype(jnp.float32)).astype(jnp.bfloat16)


def local(tiles, tile_out, tile_in, tile_count, out_degree, seed_ids, prior):
    rows, cols = lax.axis_size("row"), lax.axis_size("col")
    sets, owned = prior.shape
    slots, edge = tiles.shape[2], tiles.shape[3]
    owned_blocks = owned // edge
    in_blocks, out_blocks = cols * owned_blocks, rows * owned_blocks
    degree = out_degree.reshape(1, owned)
    low = jnp.bfloat16

    scaled, out_ids, in_ids, seeds = call(
        scale_kernel,
        [
            jax.ShapeDtypeStruct((sets, owned), low),
            pltpu.SMEM(tile_out.shape, jnp.int32),
            pltpu.SMEM(tile_in.shape, jnp.int32),
            jax.ShapeDtypeStruct((seed_ids.shape[1], sets), jnp.int32),
        ],
        "scale",
        in_specs=[HBM] * 5,
        out_specs=[VMEM, SMEM, SMEM, VMEM],
        scratch_shapes=[
            pltpu.VMEM((sets, owned), jnp.float32),
            pltpu.VMEM((1, owned), jnp.int32),
            pltpu.SemaphoreType.DMA((5,)),
        ],
        flops=16 * slots * edge**3,
        size=6 * sets * owned,
    )(*in_hbm(prior, degree, tile_out, tile_in, seed_ids.T))

    def spread(value):
        return [from_column(value, cols, offset) if offset else value for offset in range(cols)]

    parts = spread(scaled)

    weights = call(
        functools.partial(sum_kernel, rows, cols, owned_blocks),
        [jax.ShapeDtypeStruct((cols, owned, 2 * owned), low)] * rows,
        "sum_tiles",
        in_specs=[ANY] + [SMEM] * 3 + [VMEM],
        out_specs=[VMEM] * rows,
        scratch_shapes=[pltpu.VMEM((out_blocks * in_blocks + 1, edge // STRIPS, edge), jnp.float32)] * STRIPS,
        vmem=TILES_VMEM,
        flops=slots * edge * edge,
        size=2 * slots * edge * edge,
    )(scaled, tile_count, out_ids, in_ids, tiles)

    piece = jax.ShapeDtypeStruct((sets, owned), jnp.float32)

    def multiply(parts, weights, after=()):
        return call(
            functools.partial(product_kernel, rows, cols, len(after)),
            [piece] * len(weights),
            "product",
            in_specs=[ANY] * len(after) + [VMEM] * (cols + len(weights)),
            out_specs=[VMEM] * len(weights),
            flops=4 * sets * len(weights) * cols * owned * owned,
            size=4 * len(weights) * cols * owned * owned,
        )(*after, *parts, *weights)

    def count_restart(places, after):
        return call(
            functools.partial(restart_kernel, rows, cols),
            jax.ShapeDtypeStruct((places, sets, owned), jnp.float32),
            "restart",
            in_specs=[ANY, VMEM],
            out_specs=VMEM,
            flops=2 * places * sets * owned * seed_ids.shape[1],
            size=4 * places * sets * owned,
        )(after, seeds)

    def finish(incoming, restart, last):
        return call(
            functools.partial(finish_kernel, last),
            piece if last else jax.ShapeDtypeStruct((sets, owned), low),
            "last" if last else "next",
            in_specs=[VMEM] * (len(incoming) + 2),
            out_specs=VMEM,
            size=12 * sets * owned,
        )(*incoming, restart, degree)

    if (rows, cols, ITERATIONS) == (2, 4, 2):
        mine = call(
            functools.partial(first_kernel, cols),
            jax.ShapeDtypeStruct((2, sets + owned + DEGREE_LINES, owned), jnp.float32),
            "first",
            in_specs=[VMEM] * (cols + 3),
            out_specs=VMEM,
            flops=8 * sets * cols * owned * owned,
            size=8 * cols * owned * owned,
        )(*parts, *weights, degree)
        theirs = swap_rows(mine)
        restart = count_restart(2, mine)
        other, both = call(
            both_kernel,
            [jax.ShapeDtypeStruct((sets, owned), low), jax.ShapeDtypeStruct((2, sets, owned), low)],
            "both",
            in_specs=[VMEM] * 3,
            out_specs=[VMEM] * 2,
            size=24 * sets * owned,
        )(mine, theirs, restart)
        side = from_side(other, cols)
        near = from_hop(both, cols)
        foreign = call(
            foreign_kernel,
            jax.ShapeDtypeStruct((2, owned, 2 * owned), low),
            "foreign",
            in_specs=[ANY, VMEM],
            out_specs=VMEM,
            size=16 * owned * owned,
        )(other, theirs)

        def second(place, *after):
            return call(
                functools.partial(second_kernel, place, len(after)),
                piece,
                "second",
                in_specs=[ANY] * len(after) + [VMEM] * 5,
                out_specs=VMEM,
                flops=4 * sets * cols * owned * owned,
                size=4 * cols * owned * owned,
            )(*after, both, side, near, weights[place], foreign)

        leaving = second(1)
        received = swap_rows(leaving)
        return finish((second(0, leaving), received), restart, True)

    for round_index in range(ITERATIONS):
        last = round_index == ITERATIONS - 1
        if rows == 2:
            leaving, = multiply(parts, weights[1:])
            received = swap_rows(leaving)
            staying, = multiply(parts, weights[:1], (leaving,))
            incoming = (staying, received)
        else:
            leaving = jnp.stack(multiply(parts, weights))
            incoming = (lax.psum_scatter(leaving, "row", scatter_dimension=0, tiled=False),)
        if not round_index:
            restart = count_restart(1, leaving)
        value = finish(incoming, restart, last)
        if not last:
            parts = spread(value)
    return value


def solution(mesh):
    placed = (
        P("row", "col", None, None, None),
        P("row", "col", None),
        P("row", "col", None),
        P("row", "col"),
        P(("row", "col")),
        P("seed", None),
        P("seed", ("row", "col")),
    )
    return jax.shard_map(
        local, mesh=mesh, in_specs=placed, out_specs=P("seed", ("row", "col")), check_vma=False
    )
```

```python
import functools
import math

import jax
import jax.numpy as jnp
from jax import lax
from jax.experimental import pallas as pl
from jax.experimental.pallas import tpu as pltpu
from jax.sharding import PartitionSpec as P

ITERATIONS = 2


damping = 0.85

VMEM = pl.BlockSpec(memory_space=pltpu.VMEM)
SMEM = pl.BlockSpec(memory_space=pltpu.SMEM)
HBM = pl.BlockSpec(memory_space=pltpu.HBM)
ANY = pl.BlockSpec(memory_space=pl.ANY)

TILES_VMEM = 32 * 1024 * 1024
SMALL_VMEM = 8 * 1024 * 1024
STRIPS = 4
UNROLL = 32
DEGREE_LINES = 8


def in_hbm(*arrays):
    return [pltpu.with_memory_space_constraint(array, pltpu.HBM) for array in arrays]


def call(kernel, out_shape, name, **options):
    return pl.pallas_call(
        kernel,
        out_shape=out_shape,
        compiler_params=pltpu.CompilerParams(vmem_limit_bytes=options.pop("vmem", SMALL_VMEM)),
        cost_estimate=pl.CostEstimate(
            flops=options.pop("flops", 0), bytes_accessed=options.pop("size", 0), transcendentals=0
        ),
        name=name,
        **options,
    )


def partner(index, offset, extent):
    if extent & (extent - 1) == 0:
        return index ^ offset
    return (index + offset) % extent


def from_column(value, cols, offset):
    return lax.ppermute(value, "col", [(partner(col, offset, cols), col) for col in range(cols)])


def hop(row):
    return row + 2


def from_hop(value, cols):
    pairs = [((1 - row) * cols + (col ^ hop(row)), row * cols + col) for row in range(2) for col in range(cols)]
    return lax.ppermute(value, ("row", "col"), pairs)


def from_side(value, cols):
    pairs = [((1 - row) * cols + (col ^ 1), row * cols + col) for row in range(2) for col in range(cols)]
    return lax.ppermute(value, ("row", "col"), pairs)


def swap_rows(value):
    return lax.ppermute(value, "row", [(0, 1), (1, 0)])


def scale_kernel(
    prior_hbm, degree_hbm, out_hbm, in_hbm, seeds_hbm,
    scaled_ref, out_ref, in_ref, seeds_ref, prior_ref, degree_ref, arrived,
):
    moves = (
        (prior_hbm, prior_ref), (degree_hbm, degree_ref),
        (out_hbm, out_ref), (in_hbm, in_ref), (seeds_hbm, seeds_ref),
    )
    copies = [
        pltpu.make_async_copy(source, place, arrived.at[index])
        for index, (source, place) in enumerate(moves)
    ]
    for copy in copies:
        copy.start()
    for copy in copies[:2]:
        copy.wait()
    scaled = (prior_ref[...] / degree_ref[...].astype(jnp.float32)).astype(jnp.bfloat16)
    scaled_ref[...] = scaled
    for copy in copies[2:]:
        copy.wait()


def sum_kernel(
    rows, cols, owned_blocks, after_ref, count_ref, out_ref, in_ref, tiles_ref, *rest
):
    weight_refs, totals = rest[:rows], rest[rows:]
    in_blocks = cols * owned_blocks
    slots, edge = tiles_ref.shape[2], tiles_ref.shape[3]
    owned = owned_blocks * edge
    spare, strip = totals[0].shape[0] - 1, totals[0].shape[1]
    unroll = math.gcd(slots, UNROLL)
    row = lax.axis_index("row")
    occupied = count_ref[0, 0]

    for total in totals:
        total[...] = jnp.zeros(total.shape, jnp.float32)

    def add_tiles(step, carry):
        at = step * unroll
        places = []
        for lane in range(unroll):
            slot = at + lane
            pair = out_ref[0, 0, slot] * in_blocks + in_ref[0, 0, slot]
            places.append((slot, jnp.where(slot < occupied, pair, spare)))
        for slot, pair in places:
            for index, total in enumerate(totals):
                lines = slice(index * strip, (index + 1) * strip)
                total[pair] += tiles_ref[0, 0, slot, lines].astype(jnp.float32)
        return carry

    lax.fori_loop(0, (occupied + unroll - 1) // unroll, add_tiles, 0)

    for place in range(rows):
        owner = partner(row, place, rows) if rows == 2 else place
        for block in range(owned_blocks):
            columns = slice(block * edge, (block + 1) * edge)
            for source in range(in_blocks):
                pair = (owner * owned_blocks + block) * in_blocks + source
                for index, total in enumerate(totals):
                    value = total[pair]
                    high = value.astype(jnp.bfloat16)
                    low = (value - high.astype(jnp.float32)).astype(jnp.bfloat16)
                    column, line = source // owned_blocks, source % owned_blocks * edge + index * strip
                    lines = slice(line, line + strip)
                    weight_refs[place][column, lines, columns] = high
                    weight_refs[place][column, lines, owned + block * edge:owned + (block + 1) * edge] = low


def times_weight(parts, weights):
    incoming = None
    for start in range(0, len(parts), 2):
        term = jnp.dot(
            jnp.concatenate(parts[start:start + 2], axis=1),
            jnp.concatenate(weights[start:start + 2], axis=0),
            preferred_element_type=jnp.float32,
        )
        incoming = term if incoming is None else incoming + term
    owned = incoming.shape[1] // 2
    return incoming[:, :owned] + incoming[:, owned:]


def product_kernel(rows, cols, after, *refs):
    part_refs, refs = refs[after:after + cols], refs[after + cols:]
    weight_refs, result_refs = refs[:len(refs) // 2], refs[len(refs) // 2:]
    col = lax.axis_index("col")
    parts = [ref[...] for ref in part_refs]
    for weight_ref, result_ref in zip(weight_refs, result_refs):
        weights = [weight_ref[partner(col, offset, cols)] for offset in range(cols)]
        result_ref[...] = times_weight(parts, weights)


def restart_kernel(rows, cols, after_ref, seeds_ref, restart_ref):
    seed_total, sets = seeds_ref.shape
    places, _, owned = restart_ref.shape
    for place in range(places):
        row = partner(lax.axis_index("row"), place, rows)
        first = (row * cols + lax.axis_index("col")) * owned
        vertex = lax.broadcasted_iota(jnp.int32, (owned, sets), 0) + first
        restart = jnp.zeros((owned, sets), jnp.float32)
        for seed in range(seed_total):
            restart += (seeds_ref[seed:seed + 1, :] == vertex).astype(jnp.float32)
        restart_ref[place] = (1.0 - damping) * restart.T


def first_kernel(cols, *refs):
    part_refs, (own_ref, other_ref, degree_ref, given_ref) = refs[:cols - 1], refs[cols - 1:]
    row, col = lax.axis_index("row"), lax.axis_index("col")
    parts = [ref[...] for ref in part_refs]
    sets, owned = parts[0].shape
    columns = [col] + [partner(col, offset, cols) for offset in range(2, cols)]
    wanted = col ^ hop(1 - row)
    for place, weight_ref in enumerate((own_ref, other_ref)):
        given_ref[place, :sets] = times_weight(parts, [weight_ref[column] for column in columns])
        given_ref[place, sets:sets + owned] = weight_ref[wanted, :, :owned].astype(
            jnp.float32
        ) + weight_ref[wanted, :, owned:].astype(jnp.float32)
        given_ref[place, sets + owned:] = jnp.broadcast_to(
            degree_ref[...].astype(jnp.float32), (given_ref.shape[1] - sets - owned, owned)
        )


def nearest_kernel(early_ref, part_ref, own_ref, other_ref, given_ref):
    col = lax.axis_index("col")
    sets = part_ref.shape[0]
    for place, weight_ref in enumerate((own_ref, other_ref)):
        given_ref[place, :sets] = early_ref[place, :sets] + times_weight([part_ref[...]], [weight_ref[col ^ 1]])
        given_ref[place, sets:] = early_ref[place, sets:]


def both_kernel(mine_ref, theirs_ref, restart_ref, other_ref, scaled_ref):
    _, sets, owned = restart_ref.shape
    for place in range(2):
        incoming = mine_ref[place, :sets] + theirs_ref[1 - place, :sets]
        degree = (theirs_ref if place else mine_ref)[0, sets + owned:sets + owned + 1]
        risk = restart_ref[place] + damping * incoming
        scaled = (risk / degree).astype(jnp.bfloat16)
        scaled_ref[place] = scaled
        if place:
            other_ref[...] = scaled


def foreign_kernel(after_ref, theirs_ref, weight_ref):
    _, owned, double = weight_ref.shape
    sets = theirs_ref.shape[1] - owned - DEGREE_LINES
    for place in range(2):
        value = theirs_ref[1 - place, sets:sets + owned]
        high = value.astype(jnp.bfloat16)
        weight_ref[place, :, :owned] = high
        weight_ref[place, :, owned:] = (value - high.astype(jnp.float32)).astype(jnp.bfloat16)


def second_kernel(place, after, *refs):
    both_ref, hop_ref, weight_ref, foreign_ref, result_ref = refs[after:]
    row, col = lax.axis_index("row"), lax.axis_index("col")
    parts = [hop_ref[1], hop_ref[0], both_ref[0]]
    weights = [weight_ref[col ^ hop(row)], foreign_ref[place], weight_ref[col]]
    result_ref[...] = times_weight(parts, weights)


def side_kernel(early_ref, side_ref, weight_ref, result_ref):
    result_ref[...] = early_ref[...] + times_weight([side_ref[...]], [weight_ref[lax.axis_index("col") ^ 1]])


def finish_kernel(last, *refs):
    *incoming_refs, restart_ref, degree_ref, result_ref = refs
    risk = restart_ref[0] + damping * sum(ref[...] for ref in incoming_refs)
    if last:
        result_ref[...] = risk
    else:
        result_ref[...] = (risk / degree_ref[...].astype(jnp.float32)).astype(jnp.bfloat16)


def local(tiles, tile_out, tile_in, tile_count, out_degree, seed_ids, prior):
    rows, cols = lax.axis_size("row"), lax.axis_size("col")
    sets, owned = prior.shape
    slots, edge = tiles.shape[2], tiles.shape[3]
    owned_blocks = owned // edge
    in_blocks, out_blocks = cols * owned_blocks, rows * owned_blocks
    degree = out_degree.reshape(1, owned)
    low = jnp.bfloat16

    scaled, out_ids, in_ids, seeds = call(
        scale_kernel,
        [
            jax.ShapeDtypeStruct((sets, owned), low),
            pltpu.SMEM(tile_out.shape, jnp.int32),
            pltpu.SMEM(tile_in.shape, jnp.int32),
            jax.ShapeDtypeStruct((seed_ids.shape[1], sets), jnp.int32),
        ],
        "scale",
        in_specs=[HBM] * 5,
        out_specs=[VMEM, SMEM, SMEM, VMEM],
        scratch_shapes=[
            pltpu.VMEM((sets, owned), jnp.float32),
            pltpu.VMEM((1, owned), jnp.int32),
            pltpu.SemaphoreType.DMA((5,)),
        ],
        flops=16 * slots * edge**3,
        size=6 * sets * owned,
    )(*in_hbm(prior, degree, tile_out, tile_in, seed_ids.T))

    def spread(value):
        return [from_column(value, cols, offset) if offset else value for offset in range(cols)]

    parts = spread(scaled)

    weights = call(
        functools.partial(sum_kernel, rows, cols, owned_blocks),
        [jax.ShapeDtypeStruct((cols, owned, 2 * owned), low)] * rows,
        "sum_tiles",
        in_specs=[ANY] + [SMEM] * 3 + [VMEM],
        out_specs=[VMEM] * rows,
        scratch_shapes=[pltpu.VMEM((out_blocks * in_blocks + 1, edge // STRIPS, edge), jnp.float32)] * STRIPS,
        vmem=TILES_VMEM,
        flops=slots * edge * edge,
        size=2 * slots * edge * edge,
    )(scaled, tile_count, out_ids, in_ids, tiles)

    piece = jax.ShapeDtypeStruct((sets, owned), jnp.float32)

    def multiply(parts, weights, after=()):
        return call(
            functools.partial(product_kernel, rows, cols, len(after)),
            [piece] * len(weights),
            "product",
            in_specs=[ANY] * len(after) + [VMEM] * (cols + len(weights)),
            out_specs=[VMEM] * len(weights),
            flops=4 * sets * len(weights) * cols * owned * owned,
            size=4 * len(weights) * cols * owned * owned,
        )(*after, *parts, *weights)

    def count_restart(places, after):
        return call(
            functools.partial(restart_kernel, rows, cols),
            jax.ShapeDtypeStruct((places, sets, owned), jnp.float32),
            "restart",
            in_specs=[ANY, VMEM],
            out_specs=VMEM,
            flops=2 * places * sets * owned * seed_ids.shape[1],
            size=4 * places * sets * owned,
        )(after, seeds)

    def finish(incoming, restart, last):
        return call(
            functools.partial(finish_kernel, last),
            piece if last else jax.ShapeDtypeStruct((sets, owned), low),
            "last" if last else "next",
            in_specs=[VMEM] * (len(incoming) + 2),
            out_specs=VMEM,
            size=12 * sets * owned,
        )(*incoming, restart, degree)

    if (rows, cols, ITERATIONS) == (2, 4, 2):
        given = jax.ShapeDtypeStruct((2, sets + owned + DEGREE_LINES, owned), jnp.float32)
        early = call(
            functools.partial(first_kernel, cols),
            given,
            "first",
            in_specs=[VMEM] * (cols + 2),
            out_specs=VMEM,
            flops=8 * sets * (cols - 1) * owned * owned,
            size=8 * cols * owned * owned,
        )(parts[0], *parts[2:], *weights, degree)
        mine = call(
            nearest_kernel,
            given,
            "nearest",
            in_specs=[VMEM] * 4,
            out_specs=VMEM,
            flops=8 * sets * owned * owned,
            size=24 * sets * owned,
        )(early, parts[1], *weights)
        theirs = swap_rows(mine)
        restart = count_restart(2, mine)
        other, both = call(
            both_kernel,
            [jax.ShapeDtypeStruct((sets, owned), low), jax.ShapeDtypeStruct((2, sets, owned), low)],
            "both",
            in_specs=[VMEM] * 3,
            out_specs=[VMEM] * 2,
            size=24 * sets * owned,
        )(mine, theirs, restart)
        side = from_side(other, cols)
        near = from_hop(both, cols)
        foreign = call(
            foreign_kernel,
            jax.ShapeDtypeStruct((2, owned, 2 * owned), low),
            "foreign",
            in_specs=[ANY, VMEM],
            out_specs=VMEM,
            size=16 * owned * owned,
        )(other, theirs)

        def second(place, *after):
            early = call(
                functools.partial(second_kernel, place, len(after)),
                piece,
                "second",
                in_specs=[ANY] * len(after) + [VMEM] * 4,
                out_specs=VMEM,
                flops=12 * sets * owned * owned,
                size=12 * owned * owned,
            )(*after, both, near, weights[place], foreign)
            return call(
                side_kernel,
                piece,
                "side",
                in_specs=[VMEM] * 3,
                out_specs=VMEM,
                flops=4 * sets * owned * owned,
                size=16 * sets * owned,
            )(early, side, weights[place])

        leaving = second(1)
        received = swap_rows(leaving)
        return finish((second(0, leaving), received), restart, True)

    for round_index in range(ITERATIONS):
        last = round_index == ITERATIONS - 1
        if rows == 2:
            leaving, = multiply(parts, weights[1:])
            received = swap_rows(leaving)
            staying, = multiply(parts, weights[:1], (leaving,))
            incoming = (staying, received)
        else:
            leaving = jnp.stack(multiply(parts, weights))
            incoming = (lax.psum_scatter(leaving, "row", scatter_dimension=0, tiled=False),)
        if not round_index:
            restart = count_restart(1, leaving)
        value = finish(incoming, restart, last)
        if not last:
            parts = spread(value)
    return value


def solution(mesh):
    placed = (
        P("row", "col", None, None, None),
        P("row", "col", None),
        P("row", "col", None),
        P("row", "col"),
        P(("row", "col")),
        P("seed", None),
        P("seed", ("row", "col")),
    )
    return jax.shard_map(
        local, mesh=mesh, in_specs=placed, out_specs=P("seed", ("row", "col")), check_vma=False
    )
```

```python
import functools
import math

import jax
import jax.numpy as jnp
from jax import lax
from jax.experimental import pallas as pl
from jax.experimental.pallas import tpu as pltpu
from jax.sharding import PartitionSpec as P

ITERATIONS = 2


damping = 0.85

VMEM = pl.BlockSpec(memory_space=pltpu.VMEM)
SMEM = pl.BlockSpec(memory_space=pltpu.SMEM)
HBM = pl.BlockSpec(memory_space=pltpu.HBM)
ANY = pl.BlockSpec(memory_space=pl.ANY)

TILES_VMEM = 32 * 1024 * 1024
SMALL_VMEM = 8 * 1024 * 1024
STRIPS = 4
UNROLL = 32
PIECES = 4
DEGREE_LINES = 8


def in_hbm(*arrays):
    return [pltpu.with_memory_space_constraint(array, pltpu.HBM) for array in arrays]


def call(kernel, out_shape, name, **options):
    return pl.pallas_call(
        kernel,
        out_shape=out_shape,
        compiler_params=pltpu.CompilerParams(vmem_limit_bytes=options.pop("vmem", SMALL_VMEM)),
        cost_estimate=pl.CostEstimate(
            flops=options.pop("flops", 0), bytes_accessed=options.pop("size", 0), transcendentals=0
        ),
        name=name,
        **options,
    )


def partner(index, offset, extent):
    if extent & (extent - 1) == 0:
        return index ^ offset
    return (index + offset) % extent


def from_column(value, cols, offset):
    return lax.ppermute(value, "col", [(partner(col, offset, cols), col) for col in range(cols)])


def hop(row):
    return row + 2


def from_hop(value, cols):
    pairs = [((1 - row) * cols + (col ^ hop(row)), row * cols + col) for row in range(2) for col in range(cols)]
    return lax.ppermute(value, ("row", "col"), pairs)


def from_side(value, cols):
    pairs = [((1 - row) * cols + (col ^ 1), row * cols + col) for row in range(2) for col in range(cols)]
    return lax.ppermute(value, ("row", "col"), pairs)


def swap_rows(value):
    return lax.ppermute(value, "row", [(0, 1), (1, 0)])


def scale_kernel(
    prior_hbm, degree_hbm, out_hbm, in_hbm, seeds_hbm,
    scaled_ref, out_ref, in_ref, seeds_ref, prior_ref, degree_ref, arrived,
):
    pieces = prior_ref.shape[0] // PIECES
    moves = [(degree_hbm, degree_ref)]
    for piece in range(PIECES):
        lines = pl.ds(piece * pieces, pieces)
        moves.append((prior_hbm.at[lines], prior_ref.at[lines]))
    moves += [(out_hbm, out_ref), (in_hbm, in_ref), (seeds_hbm, seeds_ref)]
    copies = [
        pltpu.make_async_copy(source, place, arrived.at[index])
        for index, (source, place) in enumerate(moves)
    ]
    for copy in copies:
        copy.start()
    for copy in copies[:1 + PIECES]:
        copy.wait()
    scaled = (prior_ref[...] / degree_ref[...].astype(jnp.float32)).astype(jnp.bfloat16)
    scaled_ref[...] = scaled
    for copy in copies[1 + PIECES:]:
        copy.wait()


def sum_kernel(
    rows, cols, owned_blocks, after_ref, count_ref, out_ref, in_ref, tiles_ref, *rest
):
    weight_refs, totals = rest[:rows], rest[rows:]
    in_blocks = cols * owned_blocks
    slots, edge = tiles_ref.shape[2], tiles_ref.shape[3]
    owned = owned_blocks * edge
    spare, strip = totals[0].shape[0] - 1, totals[0].shape[1]
    unroll = math.gcd(slots, UNROLL)
    row = lax.axis_index("row")
    occupied = count_ref[0, 0]

    for total in totals:
        total[...] = jnp.zeros(total.shape, jnp.float32)

    def add_tiles(step, carry):
        at = step * unroll
        places = []
        for lane in range(unroll):
            slot = at + lane
            pair = out_ref[0, 0, slot] * in_blocks + in_ref[0, 0, slot]
            places.append((slot, jnp.where(slot < occupied, pair, spare)))
        for slot, pair in places:
            for index, total in enumerate(totals):
                lines = slice(index * strip, (index + 1) * strip)
                total[pair] += tiles_ref[0, 0, slot, lines].astype(jnp.float32)
        return carry

    lax.fori_loop(0, (occupied + unroll - 1) // unroll, add_tiles, 0)

    for place in range(rows):
        owner = partner(row, place, rows) if rows == 2 else place
        for block in range(owned_blocks):
            columns = slice(block * edge, (block + 1) * edge)
            for source in range(in_blocks):
                pair = (owner * owned_blocks + block) * in_blocks + source
                for index, total in enumerate(totals):
                    value = total[pair]
                    high = value.astype(jnp.bfloat16)
                    low = (value - high.astype(jnp.float32)).astype(jnp.bfloat16)
                    column, line = source // owned_blocks, source % owned_blocks * edge + index * strip
                    lines = slice(line, line + strip)
                    weight_refs[place][column, lines, columns] = high
                    weight_refs[place][column, lines, owned + block * edge:owned + (block + 1) * edge] = low


def times_weight(parts, weights):
    incoming = None
    for start in range(0, len(parts), 2):
        term = jnp.dot(
            jnp.concatenate(parts[start:start + 2], axis=1),
            jnp.concatenate(weights[start:start + 2], axis=0),
            preferred_element_type=jnp.float32,
        )
        incoming = term if incoming is None else incoming + term
    owned = incoming.shape[1] // 2
    return incoming[:, :owned] + incoming[:, owned:]


def product_kernel(rows, cols, after, *refs):
    part_refs, refs = refs[after:after + cols], refs[after + cols:]
    weight_refs, result_refs = refs[:len(refs) // 2], refs[len(refs) // 2:]
    col = lax.axis_index("col")
    parts = [ref[...] for ref in part_refs]
    for weight_ref, result_ref in zip(weight_refs, result_refs):
        weights = [weight_ref[partner(col, offset, cols)] for offset in range(cols)]
        result_ref[...] = times_weight(parts, weights)


def restart_kernel(rows, cols, after_ref, seeds_ref, restart_ref):
    seed_total, sets = seeds_ref.shape
    places, _, owned = restart_ref.shape
    for place in range(places):
        row = partner(lax.axis_index("row"), place, rows)
        first = (row * cols + lax.axis_index("col")) * owned
        vertex = lax.broadcasted_iota(jnp.int32, (owned, sets), 0) + first
        restart = jnp.zeros((owned, sets), jnp.float32)
        for seed in range(seed_total):
            restart += (seeds_ref[seed:seed + 1, :] == vertex).astype(jnp.float32)
        restart_ref[place] = (1.0 - damping) * restart.T


def first_kernel(cols, *refs):
    part_refs, (own_ref, other_ref, degree_ref, given_ref) = refs[:cols - 1], refs[cols - 1:]
    row, col = lax.axis_index("row"), lax.axis_index("col")
    parts = [ref[...] for ref in part_refs]
    sets, owned = parts[0].shape
    columns = [col] + [partner(col, offset, cols) for offset in range(2, cols)]
    wanted = col ^ hop(1 - row)
    for place, weight_ref in enumerate((own_ref, other_ref)):
        given_ref[place, :sets] = times_weight(parts, [weight_ref[column] for column in columns])
        given_ref[place, sets:sets + owned] = weight_ref[wanted, :, :owned].astype(
            jnp.float32
        ) + weight_ref[wanted, :, owned:].astype(jnp.float32)
        given_ref[place, sets + owned:] = jnp.broadcast_to(
            degree_ref[...].astype(jnp.float32), (given_ref.shape[1] - sets - owned, owned)
        )


def nearest_kernel(early_ref, part_ref, own_ref, other_ref, given_ref):
    col = lax.axis_index("col")
    sets = part_ref.shape[0]
    for place, weight_ref in enumerate((own_ref, other_ref)):
        given_ref[place, :sets] = early_ref[place, :sets] + times_weight([part_ref[...]], [weight_ref[col ^ 1]])
        given_ref[place, sets:] = early_ref[place, sets:]


def both_kernel(mine_ref, theirs_ref, restart_ref, other_ref, scaled_ref):
    _, sets, owned = restart_ref.shape
    for place in range(2):
        incoming = mine_ref[place, :sets] + theirs_ref[1 - place, :sets]
        degree = (theirs_ref if place else mine_ref)[0, sets + owned:sets + owned + 1]
        risk = restart_ref[place] + damping * incoming
        scaled = (risk / degree).astype(jnp.bfloat16)
        scaled_ref[place] = scaled
        if place:
            other_ref[...] = scaled


def foreign_kernel(after_ref, theirs_ref, weight_ref):
    _, owned, double = weight_ref.shape
    sets = theirs_ref.shape[1] - owned - DEGREE_LINES
    for place in range(2):
        value = theirs_ref[1 - place, sets:sets + owned]
        high = value.astype(jnp.bfloat16)
        weight_ref[place, :, :owned] = high
        weight_ref[place, :, owned:] = (value - high.astype(jnp.float32)).astype(jnp.bfloat16)


def second_kernel(place, after, *refs):
    both_ref, hop_ref, weight_ref, foreign_ref, result_ref = refs[after:]
    row, col = lax.axis_index("row"), lax.axis_index("col")
    parts = [hop_ref[1], hop_ref[0], both_ref[0]]
    weights = [weight_ref[col ^ hop(row)], foreign_ref[place], weight_ref[col]]
    result_ref[...] = times_weight(parts, weights)


def side_kernel(early_ref, side_ref, weight_ref, result_ref):
    result_ref[...] = early_ref[...] + times_weight([side_ref[...]], [weight_ref[lax.axis_index("col") ^ 1]])


def finish_kernel(last, *refs):
    *incoming_refs, restart_ref, degree_ref, result_ref = refs
    risk = restart_ref[0] + damping * sum(ref[...] for ref in incoming_refs)
    if last:
        result_ref[...] = risk
    else:
        result_ref[...] = (risk / degree_ref[...].astype(jnp.float32)).astype(jnp.bfloat16)


def local(tiles, tile_out, tile_in, tile_count, out_degree, seed_ids, prior):
    rows, cols = lax.axis_size("row"), lax.axis_size("col")
    sets, owned = prior.shape
    slots, edge = tiles.shape[2], tiles.shape[3]
    owned_blocks = owned // edge
    in_blocks, out_blocks = cols * owned_blocks, rows * owned_blocks
    degree = out_degree.reshape(1, owned)
    low = jnp.bfloat16

    scaled, out_ids, in_ids, seeds = call(
        scale_kernel,
        [
            jax.ShapeDtypeStruct((sets, owned), low),
            pltpu.SMEM(tile_out.shape, jnp.int32),
            pltpu.SMEM(tile_in.shape, jnp.int32),
            jax.ShapeDtypeStruct((seed_ids.shape[1], sets), jnp.int32),
        ],
        "scale",
        in_specs=[HBM] * 5,
        out_specs=[VMEM, SMEM, SMEM, VMEM],
        scratch_shapes=[
            pltpu.VMEM((sets, owned), jnp.float32),
            pltpu.VMEM((1, owned), jnp.int32),
            pltpu.SemaphoreType.DMA((4 + PIECES,)),
        ],
        flops=16 * slots * edge**3,
        size=6 * sets * owned,
    )(*in_hbm(prior, degree, tile_out, tile_in, seed_ids.T))

    def spread(value):
        return [from_column(value, cols, offset) if offset else value for offset in range(cols)]

    parts = spread(scaled)

    weights = call(
        functools.partial(sum_kernel, rows, cols, owned_blocks),
        [jax.ShapeDtypeStruct((cols, owned, 2 * owned), low)] * rows,
        "sum_tiles",
        in_specs=[ANY] + [SMEM] * 3 + [VMEM],
        out_specs=[VMEM] * rows,
        scratch_shapes=[pltpu.VMEM((out_blocks * in_blocks + 1, edge // STRIPS, edge), jnp.float32)] * STRIPS,
        vmem=TILES_VMEM,
        flops=slots * edge * edge,
        size=2 * slots * edge * edge,
    )(scaled, tile_count, out_ids, in_ids, tiles)

    piece = jax.ShapeDtypeStruct((sets, owned), jnp.float32)

    def multiply(parts, weights, after=()):
        return call(
            functools.partial(product_kernel, rows, cols, len(after)),
            [piece] * len(weights),
            "product",
            in_specs=[ANY] * len(after) + [VMEM] * (cols + len(weights)),
            out_specs=[VMEM] * len(weights),
            flops=4 * sets * len(weights) * cols * owned * owned,
            size=4 * len(weights) * cols * owned * owned,
        )(*after, *parts, *weights)

    def count_restart(places, after):
        return call(
            functools.partial(restart_kernel, rows, cols),
            jax.ShapeDtypeStruct((places, sets, owned), jnp.float32),
            "restart",
            in_specs=[ANY, VMEM],
            out_specs=VMEM,
            flops=2 * places * sets * owned * seed_ids.shape[1],
            size=4 * places * sets * owned,
        )(after, seeds)

    def finish(incoming, restart, last):
        return call(
            functools.partial(finish_kernel, last),
            piece if last else jax.ShapeDtypeStruct((sets, owned), low),
            "last" if last else "next",
            in_specs=[VMEM] * (len(incoming) + 2),
            out_specs=VMEM,
            size=12 * sets * owned,
        )(*incoming, restart, degree)

    if (rows, cols, ITERATIONS) == (2, 4, 2):
        given = jax.ShapeDtypeStruct((2, sets + owned + DEGREE_LINES, owned), jnp.float32)
        early = call(
            functools.partial(first_kernel, cols),
            given,
            "first",
            in_specs=[VMEM] * (cols + 2),
            out_specs=VMEM,
            flops=8 * sets * (cols - 1) * owned * owned,
            size=8 * cols * owned * owned,
        )(parts[0], *parts[2:], *weights, degree)
        mine = call(
            nearest_kernel,
            given,
            "nearest",
            in_specs=[VMEM] * 4,
            out_specs=VMEM,
            flops=8 * sets * owned * owned,
            size=24 * sets * owned,
        )(early, parts[1], *weights)
        theirs = swap_rows(mine)
        restart = count_restart(2, mine)
        other, both = call(
            both_kernel,
            [jax.ShapeDtypeStruct((sets, owned), low), jax.ShapeDtypeStruct((2, sets, owned), low)],
            "both",
            in_specs=[VMEM] * 3,
            out_specs=[VMEM] * 2,
            size=24 * sets * owned,
        )(mine, theirs, restart)
        side = from_side(other, cols)
        near = from_hop(both, cols)
        foreign = call(
            foreign_kernel,
            jax.ShapeDtypeStruct((2, owned, 2 * owned), low),
            "foreign",
            in_specs=[ANY, VMEM],
            out_specs=VMEM,
            size=16 * owned * owned,
        )(other, theirs)

        def second(place, *after):
            early = call(
                functools.partial(second_kernel, place, len(after)),
                piece,
                "second",
                in_specs=[ANY] * len(after) + [VMEM] * 4,
                out_specs=VMEM,
                flops=12 * sets * owned * owned,
                size=12 * owned * owned,
            )(*after, both, near, weights[place], foreign)
            return call(
                side_kernel,
                piece,
                "side",
                in_specs=[VMEM] * 3,
                out_specs=VMEM,
                flops=4 * sets * owned * owned,
                size=16 * sets * owned,
            )(early, side, weights[place])

        leaving = second(1)
        received = swap_rows(leaving)
        return finish((second(0, leaving), received), restart, True)

    for round_index in range(ITERATIONS):
        last = round_index == ITERATIONS - 1
        if rows == 2:
            leaving, = multiply(parts, weights[1:])
            received = swap_rows(leaving)
            staying, = multiply(parts, weights[:1], (leaving,))
            incoming = (staying, received)
        else:
            leaving = jnp.stack(multiply(parts, weights))
            incoming = (lax.psum_scatter(leaving, "row", scatter_dimension=0, tiled=False),)
        if not round_index:
            restart = count_restart(1, leaving)
        value = finish(incoming, restart, last)
        if not last:
            parts = spread(value)
    return value


def solution(mesh):
    placed = (
        P("row", "col", None, None, None),
        P("row", "col", None),
        P("row", "col", None),
        P("row", "col"),
        P(("row", "col")),
        P("seed", None),
        P("seed", ("row", "col")),
    )
    return jax.shard_map(
        local, mesh=mesh, in_specs=placed, out_specs=P("seed", ("row", "col")), check_vma=False
    )
```

```python
import functools
import math

import jax
import jax.numpy as jnp
from jax import lax
from jax.experimental import pallas as pl
from jax.experimental.pallas import tpu as pltpu
from jax.sharding import PartitionSpec as P

ITERATIONS = 2


damping = 0.85

VMEM = pl.BlockSpec(memory_space=pltpu.VMEM)
SMEM = pl.BlockSpec(memory_space=pltpu.SMEM)
HBM = pl.BlockSpec(memory_space=pltpu.HBM)
ANY = pl.BlockSpec(memory_space=pl.ANY)

TILES_VMEM = 32 * 1024 * 1024
SMALL_VMEM = 8 * 1024 * 1024
STRIPS = 4
UNROLL = 32
DEGREE_LINES = 8


def in_hbm(*arrays):
    return [pltpu.with_memory_space_constraint(array, pltpu.HBM) for array in arrays]


def call(kernel, out_shape, name, **options):
    return pl.pallas_call(
        kernel,
        out_shape=out_shape,
        compiler_params=pltpu.CompilerParams(vmem_limit_bytes=options.pop("vmem", SMALL_VMEM)),
        cost_estimate=pl.CostEstimate(
            flops=options.pop("flops", 0), bytes_accessed=options.pop("size", 0), transcendentals=0
        ),
        name=name,
        **options,
    )


def partner(index, offset, extent):
    if extent & (extent - 1) == 0:
        return index ^ offset
    return (index + offset) % extent


def from_column(value, cols, offset):
    return lax.ppermute(value, "col", [(partner(col, offset, cols), col) for col in range(cols)])


def hop(row):
    return row + 2


def from_hop(value, cols):
    pairs = [((1 - row) * cols + (col ^ hop(row)), row * cols + col) for row in range(2) for col in range(cols)]
    return lax.ppermute(value, ("row", "col"), pairs)


def from_side(value, cols):
    pairs = [((1 - row) * cols + (col ^ 1), row * cols + col) for row in range(2) for col in range(cols)]
    return lax.ppermute(value, ("row", "col"), pairs)


def swap_rows(value):
    return lax.ppermute(value, "row", [(0, 1), (1, 0)])


def scale_kernel(
    prior_hbm, degree_hbm, out_hbm, in_hbm, seeds_hbm,
    scaled_ref, out_ref, in_ref, seeds_ref, prior_ref, degree_ref, arrived,
):
    moves = (
        (prior_hbm, prior_ref), (degree_hbm, degree_ref),
        (out_hbm, out_ref), (in_hbm, in_ref), (seeds_hbm, seeds_ref),
    )
    copies = [
        pltpu.make_async_copy(source, place, arrived.at[index])
        for index, (source, place) in enumerate(moves)
    ]
    for copy in copies:
        copy.start()
    for copy in copies[:2]:
        copy.wait()
    scaled = (prior_ref[...] / degree_ref[...].astype(jnp.float32)).astype(jnp.bfloat16)
    scaled_ref[...] = scaled
    for copy in copies[2:]:
        copy.wait()


def sum_kernel(
    rows, cols, owned_blocks, after_ref, count_ref, out_ref, in_ref, tiles_ref, *rest
):
    weight_refs, totals = rest[:rows], rest[rows:]
    in_blocks = cols * owned_blocks
    slots, edge = tiles_ref.shape[2], tiles_ref.shape[3]
    owned = owned_blocks * edge
    spare, strip = totals[0].shape[0] - 1, totals[0].shape[1]
    unroll = math.gcd(slots, UNROLL)
    row = lax.axis_index("row")
    occupied = count_ref[0, 0]

    for total in totals:
        total[...] = jnp.zeros(total.shape, jnp.float32)

    def add_tiles(step, carry):
        at = step * unroll
        places = []
        for lane in range(unroll):
            slot = at + lane
            pair = out_ref[0, 0, slot] * in_blocks + in_ref[0, 0, slot]
            places.append((slot, jnp.where(slot < occupied, pair, spare)))
        for slot, pair in places:
            for index, total in enumerate(totals):
                lines = slice(index * strip, (index + 1) * strip)
                total[pair] += tiles_ref[0, 0, slot, lines].astype(jnp.float32)
        return carry

    lax.fori_loop(0, (occupied + unroll - 1) // unroll, add_tiles, 0)

    for place in range(rows):
        owner = partner(row, place, rows) if rows == 2 else place
        for block in range(owned_blocks):
            columns = slice(block * edge, (block + 1) * edge)
            for source in range(in_blocks):
                pair = (owner * owned_blocks + block) * in_blocks + source
                for index, total in enumerate(totals):
                    value = total[pair]
                    high = value.astype(jnp.bfloat16)
                    low = (value - high.astype(jnp.float32)).astype(jnp.bfloat16)
                    column, line = source // owned_blocks, source % owned_blocks * edge + index * strip
                    lines = slice(line, line + strip)
                    weight_refs[place][column, lines, columns] = high
                    weight_refs[place][column, lines, owned + block * edge:owned + (block + 1) * edge] = low


def times_weight(parts, weights):
    incoming = None
    for start in range(0, len(parts), 2):
        term = jnp.dot(
            jnp.concatenate(parts[start:start + 2], axis=1),
            jnp.concatenate(weights[start:start + 2], axis=0),
            preferred_element_type=jnp.float32,
        )
        incoming = term if incoming is None else incoming + term
    owned = incoming.shape[1] // 2
    return incoming[:, :owned] + incoming[:, owned:]


def product_kernel(rows, cols, after, *refs):
    part_refs, refs = refs[after:after + cols], refs[after + cols:]
    weight_refs, result_refs = refs[:len(refs) // 2], refs[len(refs) // 2:]
    col = lax.axis_index("col")
    parts = [ref[...] for ref in part_refs]
    for weight_ref, result_ref in zip(weight_refs, result_refs):
        weights = [weight_ref[partner(col, offset, cols)] for offset in range(cols)]
        result_ref[...] = times_weight(parts, weights)


def restart_kernel(rows, cols, after_ref, seeds_ref, restart_ref):
    seed_total, sets = seeds_ref.shape
    places, _, owned = restart_ref.shape
    for place in range(places):
        row = partner(lax.axis_index("row"), place, rows)
        first = (row * cols + lax.axis_index("col")) * owned
        vertex = lax.broadcasted_iota(jnp.int32, (owned, sets), 0) + first
        restart = jnp.zeros((owned, sets), jnp.float32)
        for seed in range(seed_total):
            restart += (seeds_ref[seed:seed + 1, :] == vertex).astype(jnp.float32)
        restart_ref[place] = (1.0 - damping) * restart.T


def first_kernel(cols, *refs):
    part_refs, (own_ref, other_ref, degree_ref, given_ref) = refs[:cols - 1], refs[cols - 1:]
    row, col = lax.axis_index("row"), lax.axis_index("col")
    parts = [ref[...] for ref in part_refs]
    sets, owned = parts[0].shape
    columns = [col] + [partner(col, offset, cols) for offset in range(2, cols)]
    wanted = col ^ hop(1 - row)
    for place, weight_ref in enumerate((own_ref, other_ref)):
        given_ref[place, :sets] = times_weight(parts, [weight_ref[column] for column in columns])
        given_ref[place, sets:sets + owned] = weight_ref[wanted, :, :owned].astype(
            jnp.float32
        ) + weight_ref[wanted, :, owned:].astype(jnp.float32)
        given_ref[place, sets + owned:] = jnp.broadcast_to(
            degree_ref[...].astype(jnp.float32), (given_ref.shape[1] - sets - owned, owned)
        )


def nearest_kernel(early_ref, part_ref, own_ref, other_ref, given_ref):
    col = lax.axis_index("col")
    sets, owned = part_ref.shape
    terms = jnp.dot(
        part_ref[...],
        jnp.concatenate([own_ref[col ^ 1], other_ref[col ^ 1]], axis=1),
        preferred_element_type=jnp.float32,
    )
    for place in range(2):
        at = 2 * place * owned
        term = terms[:, at:at + owned] + terms[:, at + owned:at + 2 * owned]
        given_ref[place, :sets] = early_ref[place, :sets] + term
        given_ref[place, sets:] = early_ref[place, sets:]


def both_kernel(mine_ref, theirs_ref, restart_ref, other_ref, scaled_ref):
    _, sets, owned = restart_ref.shape
    for place in range(2):
        incoming = mine_ref[place, :sets] + theirs_ref[1 - place, :sets]
        degree = (theirs_ref if place else mine_ref)[0, sets + owned:sets + owned + 1]
        risk = restart_ref[place] + damping * incoming
        scaled = (risk / degree).astype(jnp.bfloat16)
        scaled_ref[place] = scaled
        if place:
            other_ref[...] = scaled


def foreign_kernel(after_ref, theirs_ref, weight_ref):
    _, owned, double = weight_ref.shape
    sets = theirs_ref.shape[1] - owned - DEGREE_LINES
    for place in range(2):
        value = theirs_ref[1 - place, sets:sets + owned]
        high = value.astype(jnp.bfloat16)
        weight_ref[place, :, :owned] = high
        weight_ref[place, :, owned:] = (value - high.astype(jnp.float32)).astype(jnp.bfloat16)


def second_kernel(place, after, *refs):
    both_ref, hop_ref, weight_ref, foreign_ref, result_ref = refs[after:]
    row, col = lax.axis_index("row"), lax.axis_index("col")
    parts = [hop_ref[1], hop_ref[0], both_ref[0]]
    weights = [weight_ref[col ^ hop(row)], foreign_ref[place], weight_ref[col]]
    result_ref[...] = times_weight(parts, weights)


def side_kernel(early_ref, side_ref, weight_ref, result_ref):
    result_ref[...] = early_ref[...] + times_weight([side_ref[...]], [weight_ref[lax.axis_index("col") ^ 1]])


def finish_kernel(last, *refs):
    *incoming_refs, restart_ref, degree_ref, result_ref = refs
    risk = restart_ref[0] + damping * sum(ref[...] for ref in incoming_refs)
    if last:
        result_ref[...] = risk
    else:
        result_ref[...] = (risk / degree_ref[...].astype(jnp.float32)).astype(jnp.bfloat16)


def local(tiles, tile_out, tile_in, tile_count, out_degree, seed_ids, prior):
    rows, cols = lax.axis_size("row"), lax.axis_size("col")
    sets, owned = prior.shape
    slots, edge = tiles.shape[2], tiles.shape[3]
    owned_blocks = owned // edge
    in_blocks, out_blocks = cols * owned_blocks, rows * owned_blocks
    degree = out_degree.reshape(1, owned)
    low = jnp.bfloat16

    scaled, out_ids, in_ids, seeds = call(
        scale_kernel,
        [
            jax.ShapeDtypeStruct((sets, owned), low),
            pltpu.SMEM(tile_out.shape, jnp.int32),
            pltpu.SMEM(tile_in.shape, jnp.int32),
            jax.ShapeDtypeStruct((seed_ids.shape[1], sets), jnp.int32),
        ],
        "scale",
        in_specs=[HBM] * 5,
        out_specs=[VMEM, SMEM, SMEM, VMEM],
        scratch_shapes=[
            pltpu.VMEM((sets, owned), jnp.float32),
            pltpu.VMEM((1, owned), jnp.int32),
            pltpu.SemaphoreType.DMA((5,)),
        ],
        flops=16 * slots * edge**3,
        size=6 * sets * owned,
    )(*in_hbm(prior, degree, tile_out, tile_in, seed_ids.T))

    def spread(value):
        return [from_column(value, cols, offset) if offset else value for offset in range(cols)]

    parts = spread(scaled)

    weights = call(
        functools.partial(sum_kernel, rows, cols, owned_blocks),
        [jax.ShapeDtypeStruct((cols, owned, 2 * owned), low)] * rows,
        "sum_tiles",
        in_specs=[ANY] + [SMEM] * 3 + [VMEM],
        out_specs=[VMEM] * rows,
        scratch_shapes=[pltpu.VMEM((out_blocks * in_blocks + 1, edge // STRIPS, edge), jnp.float32)] * STRIPS,
        vmem=TILES_VMEM,
        flops=slots * edge * edge,
        size=2 * slots * edge * edge,
    )(scaled, tile_count, out_ids, in_ids, tiles)

    piece = jax.ShapeDtypeStruct((sets, owned), jnp.float32)

    def multiply(parts, weights, after=()):
        return call(
            functools.partial(product_kernel, rows, cols, len(after)),
            [piece] * len(weights),
            "product",
            in_specs=[ANY] * len(after) + [VMEM] * (cols + len(weights)),
            out_specs=[VMEM] * len(weights),
            flops=4 * sets * len(weights) * cols * owned * owned,
            size=4 * len(weights) * cols * owned * owned,
        )(*after, *parts, *weights)

    def count_restart(places, after):
        return call(
            functools.partial(restart_kernel, rows, cols),
            jax.ShapeDtypeStruct((places, sets, owned), jnp.float32),
            "restart",
            in_specs=[ANY, VMEM],
            out_specs=VMEM,
            flops=2 * places * sets * owned * seed_ids.shape[1],
            size=4 * places * sets * owned,
        )(after, seeds)

    def finish(incoming, restart, last):
        return call(
            functools.partial(finish_kernel, last),
            piece if last else jax.ShapeDtypeStruct((sets, owned), low),
            "last" if last else "next",
            in_specs=[VMEM] * (len(incoming) + 2),
            out_specs=VMEM,
            size=12 * sets * owned,
        )(*incoming, restart, degree)

    if (rows, cols, ITERATIONS) == (2, 4, 2):
        given = jax.ShapeDtypeStruct((2, sets + owned + DEGREE_LINES, owned), jnp.float32)
        early = call(
            functools.partial(first_kernel, cols),
            given,
            "first",
            in_specs=[VMEM] * (cols + 2),
            out_specs=VMEM,
            flops=8 * sets * (cols - 1) * owned * owned,
            size=8 * cols * owned * owned,
        )(parts[0], *parts[2:], *weights, degree)
        mine = call(
            nearest_kernel,
            given,
            "nearest",
            in_specs=[VMEM] * 4,
            out_specs=VMEM,
            flops=8 * sets * owned * owned,
            size=24 * sets * owned,
        )(early, parts[1], *weights)
        theirs = swap_rows(mine)
        restart = count_restart(2, mine)
        other, both = call(
            both_kernel,
            [jax.ShapeDtypeStruct((sets, owned), low), jax.ShapeDtypeStruct((2, sets, owned), low)],
            "both",
            in_specs=[VMEM] * 3,
            out_specs=[VMEM] * 2,
            size=24 * sets * owned,
        )(mine, theirs, restart)
        side = from_side(other, cols)
        near = from_hop(both, cols)
        foreign = call(
            foreign_kernel,
            jax.ShapeDtypeStruct((2, owned, 2 * owned), low),
            "foreign",
            in_specs=[ANY, VMEM],
            out_specs=VMEM,
            size=16 * owned * owned,
        )(other, theirs)

        def second(place, *after):
            early = call(
                functools.partial(second_kernel, place, len(after)),
                piece,
                "second",
                in_specs=[ANY] * len(after) + [VMEM] * 4,
                out_specs=VMEM,
                flops=12 * sets * owned * owned,
                size=12 * owned * owned,
            )(*after, both, near, weights[place], foreign)
            return call(
                side_kernel,
                piece,
                "side",
                in_specs=[VMEM] * 3,
                out_specs=VMEM,
                flops=4 * sets * owned * owned,
                size=16 * sets * owned,
            )(early, side, weights[place])

        leaving = second(1)
        received = swap_rows(leaving)
        return finish((second(0, leaving), received), restart, True)

    for round_index in range(ITERATIONS):
        last = round_index == ITERATIONS - 1
        if rows == 2:
            leaving, = multiply(parts, weights[1:])
            received = swap_rows(leaving)
            staying, = multiply(parts, weights[:1], (leaving,))
            incoming = (staying, received)
        else:
            leaving = jnp.stack(multiply(parts, weights))
            incoming = (lax.psum_scatter(leaving, "row", scatter_dimension=0, tiled=False),)
        if not round_index:
            restart = count_restart(1, leaving)
        value = finish(incoming, restart, last)
        if not last:
            parts = spread(value)
    return value


def solution(mesh):
    placed = (
        P("row", "col", None, None, None),
        P("row", "col", None),
        P("row", "col", None),
        P("row", "col"),
        P(("row", "col")),
        P("seed", None),
        P("seed", ("row", "col")),
    )
    return jax.shard_map(
        local, mesh=mesh, in_specs=placed, out_specs=P("seed", ("row", "col")), check_vma=False
    )
```

```python
import functools
import math

import jax
import jax.numpy as jnp
from jax import lax
from jax.experimental import pallas as pl
from jax.experimental.pallas import tpu as pltpu
from jax.sharding import PartitionSpec as P

ITERATIONS = 2


damping = 0.85

VMEM = pl.BlockSpec(memory_space=pltpu.VMEM)
SMEM = pl.BlockSpec(memory_space=pltpu.SMEM)
HBM = pl.BlockSpec(memory_space=pltpu.HBM)
ANY = pl.BlockSpec(memory_space=pl.ANY)

TILES_VMEM = 32 * 1024 * 1024
SMALL_VMEM = 8 * 1024 * 1024
STRIPS = 4
UNROLL = 64
DEGREE_LINES = 8


def in_hbm(*arrays):
    return [pltpu.with_memory_space_constraint(array, pltpu.HBM) for array in arrays]


def call(kernel, out_shape, name, **options):
    return pl.pallas_call(
        kernel,
        out_shape=out_shape,
        compiler_params=pltpu.CompilerParams(vmem_limit_bytes=options.pop("vmem", SMALL_VMEM)),
        cost_estimate=pl.CostEstimate(
            flops=options.pop("flops", 0), bytes_accessed=options.pop("size", 0), transcendentals=0
        ),
        name=name,
        **options,
    )


def partner(index, offset, extent):
    if extent & (extent - 1) == 0:
        return index ^ offset
    return (index + offset) % extent


def from_column(value, cols, offset):
    return lax.ppermute(value, "col", [(partner(col, offset, cols), col) for col in range(cols)])


def hop(row):
    return row + 2


def from_hop(value, cols):
    pairs = [((1 - row) * cols + (col ^ hop(row)), row * cols + col) for row in range(2) for col in range(cols)]
    return lax.ppermute(value, ("row", "col"), pairs)


def from_side(value, cols):
    pairs = [((1 - row) * cols + (col ^ 1), row * cols + col) for row in range(2) for col in range(cols)]
    return lax.ppermute(value, ("row", "col"), pairs)


def swap_rows(value):
    return lax.ppermute(value, "row", [(0, 1), (1, 0)])


def scale_kernel(
    prior_hbm, degree_hbm, out_hbm, in_hbm, seeds_hbm,
    scaled_ref, out_ref, in_ref, seeds_ref, prior_ref, degree_ref, arrived,
):
    moves = (
        (prior_hbm, prior_ref), (degree_hbm, degree_ref),
        (out_hbm, out_ref), (in_hbm, in_ref), (seeds_hbm, seeds_ref),
    )
    copies = [
        pltpu.make_async_copy(source, place, arrived.at[index])
        for index, (source, place) in enumerate(moves)
    ]
    for copy in copies:
        copy.start()
    for copy in copies[:2]:
        copy.wait()
    scaled = (prior_ref[...] / degree_ref[...].astype(jnp.float32)).astype(jnp.bfloat16)
    scaled_ref[...] = scaled
    for copy in copies[2:]:
        copy.wait()


def sum_kernel(
    rows, cols, owned_blocks, after_ref, count_ref, out_ref, in_ref, tiles_ref, *rest
):
    weight_refs, totals = rest[:rows], rest[rows:]
    in_blocks = cols * owned_blocks
    slots, edge = tiles_ref.shape[2], tiles_ref.shape[3]
    owned = owned_blocks * edge
    spare, strip = totals[0].shape[0] - 1, totals[0].shape[1]
    unroll = math.gcd(slots, UNROLL)
    row = lax.axis_index("row")
    occupied = count_ref[0, 0]

    for total in totals:
        total[...] = jnp.zeros(total.shape, jnp.float32)

    def add_tiles(step, carry):
        at = step * unroll
        places = []
        for lane in range(unroll):
            slot = at + lane
            pair = out_ref[0, 0, slot] * in_blocks + in_ref[0, 0, slot]
            places.append((slot, jnp.where(slot < occupied, pair, spare)))
        for slot, pair in places:
            for index, total in enumerate(totals):
                lines = slice(index * strip, (index + 1) * strip)
                total[pair] += tiles_ref[0, 0, slot, lines].astype(jnp.float32)
        return carry

    lax.fori_loop(0, (occupied + unroll - 1) // unroll, add_tiles, 0)

    for place in range(rows):
        owner = partner(row, place, rows) if rows == 2 else place
        for block in range(owned_blocks):
            columns = slice(block * edge, (block + 1) * edge)
            for source in range(in_blocks):
                pair = (owner * owned_blocks + block) * in_blocks + source
                for index, total in enumerate(totals):
                    value = total[pair]
                    high = value.astype(jnp.bfloat16)
                    low = (value - high.astype(jnp.float32)).astype(jnp.bfloat16)
                    column, line = source // owned_blocks, source % owned_blocks * edge + index * strip
                    lines = slice(line, line + strip)
                    weight_refs[place][column, lines, columns] = high
                    weight_refs[place][column, lines, owned + block * edge:owned + (block + 1) * edge] = low


def times_weight(parts, weights):
    incoming = None
    for start in range(0, len(parts), 2):
        term = jnp.dot(
            jnp.concatenate(parts[start:start + 2], axis=1),
            jnp.concatenate(weights[start:start + 2], axis=0),
            preferred_element_type=jnp.float32,
        )
        incoming = term if incoming is None else incoming + term
    owned = incoming.shape[1] // 2
    return incoming[:, :owned] + incoming[:, owned:]


def product_kernel(rows, cols, after, *refs):
    part_refs, refs = refs[after:after + cols], refs[after + cols:]
    weight_refs, result_refs = refs[:len(refs) // 2], refs[len(refs) // 2:]
    col = lax.axis_index("col")
    parts = [ref[...] for ref in part_refs]
    for weight_ref, result_ref in zip(weight_refs, result_refs):
        weights = [weight_ref[partner(col, offset, cols)] for offset in range(cols)]
        result_ref[...] = times_weight(parts, weights)


def restart_kernel(rows, cols, after_ref, seeds_ref, restart_ref):
    seed_total, sets = seeds_ref.shape
    places, _, owned = restart_ref.shape
    for place in range(places):
        row = partner(lax.axis_index("row"), place, rows)
        first = (row * cols + lax.axis_index("col")) * owned
        vertex = lax.broadcasted_iota(jnp.int32, (owned, sets), 0) + first
        restart = jnp.zeros((owned, sets), jnp.float32)
        for seed in range(seed_total):
            restart += (seeds_ref[seed:seed + 1, :] == vertex).astype(jnp.float32)
        restart_ref[place] = (1.0 - damping) * restart.T


def first_kernel(cols, *refs):
    part_refs, (own_ref, other_ref, degree_ref, given_ref) = refs[:cols - 1], refs[cols - 1:]
    row, col = lax.axis_index("row"), lax.axis_index("col")
    parts = [ref[...] for ref in part_refs]
    sets, owned = parts[0].shape
    columns = [col] + [partner(col, offset, cols) for offset in range(2, cols)]
    wanted = col ^ hop(1 - row)
    for place, weight_ref in enumerate((own_ref, other_ref)):
        given_ref[place, :sets] = times_weight(parts, [weight_ref[column] for column in columns])
        given_ref[place, sets:sets + owned] = weight_ref[wanted, :, :owned].astype(
            jnp.float32
        ) + weight_ref[wanted, :, owned:].astype(jnp.float32)
        given_ref[place, sets + owned:] = jnp.broadcast_to(
            degree_ref[...].astype(jnp.float32), (given_ref.shape[1] - sets - owned, owned)
        )


def nearest_kernel(early_ref, part_ref, own_ref, other_ref, given_ref):
    col = lax.axis_index("col")
    sets = part_ref.shape[0]
    for place, weight_ref in enumerate((own_ref, other_ref)):
        given_ref[place, :sets] = early_ref[place, :sets] + times_weight([part_ref[...]], [weight_ref[col ^ 1]])
        given_ref[place, sets:] = early_ref[place, sets:]


def both_kernel(mine_ref, theirs_ref, restart_ref, other_ref, scaled_ref):
    _, sets, owned = restart_ref.shape
    for place in range(2):
        incoming = mine_ref[place, :sets] + theirs_ref[1 - place, :sets]
        degree = (theirs_ref if place else mine_ref)[0, sets + owned:sets + owned + 1]
        risk = restart_ref[place] + damping * incoming
        scaled = (risk / degree).astype(jnp.bfloat16)
        scaled_ref[place] = scaled
        if place:
            other_ref[...] = scaled


def foreign_kernel(after_ref, theirs_ref, weight_ref):
    _, owned, double = weight_ref.shape
    sets = theirs_ref.shape[1] - owned - DEGREE_LINES
    for place in range(2):
        value = theirs_ref[1 - place, sets:sets + owned]
        high = value.astype(jnp.bfloat16)
        weight_ref[place, :, :owned] = high
        weight_ref[place, :, owned:] = (value - high.astype(jnp.float32)).astype(jnp.bfloat16)


def second_kernel(place, after, *refs):
    both_ref, hop_ref, weight_ref, foreign_ref, result_ref = refs[after:]
    row, col = lax.axis_index("row"), lax.axis_index("col")
    parts = [hop_ref[1], hop_ref[0], both_ref[0]]
    weights = [weight_ref[col ^ hop(row)], foreign_ref[place], weight_ref[col]]
    result_ref[...] = times_weight(parts, weights)


def side_kernel(early_ref, side_ref, weight_ref, result_ref):
    result_ref[...] = early_ref[...] + times_weight([side_ref[...]], [weight_ref[lax.axis_index("col") ^ 1]])


def finish_kernel(last, *refs):
    *incoming_refs, restart_ref, degree_ref, result_ref = refs
    risk = restart_ref[0] + damping * sum(ref[...] for ref in incoming_refs)
    if last:
        result_ref[...] = risk
    else:
        result_ref[...] = (risk / degree_ref[...].astype(jnp.float32)).astype(jnp.bfloat16)


def local(tiles, tile_out, tile_in, tile_count, out_degree, seed_ids, prior):
    rows, cols = lax.axis_size("row"), lax.axis_size("col")
    sets, owned = prior.shape
    slots, edge = tiles.shape[2], tiles.shape[3]
    owned_blocks = owned // edge
    in_blocks, out_blocks = cols * owned_blocks, rows * owned_blocks
    degree = out_degree.reshape(1, owned)
    low = jnp.bfloat16

    scaled, out_ids, in_ids, seeds = call(
        scale_kernel,
        [
            jax.ShapeDtypeStruct((sets, owned), low),
            pltpu.SMEM(tile_out.shape, jnp.int32),
            pltpu.SMEM(tile_in.shape, jnp.int32),
            jax.ShapeDtypeStruct((seed_ids.shape[1], sets), jnp.int32),
        ],
        "scale",
        in_specs=[HBM] * 5,
        out_specs=[VMEM, SMEM, SMEM, VMEM],
        scratch_shapes=[
            pltpu.VMEM((sets, owned), jnp.float32),
            pltpu.VMEM((1, owned), jnp.int32),
            pltpu.SemaphoreType.DMA((5,)),
        ],
        flops=16 * slots * edge**3,
        size=6 * sets * owned,
    )(*in_hbm(prior, degree, tile_out, tile_in, seed_ids.T))

    def spread(value):
        return [from_column(value, cols, offset) if offset else value for offset in range(cols)]

    parts = spread(scaled)

    weights = call(
        functools.partial(sum_kernel, rows, cols, owned_blocks),
        [jax.ShapeDtypeStruct((cols, owned, 2 * owned), low)] * rows,
        "sum_tiles",
        in_specs=[ANY] + [SMEM] * 3 + [VMEM],
        out_specs=[VMEM] * rows,
        scratch_shapes=[pltpu.VMEM((out_blocks * in_blocks + 1, edge // STRIPS, edge), jnp.float32)] * STRIPS,
        vmem=TILES_VMEM,
        flops=slots * edge * edge,
        size=2 * slots * edge * edge,
    )(scaled, tile_count, out_ids, in_ids, tiles)

    piece = jax.ShapeDtypeStruct((sets, owned), jnp.float32)

    def multiply(parts, weights, after=()):
        return call(
            functools.partial(product_kernel, rows, cols, len(after)),
            [piece] * len(weights),
            "product",
            in_specs=[ANY] * len(after) + [VMEM] * (cols + len(weights)),
            out_specs=[VMEM] * len(weights),
            flops=4 * sets * len(weights) * cols * owned * owned,
            size=4 * len(weights) * cols * owned * owned,
        )(*after, *parts, *weights)

    def count_restart(places, after):
        return call(
            functools.partial(restart_kernel, rows, cols),
            jax.ShapeDtypeStruct((places, sets, owned), jnp.float32),
            "restart",
            in_specs=[ANY, VMEM],
            out_specs=VMEM,
            flops=2 * places * sets * owned * seed_ids.shape[1],
            size=4 * places * sets * owned,
        )(after, seeds)

    def finish(incoming, restart, last):
        return call(
            functools.partial(finish_kernel, last),
            piece if last else jax.ShapeDtypeStruct((sets, owned), low),
            "last" if last else "next",
            in_specs=[VMEM] * (len(incoming) + 2),
            out_specs=VMEM,
            size=12 * sets * owned,
        )(*incoming, restart, degree)

    if (rows, cols, ITERATIONS) == (2, 4, 2):
        given = jax.ShapeDtypeStruct((2, sets + owned + DEGREE_LINES, owned), jnp.float32)
        early = call(
            functools.partial(first_kernel, cols),
            given,
            "first",
            in_specs=[VMEM] * (cols + 2),
            out_specs=VMEM,
            flops=8 * sets * (cols - 1) * owned * owned,
            size=8 * cols * owned * owned,
        )(parts[0], *parts[2:], *weights, degree)
        mine = call(
            nearest_kernel,
            given,
            "nearest",
            in_specs=[VMEM] * 4,
            out_specs=VMEM,
            flops=8 * sets * owned * owned,
            size=24 * sets * owned,
        )(early, parts[1], *weights)
        theirs = swap_rows(mine)
        restart = count_restart(2, mine)
        other, both = call(
            both_kernel,
            [jax.ShapeDtypeStruct((sets, owned), low), jax.ShapeDtypeStruct((2, sets, owned), low)],
            "both",
            in_specs=[VMEM] * 3,
            out_specs=[VMEM] * 2,
            size=24 * sets * owned,
        )(mine, theirs, restart)
        side = from_side(other, cols)
        near = from_hop(both, cols)
        foreign = call(
            foreign_kernel,
            jax.ShapeDtypeStruct((2, owned, 2 * owned), low),
            "foreign",
            in_specs=[ANY, VMEM],
            out_specs=VMEM,
            size=16 * owned * owned,
        )(other, theirs)

        def second(place, *after):
            early = call(
                functools.partial(second_kernel, place, len(after)),
                piece,
                "second",
                in_specs=[ANY] * len(after) + [VMEM] * 4,
                out_specs=VMEM,
                flops=12 * sets * owned * owned,
                size=12 * owned * owned,
            )(*after, both, near, weights[place], foreign)
            return call(
                side_kernel,
                piece,
                "side",
                in_specs=[VMEM] * 3,
                out_specs=VMEM,
                flops=4 * sets * owned * owned,
                size=16 * sets * owned,
            )(early, side, weights[place])

        leaving = second(1)
        received = swap_rows(leaving)
        return finish((second(0, leaving), received), restart, True)

    for round_index in range(ITERATIONS):
        last = round_index == ITERATIONS - 1
        if rows == 2:
            leaving, = multiply(parts, weights[1:])
            received = swap_rows(leaving)
            staying, = multiply(parts, weights[:1], (leaving,))
            incoming = (staying, received)
        else:
            leaving = jnp.stack(multiply(parts, weights))
            incoming = (lax.psum_scatter(leaving, "row", scatter_dimension=0, tiled=False),)
        if not round_index:
            restart = count_restart(1, leaving)
        value = finish(incoming, restart, last)
        if not last:
            parts = spread(value)
    return value


def solution(mesh):
    placed = (
        P("row", "col", None, None, None),
        P("row", "col", None),
        P("row", "col", None),
        P("row", "col"),
        P(("row", "col")),
        P("seed", None),
        P("seed", ("row", "col")),
    )
    return jax.shard_map(
        local, mesh=mesh, in_specs=placed, out_specs=P("seed", ("row", "col")), check_vma=False
    )
```
